32 devices in a mesh: batch: 8 (over z, core), tensor: 4 (over y, x).
Axes of the slice: x: 2, y: 2, z: 4, core: 2. Of those that a mesh axis runs over, the one named last changes fastest.
Arguments:
- tokens: bfloat16 [12288, 1024], P(('batch', 'tensor')), may hold values from -60 to 60
- output_grad: bfloat16 [12288, 1024], P(('batch', 'tensor')), may hold values from -6 to 6
- attn_norm_gain: bfloat16 [1024], replicated, may hold values from 0.099609375 to 1.8984375
- attn_norm_bias: bfloat16 [1024], replicated, may hold values from -3 to 3
- mlp_norm_gain: bfloat16 [1024], replicated, may hold values from 0.099609375 to 1.8984375
- mlp_norm_bias: bfloat16 [1024], replicated, may hold values from -3 to 3
- qkv_weight: bfloat16 [1024, 3072], P(None, 'tensor'), may hold values from -0.1875 to 0.1875
- qkv_bias: bfloat16 [3072], P('tensor'), may hold values from -3 to 3
- dense_weight: bfloat16 [1024, 1024], P('tensor'), may hold values from -0.75 to 0.75
- dense_bias: bfloat16 [1024], replicated, may hold values from -3 to 3
- fc_weight: bfloat16 [1024, 4096], P(None, 'tensor'), may hold values from -0.1875 to 0.1875
- fc_bias: bfloat16 [4096], P('tensor'), may hold values from -3 to 3
- proj_weight: bfloat16 [4096, 1024], P('tensor'), may hold values from -0.09375 to 0.09375
- feature_weight: bfloat16 [16, 64, 64], P('tensor'), may hold values from -0.75 to 0.75
- seq_units: int32 [8, 4], P('batch'), may hold values from 1 to 6, 12 in all within a row
- pad_tokens: int32 [8, 4], P('batch'), may hold values from 0 to 63
Outputs:
- output: bfloat16 [12288, 1024], P(('batch', 'tensor'))
- tokens_grad: bfloat16 [12288, 1024], P(('batch', 'tensor'))
- attn_norm_gain_grad: float32 [1024], replicated
- attn_norm_bias_grad: float32 [1024], replicated
- mlp_norm_gain_grad: float32 [1024], replicated
- mlp_norm_bias_grad: float32 [1024], replicated
- qkv_weight_grad: float32 [1024, 3072], P(None, 'tensor')
- qkv_bias_grad: float32 [3072], P('tensor')
- dense_weight_grad: float32 [1024, 1024], P('tensor')
- dense_bias_grad: float32 [1024], replicated
- fc_weight_grad: float32 [1024, 4096], P(None, 'tensor')
- fc_bias_grad: float32 [4096], P('tensor')
- proj_weight_grad: float32 [4096, 1024], P('tensor')
- feature_weight_grad: float32 [16, 64, 64], P('tensor')
The draws below stay inside these ranges and needn't reach their ends.
Inputs may be any that keep to these rules, and one draw needn't show every extreme that they name: `seq_units`: the lengths of a group's 4 sequences add up to 12 units.
All inputs are finite; a program needn't handle non-finite values.
Results may differ from the reference program's by a relative error of at most 0.011.
Values may be sent and summed in bfloat16 or wider, within the bound.
No kernel may reach another device: no remote copies, remote signals or barrier semaphores. Data moves between devices by JAX's collectives and lax.ppermute only.
A program may use at most 192 MiB of HBM per device.

```python
import math
import jax
import jax.numpy as jnp
import numpy as np
from jax import lax

D = 1024
HEADS = 16
HD = 64
ROT = 16
FF = 4096
NFEAT = 64
SPAN = 64
GROUP = 1536
TOKENS = 12288
UNIT = 128
UNITS = 12
NSEQ = 4
MOST = 6
N_BATCH = 8


def draw_tokens(key, part):
    key_base, key_rows, key_cols = jax.random.split(key, 3)
    row_scale = jnp.exp(jax.random.uniform(key_rows, (TOKENS, 1), jnp.float32, 0.0, math.log(10.0)))
    col_scale = jnp.exp(jax.random.uniform(key_cols, (1, D), jnp.float32, 0.0, math.log(10.0)))
    base = jnp.clip(jax.random.normal(key_base, (TOKENS, D), jnp.float32), -6.0, 6.0)
    return (base * row_scale * col_scale * 0.1).astype(jnp.bfloat16)


def set_ends(values, rng, least, largest):
    longest = values.shape.index(max(values.shape))
    spots = []
    for shift in (0, 1):
        where = [jax.random.randint(jax.random.fold_in(rng, axis), (), 0, length) for axis, length in enumerate(values.shape)]
        where[longest] = (where[longest] + shift) % values.shape[longest]
        spots.append(tuple(where))
    return values.at[spots[0]].set(least).at[spots[1]].set(largest)


def block_scale(stream_key, shape, cuts, low, high):
    loudness, own = 1.0, jax.random.fold_in(stream_key, 6)
    for axis_at, blocks in cuts:
        steps = jnp.exp(jax.random.uniform(jax.random.fold_in(own, axis_at), (blocks,), jnp.float32, low / len(cuts), high / len(cuts)))
        loudness = loudness * jnp.repeat(steps, shape[axis_at] // blocks).reshape([-1 if axis == axis_at else 1 for axis in range(len(shape))])
    return loudness


def split_up(count, total, limit, lean):
    weights = [(1 << 20) // math.isqrt(grade ** lean) + 1 for grade in range(2, count + 1)]
    surplus, counts = total - limit - (count - 1), [1] * (count - 1)
    while surplus > 0:
        free = [i for i in range(count - 1) if counts[i] < limit]
        whole, left = sum([weights[i] for i in free]), surplus
        for i in free:
            more = min(limit - counts[i], max(1, left * weights[i] // whole), surplus)
            counts[i] = counts[i] + more
            surplus = surplus - more
    return np.array([limit] + counts)


def uneven(stream_key, amount, total, limit, lean):
    if amount == 2:
        one = jax.random.randint(stream_key, (), max(1, total - limit), min(limit, total - 1) + 1)
        return jnp.stack([one, total - one])
    sizes = jnp.asarray(split_up(amount, total, limit, lean), jnp.int32)
    couples = (amount - 1) // 2
    source_of, receiver = sizes[1:1 + 2 * couples:2], sizes[2:2 + 2 * couples:2]
    slack = jnp.minimum(source_of - 1, limit - receiver)
    moved = jax.random.randint(jax.random.fold_in(stream_key, 1), (couples,), 0, 1 << 20) % (slack + 1)
    sizes = sizes.at[1:1 + 2 * couples:2].set(source_of - moved).at[2:2 + 2 * couples:2].set(receiver + moved)
    return sizes[jax.random.permutation(jax.random.fold_in(stream_key, 2), amount)]


def bell_draw(rng, shape, spread, reach, cuts=(), kind=jnp.bfloat16):
    values = jax.random.normal(rng, shape, jnp.float32) * spread
    if len(cuts) > 0:
        values = block_scale(rng, shape, cuts, -0.22, 0.18) * values
    return jnp.clip(values, min=-reach, max=reach).astype(kind)


def setup_inputs(seed: int = 0) -> dict:
    splits = jax.random.split(jax.random.key(seed), 17)
    return {
        "tokens": draw_tokens(jax.random.fold_in(splits[16], 71), 0),
        "output_grad": bell_draw(splits[1], (TOKENS, D), 1.0, 6.0, ((0, 32),)),
        "attn_norm_gain": jnp.clip(1.0 + 0.18 * jax.random.normal(splits[2], (D,), jnp.float32), 0.099609375, 1.8984375).astype(jnp.bfloat16),
        "attn_norm_bias": bell_draw(splits[3], (D,), 0.5, 3.0),
        "mlp_norm_gain": jnp.clip(1.0 + 0.18 * jax.random.normal(splits[4], (D,), jnp.float32), 0.099609375, 1.8984375).astype(jnp.bfloat16),
        "mlp_norm_bias": bell_draw(splits[5], (D,), 0.5, 3.0),
        "qkv_weight": bell_draw(splits[6], (D, 3 * D), D ** -0.5, 0.1875, ((1, 4),)),
        "qkv_bias": bell_draw(splits[7], (3 * D,), 0.5, 3.0, ((0, 4),)),
        "dense_weight": bell_draw(splits[8], (D, D), (D // 16) ** -0.5, 0.75, ((0, 4),)),
        "dense_bias": bell_draw(splits[9], (D,), 0.5, 3.0),
        "fc_weight": bell_draw(splits[10], (D, FF), D ** -0.5, 0.1875, ((1, 4),)),
        "fc_bias": bell_draw(splits[11], (FF,), 0.5, 3.0, ((0, 4),)),
        "proj_weight": bell_draw(splits[12], (FF, D), FF ** -0.5, 0.09375, ((0, 4),)),
        "feature_weight": bell_draw(splits[13], (HEADS, HD, NFEAT), HD ** -0.5, 0.75, ((0, 4),)),
        "seq_units": jax.vmap(lambda own: uneven(own, NSEQ, UNITS, MOST, 2))(jax.random.split(splits[14], N_BATCH)).reshape((N_BATCH, NSEQ)).astype(jnp.int32),
        "pad_tokens": set_ends(jax.random.randint(splits[15], (N_BATCH, NSEQ), 0, SPAN), jax.random.fold_in(splits[15], 1), 0, SPAN - 1).astype(jnp.int32),
    }


@jax.custom_vjp
def low(v):
    return lax.optimization_barrier(v.astype(jnp.bfloat16)).astype(jnp.float32)

@jax.custom_vjp
def low_back(v):
    return v

def low_keep(v):
    return (low(v), None)

def low_pass(kept, grad):
    return (grad,)

def back_keep(v):
    return (v, None)

def back_low(kept, grad):
    return (low(grad),)
low.defvjp(low_keep, low_pass)
low_back.defvjp(back_keep, back_low)
highest = lax.Precision.HIGHEST

def layer_norm(values, norm_gain, norm_bias):
    row_mean = lax.optimization_barrier(jnp.mean(values, axis=-1, keepdims=True))
    centered = values - row_mean
    row_var = lax.optimization_barrier(jnp.mean(centered * centered, axis=-1, keepdims=True))
    return centered * lax.rsqrt(row_var + 1e-05) * norm_gain + norm_bias

def cosine_table(dimension):
    spatial = jnp.arange(dimension, dtype=jnp.float32)[:, None]
    frequency = jnp.arange(dimension, dtype=jnp.float32)[None, :]
    dct_table = jnp.cos(math.pi * (2.0 * spatial + 1.0) * frequency / (2.0 * dimension)) * math.sqrt(2.0 / dimension)
    return jnp.where(frequency == 0.0, dct_table * math.sqrt(0.5), dct_table)

def rotate(values, cosines, sines, direction):
    half_rot = cosines.shape[-1]
    leading = values[..., :half_rot]
    trailing = values[..., half_rot:2 * half_rot]
    return jnp.concatenate([leading * cosines - direction * trailing * sines, trailing * cosines + direction * leading * sines, values[..., 2 * half_rot:]], axis=-1)

def rotary_angles(position):
    half_rot = ROT // 2
    inverse_freq = jnp.exp(-math.log(10000.0) * 2.0 * jnp.arange(half_rot, dtype=jnp.float32) / ROT)
    angles = position.astype(jnp.float32)[:, None] * inverse_freq[None, :]
    return (jnp.cos(angles)[:, None, :], jnp.sin(angles)[:, None, :])

def group_layout(unit_counts, pad_counts):
    seq_ends = jnp.cumsum(unit_counts).astype(jnp.int32) * UNIT
    starts = seq_ends - unit_counts * UNIT
    row_ids = jnp.arange(GROUP, dtype=jnp.int32)
    member = (row_ids[:, None] >= starts[None, :]) & (row_ids[:, None] < seq_ends[None, :])
    first_row = lax.optimization_barrier(jnp.sum(jnp.where(member, starts[None, :], 0), axis=1))
    last_real = lax.optimization_barrier(jnp.sum(jnp.where(member, (seq_ends - pad_counts)[None, :], 0), axis=1))
    sequence_ids = lax.optimization_barrier(jnp.sum(jnp.where(member, jnp.arange(NSEQ, dtype=jnp.int32)[None, :], 0), axis=1))
    return (sequence_ids, (row_ids - first_row).astype(jnp.int32), (row_ids < last_real).astype(jnp.float32))

def group_forward(x_rows, sequence_ids, position, is_real, weights):
    gain_one, bias_one, gain_two, bias_two, weight_qkv, bias_qkv, weight_dense, bias_dense, weight_fc, bias_fc, weight_proj, weight_feat = weights
    normed_one = low(layer_norm(x_rows, gain_one, bias_one))
    normed_two = low(layer_norm(x_rows, gain_two, bias_two))
    packed = low_back(jnp.dot(normed_one, weight_qkv, precision=highest) + bias_qkv).reshape(GROUP, HEADS, 3, HD)
    query = packed[:, :, 0]
    key_rows = packed[:, :, 1]
    value_rows = low(packed[:, :, 2])
    cosines, sines = rotary_angles(position)
    dct_table = cosine_table(HD)

    def feature_logits(head_rows):
        spectrum = jnp.einsum('ghd,de->ghe', rotate(head_rows, cosines, sines, 1.0), dct_table, precision=highest)
        return jnp.einsum('ghd,hdm->ghm', spectrum, weight_feat, precision=highest)
    query_feat = low(jnp.exp(feature_logits(query)))
    key_feat = low(is_real[:, None, None] * jnp.exp(feature_logits(key_rows)))
    row_ids = jnp.arange(GROUP, dtype=jnp.int32)
    visible = (sequence_ids[:, None] == sequence_ids[None, :]) & (row_ids[:, None] >= row_ids[None, :])

    def one_head(operands):
        head_query, head_key, head_value = operands
        scores = jnp.where(visible, jnp.dot(head_query, head_key.T, precision=highest), 0.0)
        return jnp.dot(scores, head_value, precision=highest) / lax.optimization_barrier(jnp.sum(scores, axis=1, keepdims=True))
    attended = lax.map(jax.checkpoint(one_head), (jnp.transpose(query_feat, (1, 0, 2)), jnp.transpose(key_feat, (1, 0, 2)), jnp.transpose(value_rows, (1, 0, 2))))
    mixed = low(low_back(jnp.transpose(attended, (1, 0, 2)).reshape(GROUP, D)))
    hidden = low_back(jnp.dot(normed_two, weight_fc, precision=highest) + bias_fc)
    activated = low(jax.nn.gelu(hidden, approximate=False))
    return x_rows + jnp.dot(mixed, weight_dense, precision=highest) + jnp.dot(activated, weight_proj, precision=highest) + bias_dense

def reference(tokens, output_grad, attn_norm_gain, attn_norm_bias, mlp_norm_gain, mlp_norm_bias, qkv_weight, qkv_bias, dense_weight, dense_bias, fc_weight, fc_bias, proj_weight, feature_weight, seq_units, pad_tokens):
    sequence_ids, position, is_real = jax.vmap(group_layout)(seq_units, pad_tokens)
    weights = tuple((weight_arg.astype(jnp.float32) for weight_arg in (attn_norm_gain, attn_norm_bias, mlp_norm_gain, mlp_norm_bias, qkv_weight, qkv_bias, dense_weight, dense_bias, fc_weight, fc_bias, proj_weight, feature_weight)))
    x_groups = tokens.astype(jnp.float32).reshape(N_BATCH, GROUP, D)

    def whole(x_all, layer_weights):

        def per_group(operands):
            return group_forward(operands[0], operands[1], operands[2], operands[3], layer_weights)
        return lax.map(jax.checkpoint(per_group), (x_all, sequence_ids, position, is_real))
    result, pull = jax.vjp(whole, x_groups, weights)
    grad_x, grad_weights = pull(output_grad.astype(jnp.float32).reshape(N_BATCH, GROUP, D))
    return (result.reshape(TOKENS, D).astype(jnp.bfloat16), grad_x.reshape(TOKENS, D).astype(jnp.bfloat16), grad_weights[0], grad_weights[1], grad_weights[2], grad_weights[3], grad_weights[4], grad_weights[5], grad_weights[6], grad_weights[7], grad_weights[8], grad_weights[9], grad_weights[10], grad_weights[11])
```

```python
from functools import partial
import math

import jax
import jax.numpy as jnp
from jax import lax
from jax.experimental import pallas as pl
from jax.experimental.pallas import tpu as pltpu
from jax.sharding import PartitionSpec as P

ROT = 16
UNIT = 128
EPS = 1e-05
F32 = jnp.float32
BF16 = jnp.bfloat16
VMEM_BYTES = 56 * 1024 * 1024

NN = (((1,), (0,)), ((), ()))
NT = (((1,), (1,)), ((), ()))
TN = (((0,), (0,)), ((), ()))


def mm(a, b, dims=NN):
    return lax.dot_general(a, b, dims, preferred_element_type=F32)


def split(a):
    hi = a.astype(BF16)
    return hi, (a - hi.astype(F32)).astype(BF16)


def params(grid_rank=1):
    return pltpu.CompilerParams(
        dimension_semantics=("arbitrary",) * grid_rank, vmem_limit_bytes=VMEM_BYTES
    )


def whole(shape):
    return pl.BlockSpec(shape, lambda *_: (0,) * len(shape))


def rows_of(block, width):
    return pl.BlockSpec((block, width), lambda i: (i, 0))


def norm_rows(x):
    mean = jnp.mean(x, axis=-1, keepdims=True)
    cent = x - mean
    inv = lax.rsqrt(jnp.mean(cent * cent, axis=-1, keepdims=True) + EPS)
    return cent * inv, inv


def fwd_kernel(x, vec, wqkv, bqkv, wfc, bfc, lna_o, lnm_o, qk_o, v_o, act_o, gp_o):
    xh, _ = norm_rows(x[...].astype(F32))
    lna = (xh * vec[0:1, :] + vec[1:2, :]).astype(BF16)
    lnm = (xh * vec[2:3, :] + vec[3:4, :]).astype(BF16)
    lna_o[...] = lna
    lnm_o[...] = lnm
    qkv = mm(lna, wqkv[...]) + bqkv[...]
    two = qk_o.shape[1]
    qk_o[...] = qkv[:, :two]
    v_o[...] = qkv[:, two:].astype(BF16)
    h = mm(lnm, wfc[...]) + bfc[...]
    cdf = 0.5 + 0.5 * lax.erf(h * math.sqrt(0.5))
    act_o[...] = (h * cdf).astype(BF16)
    gp_o[...] = (cdf + h * (jnp.exp(-0.5 * h * h) * (1.0 / math.sqrt(2.0 * math.pi)))).astype(BF16)


def fwd_call(x, vec, wqkv, bqkv, wfc, bfc):
    rows, width = x.shape
    cols, hid = wqkv.shape[1], wfc.shape[1]
    w = cols // 3
    rb = 256
    flops = 2 * rows * width * (cols + hid)
    return pl.pallas_call(
        fwd_kernel,
        grid=(rows // rb,),
        in_specs=[
            rows_of(rb, width),
            whole(vec.shape),
            whole(wqkv.shape),
            whole(bqkv.shape),
            whole(wfc.shape),
            whole(bfc.shape),
        ],
        out_specs=[
            rows_of(rb, width),
            rows_of(rb, width),
            rows_of(rb, 2 * w),
            rows_of(rb, w),
            rows_of(rb, hid),
            rows_of(rb, hid),
        ],
        out_shape=[
            jax.ShapeDtypeStruct((rows, width), BF16),
            jax.ShapeDtypeStruct((rows, width), BF16),
            jax.ShapeDtypeStruct((rows, 2 * w), F32),
            jax.ShapeDtypeStruct((rows, w), BF16),
            jax.ShapeDtypeStruct((rows, hid), BF16),
            jax.ShapeDtypeStruct((rows, hid), BF16),
        ],
        compiler_params=params(),
        cost_estimate=pl.CostEstimate(
            flops=flops, bytes_accessed=rows * width * 20, transcendentals=rows * hid
        ),
        name="norm_qkv_fc",
    )(x, vec, wqkv, bqkv, wfc, bfc)


def chunk_place(units, pads, chunk, nseq):
    start = jnp.int32(0)
    pos, real, last = jnp.int32(0), jnp.int32(0), jnp.int32(0)
    for n in range(nseq):
        u = units[0, n]
        inside = (chunk >= start) & (chunk < start + u)
        pos = jnp.where(inside, chunk - start, pos)
        real = jnp.where(inside, (start + u - chunk) * UNIT - pads[0, n], real)
        last = jnp.where(inside, (chunk == start + u - 1).astype(jnp.int32), last)
        start = start + u
    return pos, real, last


def lanes(table, w):
    return jnp.concatenate([table] * (w // table.shape[1]), axis=1) if w > table.shape[1] else table


def turn(a, cosines, sines, low_half):
    w = a.shape[1]
    other = jnp.where(low_half, pltpu.roll(a, w - ROT // 2, 1), pltpu.roll(a, ROT // 2, 1))
    return a * cosines + other * sines


def head_stack(a, head_of_lane, heads):
    zero = jnp.zeros_like(a)
    return jnp.concatenate([jnp.where(head_of_lane == h, a, zero) for h in range(heads)], axis=0)


def side_by_side(a, heads):
    return jnp.concatenate([a[h * UNIT : (h + 1) * UNIT, :] for h in range(heads)], axis=1)


def masks(w, hd):
    lane = lax.broadcasted_iota(jnp.int32, (UNIT, w), 1)
    head_of_lane = lane // hd
    low_half = (lane % hd) < ROT // 2
    bi = lax.broadcasted_iota(jnp.int32, (w, w), 0) // hd
    bj = lax.broadcasted_iota(jnp.int32, (w, w), 1) // hd
    heads = w // hd
    row = lax.broadcasted_iota(jnp.int32, (heads * UNIT, UNIT), 0) % UNIT
    col = lax.broadcasted_iota(jnp.int32, (heads * UNIT, UNIT), 1)
    return head_of_lane, low_half, bi == bj, row >= col


def attn_fwd_kernel(
    nseq, hd, per, units, pads, qk, v_ref, cf, cos_t, sin_t,
    ao_o, o_o, rd_o, fq_o, fk_o, rq_o, rk_o, s_o, ks_o, state, ksum,
):
    w = v_ref.shape[1]
    heads = w // hd
    step = pl.program_id(0)
    head_of_lane, low_half, diag, causal = masks(w, hd)
    ones_bd = jnp.where(diag, 1.0, 0.0).astype(BF16)
    head_ones = head_stack(jnp.ones((UNIT, w), BF16), head_of_lane, heads)
    cf_hi, cf_lo = cf[0], cf[1]

    @pl.when(step == 0)
    def _():
        state[...] = jnp.zeros_like(state)
        ksum[...] = jnp.zeros_like(ksum)

    row_id = lax.broadcasted_iota(jnp.int32, (UNIT, 1), 0)
    for i in range(per):
        pos, real, _ = chunk_place(units, pads, step * per + i, nseq)
        rows = pl.ds(i * UNIT, UNIT)
        at = pl.ds(pl.multiple_of(pos * UNIT, UNIT), UNIT)
        cosines = lanes(cos_t[at, :], w)
        sines = lanes(sin_t[at, :], w)
        keep = jnp.where(pos == 0, 0.0, 1.0)
        s_old = state[...] * keep
        k_old = ksum[...] * keep
        rq = turn(qk[rows, 0:w], cosines, sines, low_half)
        rk = turn(qk[rows, w : 2 * w], cosines, sines, low_half)
        rq_o[rows, :] = rq.astype(BF16)
        rk_o[rows, :] = rk.astype(BF16)
        qh, ql = split(rq)
        kh, kl = split(rk)
        fq = jnp.exp(mm(qh, cf_hi) + mm(ql, cf_hi) + mm(qh, cf_lo)).astype(BF16)
        ek = jnp.exp(mm(kh, cf_hi) + mm(kl, cf_hi) + mm(kh, cf_lo))
        fk = jnp.where(row_id < real, ek, 0.0).astype(BF16)
        fq_o[rows, :] = fq
        fk_o[rows, :] = fk
        v = v_ref[rows, :]
        s_hi, s_lo = split(s_old)
        s_o[i, 0] = s_hi
        s_o[i, 1] = s_lo
        ks_o[i] = k_old
        scores = jnp.where(causal, mm(head_stack(fq, head_of_lane, heads), fk, NT), 0.0).astype(BF16)
        wide = side_by_side(scores, heads)
        num = mm(wide, head_stack(v, head_of_lane, heads)) + mm(fq, s_hi) + mm(fq, s_lo)
        p_hi, p_lo = split(fq.astype(F32) * k_old)
        den = mm(wide, head_ones) + mm(p_hi, ones_bd) + mm(p_lo, ones_bd)
        rden = 1.0 / den
        o = num * rden
        o_o[rows, :] = o
        rd_o[rows, :] = rden
        ao_o[rows, :] = o.astype(BF16)
        state[...] = s_old + jnp.where(diag, mm(fk, v, TN), 0.0)
        ksum[...] = k_old + jnp.sum(fk.astype(F32), axis=0, keepdims=True)


def attn_fwd_call(units, pads, qk, v, cf, cos_t, sin_t, hd, parts):
    rows, w = v.shape
    block = rows // parts
    per = block // UNIT
    nseq = units.shape[1]
    n = rows // UNIT
    smem = pl.BlockSpec(memory_space=pltpu.SMEM)
    sds = jax.ShapeDtypeStruct
    return pl.pallas_call(
        partial(attn_fwd_kernel, nseq, hd, per),
        grid=(parts,),
        in_specs=[
            smem,
            smem,
            rows_of(block, 2 * w),
            rows_of(block, w),
            whole(cf.shape),
            whole(cos_t.shape),
            whole(sin_t.shape),
        ],
        out_specs=[rows_of(block, w)] * 7
        + [
            pl.BlockSpec((per, 2, w, w), lambda i: (i, 0, 0, 0)),
            pl.BlockSpec((per, 1, w), lambda i: (i, 0, 0)),
        ],
        out_shape=[
            sds((rows, w), BF16),
            sds((rows, w), F32),
            sds((rows, w), F32),
            sds((rows, w), BF16),
            sds((rows, w), BF16),
            sds((rows, w), BF16),
            sds((rows, w), BF16),
            sds((n, 2, w, w), BF16),
            sds((n, 1, w), F32),
        ],
        scratch_shapes=[pltpu.VMEM((w, w), F32), pltpu.VMEM((1, w), F32)],
        compiler_params=params(),
        cost_estimate=pl.CostEstimate(
            flops=6_000_000_000, bytes_accessed=rows * w * 24, transcendentals=2 * rows * w
        ),
        name="attn_fwd",
    )(units, pads, qk, v, cf, cos_t, sin_t)


def attn_bwd_kernel(
    nseq, hd, per, units, pads, dao, v_ref, o_ref, rd_ref, fq_ref, fk_ref, rq_ref, rk_ref, s_ref, ks_ref,
    cf, cos_t, sin_t, dqkv_o, g_o, sum_o, after, after_sum,
):
    w = v_ref.shape[1]
    heads = w // hd
    step = pl.program_id(0)
    block = pl.num_programs(0) - 1 - step
    head_of_lane, low_half, diag, causal = masks(w, hd)
    ones_bd = jnp.where(diag, 1.0, 0.0).astype(BF16)
    cf_hi, cf_lo = cf[0], cf[1]

    @pl.when(step == 0)
    def _():
        after[...] = jnp.zeros_like(after)
        after_sum[...] = jnp.zeros_like(after_sum)
        g_o[...] = jnp.zeros_like(g_o)
        sum_o[...] = jnp.zeros_like(sum_o)

    for i in reversed(range(per)):
        pos, _, last = chunk_place(units, pads, block * per + i, nseq)
        rows = pl.ds(i * UNIT, UNIT)
        at = pl.ds(pl.multiple_of(pos * UNIT, UNIT), UNIT)
        cosines = lanes(cos_t[at, :], w)
        sines = -lanes(sin_t[at, :], w)
        keep = jnp.where(last == 1, 0.0, 1.0)
        a_old = after[...] * keep
        as_old = after_sum[...] * keep
        fq, fk, v = fq_ref[rows, :], fk_ref[rows, :], v_ref[rows, :]
        fqf, fkf = fq.astype(F32), fk.astype(F32)
        dn = (dao[rows, :].astype(F32) * rd_ref[rows, :]).astype(BF16)
        p_hi, p_lo = split(dn.astype(F32) * o_ref[rows, :])
        dden = -(mm(p_hi, ones_bd) + mm(p_lo, ones_bd))
        dn_s = head_stack(dn, head_of_lane, heads)
        fq_s = head_stack(fq, head_of_lane, heads)
        dden_s = jnp.concatenate(
            [jnp.broadcast_to(dden[:, h * hd : h * hd + 1], (UNIT, UNIT)) for h in range(heads)], axis=0
        )
        da = jnp.where(causal, mm(dn_s, v, NT) + dden_s, 0.0).astype(BF16)
        a = jnp.where(causal, mm(fq_s, fk, NT), 0.0).astype(BF16)
        s_hi, s_lo = s_ref[i, 0], s_ref[i, 1]
        dfq = (
            mm(side_by_side(da, heads), head_stack(fk, head_of_lane, heads))
            + mm(dn, s_hi, NT)
            + mm(dn, s_lo, NT)
            + dden * ks_ref[i]
        )
        a_hi, a_lo = split(a_old)
        dfk = mm(da, fq_s, TN) + mm(v, a_hi, NT) + mm(v, a_lo, NT) + as_old
        dv = mm(a, dn_s, TN) + mm(fk, a_hi) + mm(fk, a_lo)
        after[...] = a_old + jnp.where(diag, mm(fq, dn, TN), 0.0)
        after_sum[...] = as_old + jnp.sum(fqf * dden, axis=0, keepdims=True)
        dsq = (dfq * fqf).astype(BF16)
        dsk = (dfk * fkf).astype(BF16)
        g_o[...] += mm(rq_ref[rows, :], dsq, TN) + mm(rk_ref[rows, :], dsk, TN)
        dq = turn(mm(dsq, cf_hi, NT) + mm(dsq, cf_lo, NT), cosines, sines, low_half)
        dk = turn(mm(dsk, cf_hi, NT) + mm(dsk, cf_lo, NT), cosines, sines, low_half)
        for j, part in enumerate((dq, dk, dv)):
            part = part.astype(BF16)
            dqkv_o[rows, j * w : (j + 1) * w] = part
            sum_o[:, j * w : (j + 1) * w] += jnp.sum(part.astype(F32), axis=0, keepdims=True)


def attn_bwd_call(units, pads, dao, v, o, rd, fq, fk, rq, rk, s, ks, cf, cos_t, sin_t, hd, parts):
    rows, w = v.shape
    block = rows // parts
    per = block // UNIT
    nseq = units.shape[1]
    smem = pl.BlockSpec(memory_space=pltpu.SMEM)
    sds = jax.ShapeDtypeStruct

    def back(width):
        return pl.BlockSpec((block, width), lambda i: (parts - 1 - i, 0))

    return pl.pallas_call(
        partial(attn_bwd_kernel, nseq, hd, per),
        grid=(parts,),
        in_specs=[smem, smem]
        + [back(w)] * 8
        + [
            pl.BlockSpec((per, 2, w, w), lambda i: (parts - 1 - i, 0, 0, 0)),
            pl.BlockSpec((per, 1, w), lambda i: (parts - 1 - i, 0, 0)),
            whole(cf.shape),
            whole(cos_t.shape),
            whole(sin_t.shape),
        ],
        out_specs=[back(3 * w), whole((w, w)), whole((1, 3 * w))],
        out_shape=[sds((rows, 3 * w), BF16), sds((w, w), F32), sds((1, 3 * w), F32)],
        scratch_shapes=[pltpu.VMEM((w, w), F32), pltpu.VMEM((1, w), F32)],
        compiler_params=params(),
        cost_estimate=pl.CostEstimate(
            flops=10_000_000_000, bytes_accessed=rows * w * 30, transcendentals=0
        ),
        name="attn_bwd",
    )(units, pads, dao, v, o, rd, fq, fk, rq, rk, s, ks, cf, cos_t, sin_t)


def out_kernel(ao, act, wd, wp, out):
    out[...] = (mm(ao[...], wd[...]) + mm(act[...], wp[...])).astype(BF16)


def out_call(ao, act, wd, wp):
    rows, w = ao.shape
    hid, width = wp.shape
    rb = 256
    return pl.pallas_call(
        out_kernel,
        grid=(rows // rb,),
        in_specs=[rows_of(rb, w), rows_of(rb, hid), whole(wd.shape), whole(wp.shape)],
        out_specs=rows_of(rb, width),
        out_shape=jax.ShapeDtypeStruct((rows, width), BF16),
        compiler_params=params(),
        cost_estimate=pl.CostEstimate(
            flops=2 * rows * width * (w + hid), bytes_accessed=rows * (w + hid + width) * 2, transcendentals=0
        ),
        name="branches",
    )(ao, act, wd, wp)


def grad_kernel(g_ref, gp, wd, wp, dao_o, dh_o, sum_o):
    @pl.when(pl.program_id(0) == 0)
    def _():
        sum_o[...] = jnp.zeros_like(sum_o)

    g = g_ref[...]
    dao_o[...] = mm(g, wd[...], NT).astype(BF16)
    dh = (mm(g, wp[...], NT) * gp[...].astype(F32)).astype(BF16)
    dh_o[...] = dh
    sum_o[...] += jnp.sum(dh.astype(F32), axis=0, keepdims=True)


def grad_call(g, gp, wd, wp):
    rows, width = g.shape
    w, hid = wd.shape[0], wp.shape[0]
    rb = 256
    sds = jax.ShapeDtypeStruct
    return pl.pallas_call(
        grad_kernel,
        grid=(rows // rb,),
        in_specs=[rows_of(rb, width), rows_of(rb, hid), whole(wd.shape), whole(wp.shape)],
        out_specs=[rows_of(rb, w), rows_of(rb, hid), whole((1, hid))],
        out_shape=[sds((rows, w), BF16), sds((rows, hid), BF16), sds((1, hid), F32)],
        compiler_params=params(),
        cost_estimate=pl.CostEstimate(
            flops=2 * rows * width * (w + hid), bytes_accessed=rows * (w + 2 * hid + width) * 2, transcendentals=0
        ),
        name="branch_grads",
    )(g, gp, wd, wp)


def back_kernel(x, dqkv, dh, vec, wqkv, wfc, e_o, sum_o):
    @pl.when(pl.program_id(0) == 0)
    def _():
        sum_o[...] = jnp.zeros_like(sum_o)

    xh, _ = norm_rows(x[...].astype(F32))
    da = mm(dqkv[...], wqkv[...], NT)
    dm = mm(dh[...], wfc[...], NT)
    e_o[...] = (da * vec[0:1, :] + dm * vec[2:3, :]).astype(BF16)
    for j, part in enumerate((da * xh, da, dm * xh, dm)):
        sum_o[j : j + 1, :] += jnp.sum(part, axis=0, keepdims=True)


def back_call(x, dqkv, dh, vec, wqkv, wfc):
    rows, width = x.shape
    cols, hid = dqkv.shape[1], dh.shape[1]
    rb = 256
    sds = jax.ShapeDtypeStruct
    return pl.pallas_call(
        back_kernel,
        grid=(rows // rb,),
        in_specs=[
            rows_of(rb, width),
            rows_of(rb, cols),
            rows_of(rb, hid),
            whole(vec.shape),
            whole(wqkv.shape),
            whole(wfc.shape),
        ],
        out_specs=[rows_of(rb, width), whole((4, width))],
        out_shape=[sds((rows, width), BF16), sds((4, width), F32)],
        compiler_params=params(),
        cost_estimate=pl.CostEstimate(
            flops=2 * rows * width * (cols + hid), bytes_accessed=rows * (cols + hid + 2 * width) * 2, transcendentals=0
        ),
        name="norm_grads",
    )(x, dqkv, dh, vec, wqkv, wfc)


def both(a, b):
    return (a.astype(F32) + b.astype(F32)).astype(BF16)


def line_sum(pieces):
    index = lax.axis_index("batch")
    core, z = index % 2, index // 2
    mid = (z == 1) | (z == 2)
    swap = [(i, i ^ 1) for i in range(8)]
    outer = [(0, 2), (2, 0), (1, 3), (3, 1), (4, 6), (6, 4), (5, 7), (7, 5)]
    inner = [(2, 4), (4, 2), (3, 5), (5, 3)]
    count = len(pieces)
    mine, totals, done = {}, {}, {}
    for k in range(count + 2):
        if k < count:
            own = lax.dynamic_index_in_dim(pieces[k], core, 0, keepdims=False)
            other = lax.dynamic_index_in_dim(pieces[k], 1 - core, 0, keepdims=False)
            mine[k] = both(own, lax.ppermute(other, "batch", swap))
        if k < 2:
            send = mine[k]
        elif k < count:
            send = jnp.where(mid, totals[k - 2], mine[k])
        else:
            send = totals[k - 2]
        got = lax.ppermute(send, "batch", outer)
        if k < count:
            part = both(mine[k], got)
            totals[k] = both(part, lax.ppermute(part, "batch", inner))
        if k >= 2:
            total = jnp.where(mid, totals[k - 2], got)
            far = lax.ppermute(total, "batch", swap)
            done[k - 2] = jnp.stack([jnp.where(core == 0, total, far), jnp.where(core == 0, far, total)])
    return [done[k] for k in range(count)]


def sum_weight_grads(proj, fc, dense, qkv, n_batch):
    hid, width = proj.shape
    w = dense.shape[0]
    if n_batch != 8 or fc.shape != proj.shape or 4 * w != width:
        return tuple(lax.psum(a, "batch") for a in (proj, fc, dense, qkv))
    piece = (2, width // 4, width)
    half = width // 2
    last = jnp.concatenate([dense, qkv[:w]])
    pieces = [proj[:half], proj[half:], fc[:half], fc[half:], last, qkv[w:]]
    p0, p1, f0, f1, dq, q = (a.reshape(half, width) for a in line_sum([a.reshape(piece) for a in pieces]))
    return (
        jnp.concatenate([p0, p1]),
        jnp.concatenate([f0, f1]),
        dq[:w],
        jnp.concatenate([dq[w:], q]),
    )


def cosine_table(dimension):
    spatial = jnp.arange(dimension, dtype=F32)[:, None]
    frequency = jnp.arange(dimension, dtype=F32)[None, :]
    dct_table = jnp.cos(math.pi * (2.0 * spatial + 1.0) * frequency / (2.0 * dimension)) * math.sqrt(
        2.0 / dimension
    )
    return jnp.where(frequency == 0.0, dct_table * math.sqrt(0.5), dct_table)


def turn_tables(rows, hd):
    half = ROT // 2
    inverse_freq = jnp.exp(-math.log(10000.0) * 2.0 * jnp.arange(half, dtype=F32) / ROT)
    angles = jnp.arange(rows, dtype=F32)[:, None] * inverse_freq[None, :]
    cosines, sines = jnp.cos(angles), jnp.sin(angles)
    ones, zeros = jnp.ones((rows, hd - ROT), F32), jnp.zeros((rows, hd - ROT), F32)
    reps = 128 // hd
    return (
        jnp.tile(jnp.concatenate([cosines, cosines, ones], axis=1), (1, reps)),
        jnp.tile(jnp.concatenate([-sines, sines, zeros], axis=1), (1, reps)),
    )


def body(
    tokens,
    output_grad,
    attn_norm_gain,
    attn_norm_bias,
    mlp_norm_gain,
    mlp_norm_bias,
    qkv_weight,
    qkv_bias,
    dense_weight,
    dense_bias,
    fc_weight,
    fc_bias,
    proj_weight,
    feature_weight,
    seq_units,
    pad_tokens,
):
    rows_dev, width = tokens.shape
    parts = lax.axis_size("tensor")
    n_batch = lax.axis_size("batch")
    rows = rows_dev * parts
    heads, hd, _ = feature_weight.shape
    w = heads * hd
    hid = fc_weight.shape[1]

    vec = jnp.stack([attn_norm_gain, attn_norm_bias, mlp_norm_gain, mlp_norm_bias]).astype(F32)
    wqkv = qkv_weight.reshape(width, heads, 3, hd).transpose(0, 2, 1, 3).reshape(width, 3 * w)
    bqkv = qkv_bias.reshape(heads, 3, hd).transpose(1, 0, 2).reshape(1, 3 * w).astype(F32)
    dct = cosine_table(hd)
    cf = jnp.einsum("de,hem->hdm", dct, feature_weight.astype(F32), precision=lax.Precision.HIGHEST)
    eye = jnp.eye(heads, dtype=F32)
    cf_bd = (cf[:, :, None, :] * eye[:, None, :, None]).reshape(w, w)
    cf_pair = jnp.stack(split(cf_bd))
    cos_t, sin_t = turn_tables(rows, hd)

    x_all = lax.all_gather(tokens, "tensor", axis=0, tiled=True)
    g_all = lax.all_gather(output_grad, "tensor", axis=0, tiled=True)

    lna, lnm, qk, v, act, gp = fwd_call(
        x_all, vec, wqkv, bqkv, fc_weight, fc_bias.astype(F32).reshape(1, hid)
    )
    ao, o, rd, fq, fk, rq, rk, s, ks = attn_fwd_call(
        seq_units, pad_tokens, qk, v, cf_pair, cos_t, sin_t, hd, parts
    )
    branch = lax.psum_scatter(
        out_call(ao, act, dense_weight, proj_weight), "tensor", scatter_dimension=0, tiled=True
    )
    x_own = tokens.astype(F32)
    output = (x_own + branch.astype(F32) + dense_bias.astype(F32)).astype(BF16)

    dao, dh, fc_bias_sum = grad_call(g_all, gp, dense_weight, proj_weight)
    proj_grad = mm(act, g_all, TN).astype(BF16)
    dense_grad = mm(ao, g_all, TN).astype(BF16)
    fc_grad = mm(lnm, dh, TN).astype(BF16)
    dqkv, feat, qkv_bias_sum = attn_bwd_call(
        seq_units, pad_tokens, dao, v, o, rd, fq, fk, rq, rk, s, ks, cf_pair, cos_t, sin_t, hd, parts
    )
    qkv_grad = mm(dqkv, lna, TN).astype(BF16)
    e_part, norm_sums = back_call(x_all, dqkv, dh, vec, wqkv, fc_weight)
    e = lax.psum_scatter(e_part, "tensor", scatter_dimension=0, tiled=True).astype(F32)
    x_hat, inv_std = norm_rows(x_own)
    g_own = output_grad.astype(F32)
    tokens_grad = (
        g_own
        + inv_std
        * (e - jnp.mean(e, axis=-1, keepdims=True) - x_hat * jnp.mean(e * x_hat, axis=-1, keepdims=True))
    ).astype(BF16)

    proj_grad, fc_grad, dense_grad, qkv_grad = sum_weight_grads(
        proj_grad, fc_grad, dense_grad, qkv_grad, n_batch
    )
    proj_grad, fc_grad, dense_grad = (a.astype(F32) for a in (proj_grad, fc_grad, dense_grad))
    qkv_grad = (
        qkv_grad.reshape(3, heads, hd, width).transpose(3, 1, 0, 2).reshape(width, 3 * w).astype(F32)
    )

    feat_blocks = jnp.stack([feat[h * hd : (h + 1) * hd, h * hd : (h + 1) * hd] for h in range(heads)])
    feat_sum, qkv_bias_sum, fc_bias_sum = lax.psum((feat_blocks, qkv_bias_sum, fc_bias_sum), "batch")
    norm_sums, dense_bias_sum = lax.psum((norm_sums, jnp.sum(g_own, axis=0)), ("batch", "tensor"))
    feature_grad = jnp.einsum("de,hdm->hem", dct, feat_sum, precision=lax.Precision.HIGHEST)
    qkv_bias_grad = qkv_bias_sum.reshape(3, heads, hd).transpose(1, 0, 2).reshape(3 * w)
    return (
        output,
        tokens_grad,
        norm_sums[0],
        norm_sums[1],
        norm_sums[2],
        norm_sums[3],
        qkv_grad,
        qkv_bias_grad,
        dense_grad,
        dense_bias_sum,
        fc_grad,
        fc_bias_sum.reshape(hid),
        proj_grad,
        feature_grad,
    )


def solution(mesh):
    rows = P(("batch", "tensor"), None)
    placed = (
        rows,
        rows,
        P(),
        P(),
        P(),
        P(),
        P(None, "tensor"),
        P("tensor"),
        P("tensor", None),
        P(),
        P(None, "tensor"),
        P("tensor"),
        P("tensor", None),
        P("tensor", None, None),
        P("batch", None),
        P("batch", None),
    )
    return jax.shard_map(
        body,
        mesh=mesh,
        in_specs=placed,
        out_specs=(
            rows,
            rows,
            P(),
            P(),
            P(),
            P(),
            P(None, "tensor"),
            P("tensor"),
            P("tensor", None),
            P(),
            P(None, "tensor"),
            P("tensor"),
            P("tensor", None),
            P("tensor", None, None),
        ),
        check_vma=False,
    )
```

```python
from functools import partial
import math

import jax
import jax.numpy as jnp
import numpy as np
from jax import lax
from jax.experimental import pallas as pl
from jax.experimental.pallas import tpu as pltpu
from jax.sharding import PartitionSpec as P

ROT = 16
UNIT = 128
EPS = 1e-05
F32 = jnp.float32
BF16 = jnp.bfloat16
VMEM_BYTES = 54 * 1024 * 1024

NN = (((1,), (0,)), ((), ()))
NT = (((1,), (1,)), ((), ()))
TN = (((0,), (0,)), ((), ()))


def mm(a, b, dims=NN):
    return lax.dot_general(a, b, dims, preferred_element_type=F32)


def split(a):
    hi = a.astype(BF16)
    return hi, (a - hi.astype(F32)).astype(BF16)


HELD_SPACE = pl.ANY
SMALL_COST = pl.CostEstimate(flops=1000, bytes_accessed=1000, transcendentals=0)


def params(grid_rank=1):
    return pltpu.CompilerParams(
        dimension_semantics=("arbitrary",) * grid_rank, vmem_limit_bytes=VMEM_BYTES
    )


def whole(shape):
    return pl.BlockSpec(shape, lambda *_: (0,) * len(shape))


def rows_of(block, width):
    return pl.BlockSpec((block, width), lambda i: (i, 0))


def norm_rows(x):
    mean = jnp.mean(x, axis=-1, keepdims=True)
    cent = x - mean
    inv = lax.rsqrt(jnp.mean(cent * cent, axis=-1, keepdims=True) + EPS)
    return cent * inv, inv


def chunk_place(units, pads, chunk, nseq):
    start = jnp.int32(0)
    pos, real, last = jnp.int32(0), jnp.int32(0), jnp.int32(0)
    for n in range(nseq):
        u = units[0, n]
        inside = (chunk >= start) & (chunk < start + u)
        pos = jnp.where(inside, chunk - start, pos)
        real = jnp.where(inside, (start + u - chunk) * UNIT - pads[0, n], real)
        last = jnp.where(inside, (chunk == start + u - 1).astype(jnp.int32), last)
        start = start + u
    return pos, real, last


def lanes(table, w):
    return jnp.concatenate([table] * (w // table.shape[1]), axis=1) if w > table.shape[1] else table


def turn(a, cosines, sines, low_half):
    w = a.shape[1]
    other = jnp.where(low_half, pltpu.roll(a, w - ROT // 2, 1), pltpu.roll(a, ROT // 2, 1))
    return a * cosines + other * sines


def head_stack(a, head_of_lane, heads):
    zero = jnp.zeros_like(a)
    return jnp.concatenate([jnp.where(head_of_lane == h, a, zero) for h in range(heads)], axis=0)


def side_by_side(a, heads):
    return jnp.concatenate([a[h * UNIT : (h + 1) * UNIT, :] for h in range(heads)], axis=1)


def masks(w, hd):
    lane = lax.broadcasted_iota(jnp.int32, (UNIT, w), 1)
    head_of_lane = lane // hd
    bi = lax.broadcasted_iota(jnp.int32, (w, w), 0) // hd
    bj = lax.broadcasted_iota(jnp.int32, (w, w), 1) // hd
    heads = w // hd
    row = lax.broadcasted_iota(jnp.int32, (heads * UNIT, UNIT), 0) % UNIT
    col = lax.broadcasted_iota(jnp.int32, (heads * UNIT, UNIT), 1)
    return head_of_lane, bi == bj, row >= col


def prep_kernel(hd, wqkv, bqkv, feat, pick, dct_bd, *refs):
    wqkv_o, bqkv_o, cf_o = refs[-3:]
    w = dct_bd.shape[0]
    wqkv_o[...] = mm(wqkv[...], pick[...]).astype(BF16)
    bqkv_o[...] = mm(jnp.broadcast_to(bqkv[...], (8, 3 * w)), pick[...])
    diag = lax.broadcasted_iota(jnp.int32, (w, w), 0) // hd == lax.broadcasted_iota(jnp.int32, (w, w), 1) // hd
    spread = jnp.where(diag, jnp.concatenate([feat[...].astype(F32)] * (w // hd), axis=1), 0.0)
    cf_hi, cf_lo = split(
        lax.dot_general(dct_bd[...], spread, NN, precision=lax.Precision.HIGHEST, preferred_element_type=F32)
    )
    cf_o[0] = cf_hi
    cf_o[1] = cf_lo


def prep_call(wqkv, bqkv, feat, pick, dct_bd, hd, deps=()):
    width, cols = wqkv.shape
    w = cols // 3
    sds = jax.ShapeDtypeStruct
    return pl.pallas_call(
        partial(prep_kernel, hd),
        in_specs=[whole(a.shape) for a in (wqkv, bqkv, feat, pick, dct_bd)] + unread(deps),
        out_shape=[sds((width, cols), BF16), sds((8, cols), F32), sds((2, w, w), BF16)],
        compiler_params=pltpu.CompilerParams(vmem_limit_bytes=VMEM_BYTES),
        cost_estimate=SMALL_COST,
        name="prepare",
    )(wqkv, bqkv, feat, pick, dct_bd, *deps)


def gelu_pair(h):
    bell = jnp.exp(h * h * -0.5)
    t = 1.0 / (1.0 + jnp.abs(h) * (0.3275911 * math.sqrt(0.5)))
    tail = bell * (
        t * (0.5 * 0.254829592 + t * (0.5 * -0.284496736 + t * (0.5 * 1.421413741 + t * (0.5 * -1.453152027 + t * (0.5 * 1.061405429)))))
    )
    cdf = jnp.where(h < 0.0, tail, 1.0 - tail)
    return h * cdf, cdf + (h * bell) * (1.0 / math.sqrt(2.0 * math.pi))


def pick_rows(refs, slot, into):
    if len(refs) == 1:
        return refs[0][...]
    rb = into.shape[0]
    for j, ref in enumerate(refs):
        at = slice(0, rb) if j < 3 else slice(0, rb // 2) if j == 3 else slice(rb // 2, rb)

        @pl.when(slot == min(j, 3))
        def _():
            into[at, :] = ref[...]

    return into[...]


def rows_specs(arrays, rb, at):
    if len(arrays) == 1:
        return [pl.BlockSpec((rb, arrays[0].shape[1]), at)]
    return [const(a.shape) for a in arrays]


def put(outs, slot, value):
    if len(outs) == 1:
        outs[0][...] = value
        return
    rb, half = value.shape[0], value.shape[1] // 2
    keep_a, send_a, keep_b, send_b = outs
    for j, (a, b) in enumerate(((keep_a, keep_b), (send_a, keep_b), (keep_a, send_b), (send_a, send_b))):

        @pl.when(slot == j)
        def _():
            a[(j // 2) * rb : (j // 2 + 1) * rb, :] = value[:, :half]
            b[(j % 2) * rb : (j % 2 + 1) * rb, :] = value[:, half:]


def put_specs(apart, rb, width, total, at):
    if apart:
        shape = (2 * rb, width // 2)
        return [whole(shape)] * 4, [jax.ShapeDtypeStruct(shape, BF16)] * 4
    return [pl.BlockSpec((rb, width), at)], [jax.ShapeDtypeStruct((total, width), BF16)]


def unread(arrays):
    return [pl.BlockSpec(memory_space=pl.ANY)] * len(arrays)


def const(shape):
    return pl.BlockSpec(shape, lambda *_: (0,) * len(shape), pipeline_mode=pl.Buffered(1))


def forward_kernel(hd, shards, nseq, meta, units, pads, *refs):
    x_refs = refs[:shards]
    vec, wqkv, bqkv, wfc_a, wfc_b, bfc_a, bfc_b, cf, cos_t, sin_t, wd, wp_a, wp_b = refs[shards : shards + 13]
    lna_o, lnm_o, act_o, gp_o, fq_o, fk_o, rq_o, rk_o, v_o, ao_o, o_o, rd_o, s_o, ks_o = refs[shards + 13 : shards + 27]
    *outs, xbuf, state, ksum = refs[shards + 27 :]
    step = pl.program_id(0)
    slot = meta[step]
    w, hh, per = v_o.shape[1], bfc_a.shape[1], xbuf.shape[0] // UNIT
    heads = w // hd

    @pl.when(step == 0)
    def _():
        state[...] = jnp.zeros_like(state)
        ksum[...] = jnp.zeros_like(ksum)

    xh, _ = norm_rows(pick_rows(x_refs, slot, xbuf).astype(F32))
    lna = (xh * vec[0:1, :] + vec[1:2, :]).astype(BF16)
    lnm = (xh * vec[2:3, :] + vec[3:4, :]).astype(BF16)
    lna_o[...] = lna
    lnm_o[...] = lnm
    qkv = mm(lna, wqkv[...]) + bqkv[0:1, :]
    v_o[...] = qkv[:, 2 * w :].astype(BF16)
    for cols, wfc, bfc in ((slice(0, hh), wfc_a, bfc_a), (slice(hh, 2 * hh), wfc_b, bfc_b)):
        act, slope = gelu_pair(mm(lnm, wfc[...]) + bfc[...])
        act_o[:, cols] = act.astype(BF16)
        gp_o[:, cols] = slope.astype(BF16)

    head_of_lane, diag, causal = masks(w, hd)
    low_half = lax.broadcasted_iota(jnp.int32, (UNIT, w), 1) % hd < ROT // 2
    row_id = lax.broadcasted_iota(jnp.int32, (UNIT, 1), 0)
    ones_bd = jnp.where(diag, 1.0, 0.0).astype(BF16)
    head_ones = head_stack(jnp.ones((UNIT, w), BF16), head_of_lane, heads)
    cf_hi, cf_lo = cf[0], cf[1]
    for i in range(per):
        pos, real, _ = chunk_place(units, pads, step * per + i, nseq)
        at = pl.ds(pl.multiple_of(pos * UNIT, UNIT), UNIT)
        cosines = lanes(cos_t[at, :], w)
        sines = lanes(sin_t[at, :], w)
        rows = slice(i * UNIT, (i + 1) * UNIT)
        rq = turn(qkv[rows, 0:w], cosines, sines, low_half)
        rk = turn(qkv[rows, w : 2 * w], cosines, sines, low_half)
        qh, ql = split(rq)
        kh, kl = split(rk)
        rq_o[rows, :] = qh
        rk_o[rows, :] = kh
        fq = jnp.exp(mm(qh, cf_hi) + mm(ql, cf_hi) + mm(qh, cf_lo)).astype(BF16)
        ek = jnp.exp(mm(kh, cf_hi) + mm(kl, cf_hi) + mm(kh, cf_lo))
        fk = jnp.where(row_id < real, ek, 0.0).astype(BF16)
        fq_o[rows, :] = fq
        fk_o[rows, :] = fk
        v = v_o[rows, :]
        keep = jnp.where(pos == 0, 0.0, 1.0)
        s_old = state[...] * keep
        k_old = ksum[...] * keep
        s_hi, s_lo = split(s_old)
        s_o[i, 0] = s_hi
        s_o[i, 1] = s_lo
        ks_o[i] = k_old
        scores = jnp.where(causal, mm(head_stack(fq, head_of_lane, heads), fk, NT), 0.0).astype(BF16)
        wide = side_by_side(scores, heads)
        num = mm(wide, head_stack(v, head_of_lane, heads)) + mm(fq, s_hi) + mm(fq, s_lo)
        p_hi, p_lo = split(fq.astype(F32) * k_old)
        den = mm(wide, head_ones) + mm(p_hi, ones_bd) + mm(p_lo, ones_bd)
        rden = 1.0 / den
        o = num * rden
        o_o[rows, :] = o
        rd_o[rows, :] = rden
        ao_o[rows, :] = o.astype(BF16)
        state[...] = s_old + jnp.where(diag, mm(fk, v, TN), 0.0)
        ksum[...] = k_old + jnp.sum(fk.astype(F32), axis=0, keepdims=True)

    out = mm(ao_o[...], wd[...]) + mm(act_o[:, :hh], wp_a[...]) + mm(act_o[:, hh:], wp_b[...])
    put(outs, slot, out.astype(BF16))


def forward_call(meta, units, pads, xs, vec, wqkv, bqkv, wfc, bfc, cf, cos_t, sin_t, wd, wp, hd, parts, rows):
    width, cols = wqkv.shape
    w, hid = cols // 3, wfc.shape[1]
    hh = hid // 2
    rb = rows // parts
    per, n = rb // UNIT, rows // UNIT
    core = meta.shape[0] - 1
    smem = pl.BlockSpec(memory_space=pltpu.SMEM)
    sds = jax.ShapeDtypeStruct

    def at(i, m):
        return (m[i], 0)

    def half(shape, index):
        return pl.BlockSpec(shape, index, pipeline_mode=pl.Buffered(1))

    out_specs, out_shape = put_specs(len(xs) > 1, rb, width, rows, at)
    saved = [(width, BF16)] * 2 + [(hid, BF16)] * 2 + [(w, BF16)] * 6 + [(w, F32)] * 2
    return pl.pallas_call(
        partial(forward_kernel, hd, len(xs), units.shape[1]),
        grid_spec=pltpu.PrefetchScalarGridSpec(
            num_scalar_prefetch=1,
            grid=(parts,),
            in_specs=[smem, smem]
            + rows_specs(xs, rb, at)
            + [
                const(vec.shape),
                const(wqkv.shape),
                const(bqkv.shape),
                half((width, hh), lambda i, m: (0, m[core])),
                half((width, hh), lambda i, m: (0, 1 - m[core])),
                half((1, hh), lambda i, m: (0, m[core])),
                half((1, hh), lambda i, m: (0, 1 - m[core])),
                const(cf.shape),
                const(cos_t.shape),
                const(sin_t.shape),
                const(wd.shape),
                half((hh, width), lambda i, m: (m[core], 0)),
                half((hh, width), lambda i, m: (1 - m[core], 0)),
            ],
            out_specs=[pl.BlockSpec((rb, k), at) for k, _ in saved]
            + [
                pl.BlockSpec((per, 2, w, w), lambda i, m: (m[i], 0, 0, 0)),
                pl.BlockSpec((per, 1, w), lambda i, m: (m[i], 0, 0)),
            ]
            + out_specs,
            scratch_shapes=[pltpu.VMEM((rb, width), BF16), pltpu.VMEM((w, w), F32), pltpu.VMEM((1, w), F32)],
        ),
        out_shape=[sds((rows, k), t) for k, t in saved] + [sds((n, 2, w, w), BF16), sds((n, 1, w), F32)] + out_shape,
        compiler_params=params(),
        cost_estimate=SMALL_COST,
        name="forward",
    )(meta, units, pads, *xs, vec, wqkv, bqkv, wfc, wfc, bfc, bfc, cf, cos_t, sin_t, wd, wp, wp)


def grad_kernel(meta, g_ref, gp, wd, wp_a, wp_b, *refs):
    dao_o, dh_o, sum_o, g_sum_o = refs[-4:]

    @pl.when(pl.program_id(0) == 0)
    def _():
        sum_o[...] = jnp.zeros_like(sum_o)
        g_sum_o[...] = jnp.zeros_like(g_sum_o)

    hh = wp_a.shape[0]
    g = g_ref[...]
    g_sum_o[...] += jnp.sum(g.astype(F32), axis=0, keepdims=True)
    dao_o[...] = mm(g, wd[...], NT).astype(BF16)
    for cols, wp in ((slice(0, hh), wp_a), (slice(hh, 2 * hh), wp_b)):
        dh = (mm(g, wp[...], NT) * gp[:, cols].astype(F32)).astype(BF16)
        dh_o[:, cols] = dh
        sum_o[:, cols] += jnp.sum(dh.astype(F32), axis=0, keepdims=True)


def grad_call(meta, parts, g, gp, wd, wp, deps=()):
    rows, hid = gp.shape
    w, width = wd.shape
    rb = rows // parts
    core = meta.shape[0] - 1
    sds = jax.ShapeDtypeStruct

    def plain(n):
        return pl.BlockSpec((rb, n), lambda i, m: (i, 0))

    return pl.pallas_call(
        grad_kernel,
        grid_spec=pltpu.PrefetchScalarGridSpec(
            num_scalar_prefetch=1,
            grid=(parts,),
            in_specs=[
                plain(width),
                plain(hid),
                const(wd.shape),
                pl.BlockSpec((hid // 2, width), lambda i, m: (m[core], 0), pipeline_mode=pl.Buffered(1)),
                pl.BlockSpec((hid // 2, width), lambda i, m: (1 - m[core], 0), pipeline_mode=pl.Buffered(1)),
            ]
            + unread(deps),
            out_specs=[plain(w), plain(hid), whole((1, hid)), whole((1, width))],
        ),
        out_shape=[sds((rows, w), BF16), sds((rows, hid), BF16), sds((1, hid), F32), sds((1, width), F32)],
        compiler_params=params(),
        cost_estimate=SMALL_COST,
        name="branch_grads",
    )(meta, g, gp, wd, wp, wp, *deps)


def attn_bwd_kernel(
    hd, nseq, meta, units, pads, dao, v_ref, o_ref, rd_ref, fq_ref, fk_ref, rq_ref, rk_ref, s_ref, ks_ref,
    cf, cos_t, sin_t, dct_bd, *refs,
):
    dqkv_o, sum_o, feat_o, after, after_sum, feat = refs[-6:]
    w = v_ref.shape[1]
    heads = w // hd
    step = pl.program_id(0)
    block = pl.num_programs(0) - 1 - step
    per = dao.shape[0] // UNIT

    @pl.when(step == 0)
    def _():
        for ref in (after, after_sum, feat, sum_o):
            ref[...] = jnp.zeros_like(ref)

    head_of_lane, diag, causal = masks(w, hd)
    low_half = lax.broadcasted_iota(jnp.int32, (UNIT, w), 1) % hd < ROT // 2
    ones_bd = jnp.where(diag, 1.0, 0.0).astype(BF16)
    cf_hi, cf_lo = cf[0], cf[1]
    for i in reversed(range(per)):
        pos, _, last = chunk_place(units, pads, block * per + i, nseq)
        rows = slice(i * UNIT, (i + 1) * UNIT)
        at = pl.ds(pl.multiple_of(pos * UNIT, UNIT), UNIT)
        cosines = lanes(cos_t[at, :], w)
        sines = -lanes(sin_t[at, :], w)
        keep = jnp.where(last == 1, 0.0, 1.0)
        a_old = after[...] * keep
        as_old = after_sum[...] * keep
        fq, fk, v = fq_ref[rows, :], fk_ref[rows, :], v_ref[rows, :]
        fqf, fkf = fq.astype(F32), fk.astype(F32)
        dn = (dao[rows, :].astype(F32) * rd_ref[rows, :]).astype(BF16)
        p_hi, p_lo = split(dn.astype(F32) * o_ref[rows, :])
        dden = -(mm(p_hi, ones_bd) + mm(p_lo, ones_bd))
        dn_s = head_stack(dn, head_of_lane, heads)
        fq_s = head_stack(fq, head_of_lane, heads)
        dden_s = jnp.concatenate(
            [jnp.broadcast_to(dden[:, h * hd : h * hd + 1], (UNIT, UNIT)) for h in range(heads)], axis=0
        )
        da = jnp.where(causal, mm(dn_s, v, NT) + dden_s, 0.0).astype(BF16)
        a = jnp.where(causal, mm(fq_s, fk, NT), 0.0).astype(BF16)
        s_hi, s_lo = s_ref[i, 0], s_ref[i, 1]
        dfq = (
            mm(side_by_side(da, heads), head_stack(fk, head_of_lane, heads))
            + mm(dn, s_hi, NT)
            + mm(dn, s_lo, NT)
            + dden * ks_ref[i]
        )
        a_hi, a_lo = split(a_old)
        dfk = mm(da, fq_s, TN) + mm(v, a_hi, NT) + mm(v, a_lo, NT) + as_old
        dv = mm(a, dn_s, TN) + mm(fk, a_hi) + mm(fk, a_lo)
        after[...] = a_old + jnp.where(diag, mm(fq, dn, TN), 0.0)
        after_sum[...] = as_old + jnp.sum(fqf * dden, axis=0, keepdims=True)
        dsq = (dfq * fqf).astype(BF16)
        dsk = (dfk * fkf).astype(BF16)
        feat[...] += mm(rq_ref[rows, :], dsq, TN) + mm(rk_ref[rows, :], dsk, TN)
        dq = turn(mm(dsq, cf_hi, NT) + mm(dsq, cf_lo, NT), cosines, sines, low_half)
        dk = turn(mm(dsk, cf_hi, NT) + mm(dsk, cf_lo, NT), cosines, sines, low_half)
        for j, part in enumerate((dq, dk, dv)):
            part = part.astype(BF16)
            dqkv_o[rows, j * w : (j + 1) * w] = part
            sum_o[:, j * w : (j + 1) * w] += jnp.sum(part.astype(F32), axis=0, keepdims=True)

    @pl.when(block == 0)
    def _():
        turned = lax.dot_general(
            dct_bd[...],
            jnp.where(diag, feat[...], 0.0),
            TN,
            precision=lax.Precision.HIGHEST,
            preferred_element_type=F32,
        )
        total = turned[0:hd, :]
        for h in range(1, heads):
            total = total + turned[h * hd : (h + 1) * hd, :]
        feat_o[...] = total


def attn_bwd_call(meta, units, pads, dao, v, o, rd, fq, fk, rq, rk, s, ks, cf, cos_t, sin_t, dct_bd, hd, parts, deps=()):
    rows, w = v.shape
    rb = rows // parts
    per = rb // UNIT
    smem = pl.BlockSpec(memory_space=pltpu.SMEM)
    sds = jax.ShapeDtypeStruct

    def at(i, m):
        return (m[parts - 1 - i], 0)

    return pl.pallas_call(
        partial(attn_bwd_kernel, hd, units.shape[1]),
        grid_spec=pltpu.PrefetchScalarGridSpec(
            num_scalar_prefetch=1,
            grid=(parts,),
            in_specs=[smem, smem]
            + [pl.BlockSpec((rb, w), at)] * 8
            + [
                pl.BlockSpec((per, 2, w, w), lambda i, m: (m[parts - 1 - i], 0, 0, 0)),
                pl.BlockSpec((per, 1, w), lambda i, m: (m[parts - 1 - i], 0, 0)),
                const(cf.shape),
                const(cos_t.shape),
                const(sin_t.shape),
                const(dct_bd.shape),
            ]
            + unread(deps),
            out_specs=[pl.BlockSpec((rb, 3 * w), at), whole((1, 3 * w)), whole((hd, w))],
            scratch_shapes=[pltpu.VMEM((w, w), F32), pltpu.VMEM((1, w), F32), pltpu.VMEM((w, w), F32)],
        ),
        out_shape=[sds((rows, 3 * w), BF16), sds((1, 3 * w), F32), sds((hd, w), F32)],
        compiler_params=params(),
        cost_estimate=SMALL_COST,
        name="attn_bwd",
    )(meta, units, pads, dao, v, o, rd, fq, fk, rq, rk, s, ks, cf, cos_t, sin_t, dct_bd, *deps)


SMALL_ROWS = 32


def norms_kernel(shards, deps, meta, *refs):
    x_refs = refs[:shards]
    dqkv, dh, vec, wqkv, wfc_a, wfc_b, g_sum, hid_sum, qkv_sum, feat, *rest = refs[shards:]
    small_o, *outs, xbuf = rest[deps:]
    step = pl.program_id(0)
    hh = wfc_a.shape[1]
    slot = step

    @pl.when(step == 0)
    def _():
        small_o[...] = jnp.zeros_like(small_o)
        hid_row = hid_sum[...]
        swapped = jnp.concatenate([hid_row[:, hh:], hid_row[:, :hh]], axis=1)
        hid_row = jnp.where(meta[meta.shape[0] - 1] == 1, swapped, hid_row)
        for at, row in ((4, g_sum[...]), (5, hid_row), (6, qkv_sum[...])):
            small_o[at : at + 1, 0 : row.shape[1]] = row
        deep, w = feat.shape
        each = deep * w // small_o.shape[1]
        for j in range(deep // each):
            small_o[8 : 8 + each, j * w : (j + 1) * w] = feat[j * each : (j + 1) * each, :]

    xh, _ = norm_rows(pick_rows(x_refs, slot, xbuf).astype(F32))
    da = mm(dqkv[...], wqkv[...], NT)
    small_o[0:1, :] += jnp.sum(da * xh, axis=0, keepdims=True)
    small_o[1:2, :] += jnp.sum(da, axis=0, keepdims=True)
    dm = mm(dh[:, :hh], wfc_a[...], NT) + mm(dh[:, hh:], wfc_b[...], NT)
    small_o[2:3, :] += jnp.sum(dm * xh, axis=0, keepdims=True)
    small_o[3:4, :] += jnp.sum(dm, axis=0, keepdims=True)
    put(outs, slot, (da * vec[0:1, :] + dm * vec[2:3, :]).astype(BF16))


def norms_call(meta, parts, xs, dqkv, dh, vec, wqkv, wfc, g_sum, hid_sum, qkv_sum, feat, deps=()):
    rows, hid = dh.shape
    width, cols = wqkv.shape
    hh = hid // 2
    rb = rows // parts
    core = meta.shape[0] - 1

    def at(i, m):
        return (i, 0)

    def to(i, m):
        return (m[i], 0)

    def half(shape, index):
        return pl.BlockSpec(shape, index, pipeline_mode=pl.Buffered(1))

    out_specs, out_shape = put_specs(len(xs) > 1, rb, width, rows, at)
    small = (SMALL_ROWS, width)
    return pl.pallas_call(
        partial(norms_kernel, len(xs), len(deps)),
        grid_spec=pltpu.PrefetchScalarGridSpec(
            num_scalar_prefetch=1,
            grid=(parts,),
            in_specs=rows_specs(xs, rb, at)
            + [
                pl.BlockSpec((rb, cols), at),
                pl.BlockSpec((rb, hid), at),
                const(vec.shape),
                const(wqkv.shape),
                half((width, hh), lambda i, m: (0, m[core])),
                half((width, hh), lambda i, m: (0, 1 - m[core])),
                const(g_sum.shape),
                const(hid_sum.shape),
                const(qkv_sum.shape),
                const(feat.shape),
            ]
            + unread(deps),
            out_specs=[whole(small)] + out_specs,
            scratch_shapes=[pltpu.VMEM((rb, width), BF16)],
        ),
        out_shape=[jax.ShapeDtypeStruct(small, F32)] + out_shape,
        compiler_params=params(),
        cost_estimate=SMALL_COST,
        name="norm_grads",
    )(meta, *xs, dqkv, dh, vec, wqkv, wfc, wfc, g_sum, hid_sum, qkv_sum, feat, *deps)


class Order:
    def __init__(self):
        self.last = None

    def after(self, *arrays):
        if self.last is None:
            return arrays if len(arrays) > 1 else arrays[0]
        self.last, *arrays = lax.optimization_barrier((self.last, *arrays))
        return tuple(arrays) if len(arrays) > 1 else arrays[0]

    def did(self, array):
        self.last = array
        return array


def both(a, b):
    return (a.astype(F32) + b.astype(F32)).astype(a.dtype)


def totals_kernel(count, mid, *refs):
    total = refs[-1]
    rows = refs[0].shape[0]
    for k in range(count):
        own, sent = refs[2 * k], refs[2 * k + 1]

        @pl.when(mid[0] == 1)
        def _():
            total[k * rows : (k + 1) * rows, :] = own[...]

        @pl.when(mid[0] == 0)
        def _():
            total[k * rows : (k + 1) * rows, :] = sent[...]


def totals_call(mid, pairs, deps):
    rows, cols = pairs[0].shape
    count = len(pairs) // 2
    return pl.pallas_call(
        partial(totals_kernel, count),
        in_specs=[pl.BlockSpec(memory_space=pltpu.SMEM)] + [whole((rows, cols))] * len(pairs) + unread(deps),
        out_specs=whole((count * rows, cols)),
        out_shape=jax.ShapeDtypeStruct((count * rows, cols), BF16),
        compiler_params=pltpu.CompilerParams(vmem_limit_bytes=VMEM_BYTES),
        cost_estimate=SMALL_COST,
        name="totals",
    )(mid.astype(jnp.int32).reshape(1), *pairs, *deps)


class Line:
    swap = [(i, i ^ 1) for i in range(8)]
    inward = [(0, 2), (1, 3), (6, 4), (7, 5)]
    inner = [(2, 4), (4, 2), (3, 5), (5, 3)]
    outward = [(2, 0), (3, 1), (4, 6), (5, 7)]

    def __init__(self, order):
        index = lax.axis_index("batch")
        self.order = order
        self.core, z = index % 2, index // 2
        self.mid = (z == 1) | (z == 2)
        self.own, self.sent = {}, {}

    def start(self, k, own, other):
        self.own[k], self.sent[k] = own, lax.ppermute(other, "batch", self.swap)

    def add(self, k, to):
        own, sent = self.order.after(self.own[k], self.sent[k])
        self.own[k] = self.order.did(both(own, sent))
        self.sent[k] = lax.ppermute(self.own[k], "batch", to)

    def go_in(self, k):
        self.add(k, self.inward)

    def meet(self, k):
        self.add(k, self.inner)

    def go_out(self, k):
        self.add(k, self.outward)

    def held(self, *ks):
        return tuple(self.own[k] for k in ks)

    def arrived(self, *ks):
        return tuple(self.sent[k] for k in ks)

    def landed(self, *ks):
        for k in ks:
            self.own[k], self.sent[k] = self.order.after(self.own[k], self.sent[k])

    def end(self, *ks, deps=()):
        self.landed(*ks)
        if deps:
            total = totals_call(self.mid, [a for k in ks for a in (self.own[k], self.sent[k])], deps)
        else:
            total = jnp.concatenate([jnp.where(self.mid, self.own[k], self.sent[k]) for k in ks])
        total = self.order.did(total)
        return total, lax.ppermute(total, "batch", self.swap)

    def end_small(self, k):
        self.landed(k)
        return jnp.where(self.mid, self.own[k], self.sent[k])


def across(a, mask):
    return lax.ppermute(a, "tensor", [(i, i ^ mask) for i in range(4)])


def part_of_batch(a):
    return lax.psum_scatter(a, "batch", scatter_dimension=0, tiled=True)


class TwoStepSum:
    def __init__(self, order, blocks):
        self.order = order
        self.keep_a, send_a, self.keep_b, send_b = blocks
        self.got_a, self.got_b = across(send_a, 1), across(send_b, 2)

    def second(self):
        rb = self.keep_a.shape[0] // 2
        self.got_a, self.got_b = self.order.after(self.got_a, self.got_b)
        a = both(self.keep_a[rb:], self.got_a[rb:])
        b = both(self.keep_b[rb:], self.got_b[rb:])
        a, b = lax.optimization_barrier((a, b))
        self.order.did(b)
        self.last_a, self.last_b = across(a, 2), across(b, 1)

    def result(self):
        rb = self.keep_a.shape[0] // 2
        terms = ((self.keep_a, self.got_a, self.last_a), (self.keep_b, self.got_b, self.last_b))
        return jnp.concatenate([sum(t[:rb].astype(F32) for t in side) for side in terms], axis=1)


def cosine_blocks(hd, heads):
    spatial = np.arange(hd, dtype=np.float64)[:, None]
    frequency = np.arange(hd, dtype=np.float64)[None, :]
    table = np.cos(math.pi * (2.0 * spatial + 1.0) * frequency / (2.0 * hd)) * math.sqrt(2.0 / hd)
    table[:, 0] *= math.sqrt(0.5)
    return np.kron(np.eye(heads), table).astype(np.float32)


def turn_tables(rows, hd):
    half = ROT // 2
    inverse_freq = np.exp(-math.log(10000.0) * 2.0 * np.arange(half) / ROT)
    angles = np.arange(rows)[:, None] * inverse_freq[None, :]
    cosines, sines = np.cos(angles), np.sin(angles)
    rest = np.ones((rows, hd - ROT))
    reps = (1, 128 // hd)
    return (
        np.tile(np.concatenate([cosines, cosines, rest], axis=1), reps).astype(np.float32),
        np.tile(np.concatenate([-sines, sines, 0.0 * rest], axis=1), reps).astype(np.float32),
    )


def column_pick(heads, hd):
    n = 3 * heads * hd
    source = np.arange(n).reshape(heads, 3, hd).transpose(1, 0, 2).reshape(-1)
    pick = np.zeros((n, n), np.float32)
    pick[source, np.arange(n)] = 1.0
    return pick


def body(
    tokens,
    output_grad,
    attn_norm_gain,
    attn_norm_bias,
    mlp_norm_gain,
    mlp_norm_bias,
    qkv_weight,
    qkv_bias,
    dense_weight,
    dense_bias,
    fc_weight,
    fc_bias,
    proj_weight,
    feature_weight,
    seq_units,
    pad_tokens,
):
    rows_dev, width = tokens.shape
    parts = lax.axis_size("tensor")
    n_batch = lax.axis_size("batch")
    rows = rows_dev * parts
    heads, hd, _ = feature_weight.shape
    w = heads * hd
    hid = fc_weight.shape[1]

    square = parts == 4 and n_batch == 8 and hid == width and 4 * w == width
    position = lax.axis_index("tensor")
    order = Order()
    line = Line(order) if square else None
    slots = jnp.arange(parts, dtype=jnp.int32)
    core = jnp.int32(0)
    if square:
        slots = slots ^ position
        core = line.core
        mid = rows_dev // 2
        a1, a2 = across(tokens, 1), across(tokens, 2)
    tail = jnp.stack([jnp.int32(rows_dev // UNIT), core.astype(jnp.int32)])
    meta = jnp.concatenate([slots, tail])
    vec = jnp.stack([attn_norm_gain, attn_norm_bias, mlp_norm_gain, mlp_norm_bias]).astype(F32)
    dct_bd = jnp.asarray(cosine_blocks(hd, heads))
    cos_t, sin_t = (jnp.asarray(t) for t in turn_tables(rows, hd))
    pick = jnp.asarray(column_pick(heads, hd)).astype(BF16)
    bfc = fc_bias.astype(F32).reshape(1, hid)
    wqkv, bqkv, cf_pair = prep_call(
        qkv_weight, qkv_bias.reshape(1, 3 * w), feature_weight.reshape(w, hd), pick, dct_bd, hd, (meta, vec, bfc)
    )
    hh = hid // 2
    dm = width // 2
    g_float = output_grad.astype(F32)
    x_own = tokens.astype(F32)
    if square:
        order.did(wqkv)
        a1, a2 = order.after(a1, a2)
        b1, b2 = across(a1[:mid], 2), across(a2[mid:], 1)
        b1, b2 = order.after(b1, b2)
        g_own, b1, b2 = lax.optimization_barrier((output_grad, b1, b2))
        c1, c2, c3 = across(g_own, 1), across(g_own, 2), across(g_own, 3)
        xs = [tokens, a1, a2, b1, b2]
    else:
        xs = [lax.all_gather(tokens, "tensor", axis=0, tiled=True)]
        g_all = lax.all_gather(output_grad, "tensor", axis=0, tiled=True)
    lna, lnm, act, gp, fq, fk, rq, rk, v, ao, o, rd, s, ks, *outs = forward_call(
        meta, seq_units, pad_tokens, xs, vec, wqkv, bqkv, fc_weight, bfc, cf_pair, cos_t, sin_t,
        dense_weight, proj_weight, hd, parts, rows,
    )
    order.did(ao)
    def residual(total):
        return (x_own + total + dense_bias.astype(F32)).astype(BF16)

    def proj_piece(k, cols):
        g = order.after(g_all)[:, cols]
        line.start(k, mm(act[:, :hh], g, TN).astype(BF16), order.did(mm(act[:, hh:], g, TN).astype(BF16)))

    def fc_piece(k, cols):
        part = order.after(lnm)[:, cols]
        line.start(k, mm(part, dh[:, :hh], TN).astype(BF16), order.did(mm(part, dh[:, hh:], TN).astype(BF16)))

    def rest_piece(k, cols):
        part, cotangent = order.after(lna, dqkv)
        stack = jnp.concatenate([mm(ao, g_all[:, cols], TN), mm(cotangent, part[:, cols], TN)])
        stack = stack.astype(BF16).reshape(2, 2 * w, dm)
        own = lax.dynamic_index_in_dim(stack, line.core, 0, keepdims=False)
        other = lax.dynamic_index_in_dim(stack, 1 - line.core, 0, keepdims=False)
        order.did(other)
        line.start(k, own, other)

    left, right = slice(0, dm), slice(dm, width)
    if square:
        branch = TwoStepSum(order, outs)
        c1, c2, c3 = order.after(c1, c2, c3)
        g_all = order.did(jnp.concatenate([output_grad, c1, c2, c3]))
        proj_piece(0, left)
        proj_piece(1, right)
        line.go_in(0)
        line.go_in(1)
        g_all = order.after(g_all)
    dao, dh, hid_sum, g_sum = grad_call(meta, parts, g_all, gp, dense_weight, proj_weight, line.held(0, 1) if square else ())
    order.did(dao)
    if square:
        branch.second()
        line.meet(0)
        fc_piece(2, left)
        line.go_in(2)
        fc_piece(3, right)
        line.meet(1)
        branch.last_a, branch.last_b = order.after(branch.last_a, branch.last_b)
        output = order.did(residual(branch.result()))
        line.go_out(0)
        line.go_in(3)
    dao = order.after(dao)
    dqkv, qkv_sum, feat = attn_bwd_call(
        meta, seq_units, pad_tokens, dao, v, o, rd, fq, fk, rq, rk, s, ks, cf_pair, cos_t, sin_t, dct_bd, hd, parts,
        (*line.held(0, 1, 2, 3), output) if square else (),
    )
    order.did(dqkv)
    if square:
        line.meet(2)
        line.go_out(1)
        rest_piece(4, left)
        line.landed(0)
        line.meet(3)
        line.go_in(4)
        rest_piece(5, right)
        line.go_in(5)
        line.landed(1)
        line.go_out(2)
    dqkv = order.after(dqkv)
    small, *es = norms_call(meta, parts, xs, dqkv, dh, vec, wqkv, fc_weight, g_sum, hid_sum, qkv_sum, feat,
        (*line.held(2, 3, 4, 5), *line.arrived(0, 1)) if square else ())
    order.did(small)

    def rows_grad(e):
        x_hat, inv_std = norm_rows(x_own)
        mean = jnp.mean(e, axis=-1, keepdims=True)
        return (g_float + inv_std * (e - mean - x_hat * jnp.mean(e * x_hat, axis=-1, keepdims=True))).astype(BF16)

    if square:
        line.meet(4)
        line.go_out(3)
        line.landed(2)
        small = order.after(small)
        line.start(6, small, small)
        es[1], es[3] = order.after(es[1], es[3])
        e_sum = TwoStepSum(order, es)
        line.go_in(6)
        line.meet(5)
        line.landed(3)
        first = line.end(0, 1, 2, 3)
        line.meet(6)
        line.go_out(4)
        second = line.core == 1

        def pieces_of(pair, count):
            own, twin = order.after(*pair)
            low = jnp.where(second, twin, own).reshape(count, 2 * w, dm)
            high = jnp.where(second, own, twin).reshape(count, 2 * w, dm)
            return low, high

        low, high = pieces_of(first, 4)
        proj_grad = order.did(
            jnp.concatenate(
                [jnp.concatenate([low[k], high[k]], axis=0) for k in (0, 1)], axis=1
            ).astype(F32)
        )
        e_sum.second()
        line.go_out(6)
        fc_grad = order.did(
            jnp.concatenate([jnp.concatenate([low[k], high[k]], axis=1) for k in (2, 3)], axis=0).astype(F32)
        )
        line.go_out(5)
        small = order.did(line.end_small(6))
        norm_sums = small[:8]
        hop = across(norm_sums, 1)
        e_sum.last_a, e_sum.last_b = order.after(e_sum.last_a, e_sum.last_b)
        tokens_grad = order.did(rows_grad(e_sum.result()))
        norm_sums = order.did(norm_sums + order.after(hop))
        hop = across(norm_sums, 2)
        last = line.end(4, 5, deps=(proj_grad, fc_grad, tokens_grad, norm_sums))
        norm_sums = norm_sums + order.after(hop)
        low, high = pieces_of(last, 2)
        rest = jnp.concatenate([jnp.concatenate([low[k], high[k]], axis=0) for k in (0, 1)], axis=1)
        dense_grad, qkv_grad = rest[:w].astype(F32), rest[w:]
        hid_sum = small[5]
        pick = jnp.asarray(column_pick(heads, hd)).astype(BF16)
        qkv_grad = lax.dot_general(qkv_grad.astype(BF16), pick, (((0,), (1,)), ((), ())), preferred_element_type=F32)
    else:
        output = residual(lax.psum_scatter(outs[0], "tensor", scatter_dimension=0, tiled=True).astype(F32))
        tokens_grad = rows_grad(lax.psum_scatter(es[0], "tensor", scatter_dimension=0, tiled=True).astype(F32))
        sums = [mm(act, g_all, TN), mm(lnm, dh, TN), mm(ao, g_all, TN), mm(dqkv, lna, TN)]
        sums = lax.psum([a.astype(BF16) for a in sums], "batch")
        proj_grad, fc_grad, dense_grad, qkv_grad = (a.astype(F32) for a in sums)
        small = lax.psum(small, "batch")
        norm_sums = lax.psum(small[:4], "tensor")
        hid_sum = small[5, :hid]
        qkv_grad = qkv_grad.reshape(3, heads, hd, width).transpose(3, 1, 0, 2).reshape(width, 3 * w)
    each = hd * w // width
    feature_grad = small[8 : 8 + each].reshape(each, width // w, heads, hd).transpose(2, 1, 0, 3).reshape(heads, hd, hd)
    qkv_bias_grad = small[6, : 3 * w].reshape(3, heads, hd).transpose(1, 0, 2).reshape(3 * w)

    return (
        output,
        tokens_grad,
        norm_sums[0],
        norm_sums[1],
        norm_sums[2],
        norm_sums[3],
        qkv_grad,
        qkv_bias_grad,
        dense_grad,
        small[4],
        fc_grad,
        hid_sum,
        proj_grad,
        feature_grad,
    )


def solution(mesh):
    rows = P(("batch", "tensor"), None)
    placed = (
        rows,
        rows,
        P(),
        P(),
        P(),
        P(),
        P(None, "tensor"),
        P("tensor"),
        P("tensor", None),
        P(),
        P(None, "tensor"),
        P("tensor"),
        P("tensor", None),
        P("tensor", None, None),
        P("batch", None),
        P("batch", None),
    )
    return jax.shard_map(
        body,
        mesh=mesh,
        in_specs=placed,
        out_specs=(
            rows,
            rows,
            P(),
            P(),
            P(),
            P(),
            P(None, "tensor"),
            P("tensor"),
            P("tensor", None),
            P(),
            P(None, "tensor"),
            P("tensor"),
            P("tensor", None),
            P("tensor", None, None),
        ),
        check_vma=False,
    )
```

```python
from functools import partial
import math

import jax
import jax.numpy as jnp
import numpy as np
from jax import lax
from jax.experimental import pallas as pl
from jax.experimental.pallas import tpu as pltpu
from jax.sharding import PartitionSpec as P

ROT = 16
UNIT = 128
EPS = 1e-05
F32 = jnp.float32
BF16 = jnp.bfloat16
VMEM_BYTES = 54 * 1024 * 1024

NN = (((1,), (0,)), ((), ()))
NT = (((1,), (1,)), ((), ()))
TN = (((0,), (0,)), ((), ()))


def mm(a, b, dims=NN):
    return lax.dot_general(a, b, dims, preferred_element_type=F32)


def split(a):
    hi = a.astype(BF16)
    return hi, (a - hi.astype(F32)).astype(BF16)


HELD_SPACE = pl.ANY
SMALL_COST = pl.CostEstimate(flops=1000, bytes_accessed=1000, transcendentals=0)


def params(grid_rank=1):
    return pltpu.CompilerParams(
        dimension_semantics=("arbitrary",) * grid_rank, vmem_limit_bytes=VMEM_BYTES
    )


def whole(shape):
    return pl.BlockSpec(shape, lambda *_: (0,) * len(shape))


def rows_of(block, width):
    return pl.BlockSpec((block, width), lambda i: (i, 0))


def norm_rows(x):
    mean = jnp.mean(x, axis=-1, keepdims=True)
    cent = x - mean
    inv = lax.rsqrt(jnp.mean(cent * cent, axis=-1, keepdims=True) + EPS)
    return cent * inv, inv


def chunk_place(units, pads, chunk, nseq):
    start = jnp.int32(0)
    pos, real, last = jnp.int32(0), jnp.int32(0), jnp.int32(0)
    for n in range(nseq):
        u = units[0, n]
        inside = (chunk >= start) & (chunk < start + u)
        pos = jnp.where(inside, chunk - start, pos)
        real = jnp.where(inside, (start + u - chunk) * UNIT - pads[0, n], real)
        last = jnp.where(inside, (chunk == start + u - 1).astype(jnp.int32), last)
        start = start + u
    return pos, real, last


def lanes(table, w):
    return jnp.concatenate([table] * (w // table.shape[1]), axis=1) if w > table.shape[1] else table


def turn(a, cosines, sines, low_half):
    w = a.shape[1]
    other = jnp.where(low_half, pltpu.roll(a, w - ROT // 2, 1), pltpu.roll(a, ROT // 2, 1))
    return a * cosines + other * sines


def head_stack(a, head_of_lane, heads):
    zero = jnp.zeros_like(a)
    return jnp.concatenate([jnp.where(head_of_lane == h, a, zero) for h in range(heads)], axis=0)


def side_by_side(a, heads):
    return jnp.concatenate([a[h * UNIT : (h + 1) * UNIT, :] for h in range(heads)], axis=1)


def masks(w, hd):
    lane = lax.broadcasted_iota(jnp.int32, (UNIT, w), 1)
    head_of_lane = lane // hd
    bi = lax.broadcasted_iota(jnp.int32, (w, w), 0) // hd
    bj = lax.broadcasted_iota(jnp.int32, (w, w), 1) // hd
    heads = w // hd
    row = lax.broadcasted_iota(jnp.int32, (heads * UNIT, UNIT), 0) % UNIT
    col = lax.broadcasted_iota(jnp.int32, (heads * UNIT, UNIT), 1)
    return head_of_lane, bi == bj, row >= col


def prep_kernel(hd, wqkv, bqkv, feat, pick, dct_bd, *refs):
    wqkv_o, bqkv_o, cf_o = refs[-3:]
    w = dct_bd.shape[0]
    wqkv_o[...] = mm(wqkv[...], pick[...]).astype(BF16)
    bqkv_o[...] = mm(jnp.broadcast_to(bqkv[...], (8, 3 * w)), pick[...])
    diag = lax.broadcasted_iota(jnp.int32, (w, w), 0) // hd == lax.broadcasted_iota(jnp.int32, (w, w), 1) // hd
    spread = jnp.where(diag, jnp.concatenate([feat[...].astype(F32)] * (w // hd), axis=1), 0.0)
    cf_hi, cf_lo = split(
        lax.dot_general(dct_bd[...], spread, NN, precision=lax.Precision.HIGHEST, preferred_element_type=F32)
    )
    cf_o[0] = cf_hi
    cf_o[1] = cf_lo
    back_hi, back_lo = split(
        lax.dot_general(spread, dct_bd[...], (((0,), (1,)), ((), ())), precision=lax.Precision.HIGHEST, preferred_element_type=F32)
    )
    cf_o[2] = back_hi
    cf_o[3] = back_lo


def prep_call(wqkv, bqkv, feat, pick, dct_bd, hd, deps=()):
    width, cols = wqkv.shape
    w = cols // 3
    sds = jax.ShapeDtypeStruct
    return pl.pallas_call(
        partial(prep_kernel, hd),
        in_specs=[whole(a.shape) for a in (wqkv, bqkv, feat, pick, dct_bd)] + unread(deps),
        out_shape=[sds((width, cols), BF16), sds((8, cols), F32), sds((4, w, w), BF16)],
        compiler_params=pltpu.CompilerParams(vmem_limit_bytes=VMEM_BYTES),
        cost_estimate=SMALL_COST,
        name="prepare",
    )(wqkv, bqkv, feat, pick, dct_bd, *deps)


def gelu_pair(h):
    bell = jnp.exp(h * h * -0.5)
    cdf = 0.5 + 0.5 * lax.erf(h * math.sqrt(0.5))
    return h * cdf, cdf + (h * bell) * (1.0 / math.sqrt(2.0 * math.pi))


def pick_rows(refs, slot, into):
    if len(refs) == 1:
        return refs[0][...]
    rb = into.shape[0]
    for j, ref in enumerate(refs):
        at = slice(0, rb) if j < 3 else slice(0, rb // 2) if j == 3 else slice(rb // 2, rb)

        @pl.when(slot == min(j, 3))
        def _():
            into[at, :] = ref[...]

    return into[...]


def rows_specs(arrays, rb, at):
    if len(arrays) == 1:
        return [pl.BlockSpec((rb, arrays[0].shape[1]), at)]
    return [const(a.shape) for a in arrays]


def put(outs, slot, value):
    if len(outs) == 1:
        outs[0][...] = value
        return
    rb, half = value.shape[0], value.shape[1] // 2
    keep_a, send_a, keep_b, send_b = outs
    for j, (a, b) in enumerate(((keep_a, keep_b), (send_a, keep_b), (keep_a, send_b), (send_a, send_b))):

        @pl.when(slot == j)
        def _():
            a[(j // 2) * rb : (j // 2 + 1) * rb, :] = value[:, :half]
            b[(j % 2) * rb : (j % 2 + 1) * rb, :] = value[:, half:]


def put_specs(apart, rb, width, total, at):
    if apart:
        shape = (2 * rb, width // 2)
        return [whole(shape)] * 4, [jax.ShapeDtypeStruct(shape, BF16)] * 4
    return [pl.BlockSpec((rb, width), at)], [jax.ShapeDtypeStruct((total, width), BF16)]


def unread(arrays):
    return [pl.BlockSpec(memory_space=pl.ANY)] * len(arrays)


def const(shape):
    return pl.BlockSpec(shape, lambda *_: (0,) * len(shape), pipeline_mode=pl.Buffered(1))


def forward_kernel(hd, shards, nseq, meta, units, pads, *refs):
    x_refs = refs[:shards]
    vec, wqkv, bqkv, wfc_a, wfc_b, bfc_a, bfc_b, cf, cos_t, sin_t, wd, wp_a, wp_b = refs[shards : shards + 13]
    lna_o, lnm_o, act_o, gp_o, fq_o, fk_o, rq_o, rk_o, v_o, ao_o, o_o, rd_o, s_o, ks_o = refs[shards + 13 : shards + 27]
    *outs, xbuf, state, ksum = refs[shards + 27 :]
    step = pl.program_id(0)
    slot = meta[step]
    w, hh, per = v_o.shape[1], bfc_a.shape[1], xbuf.shape[0] // UNIT
    heads = w // hd

    @pl.when(step == 0)
    def _():
        state[...] = jnp.zeros_like(state)
        ksum[...] = jnp.zeros_like(ksum)

    xh, _ = norm_rows(pick_rows(x_refs, slot, xbuf).astype(F32))
    lna = (xh * vec[0:1, :] + vec[1:2, :]).astype(BF16)
    lnm = (xh * vec[2:3, :] + vec[3:4, :]).astype(BF16)
    lna_o[...] = lna
    lnm_o[...] = lnm
    qkv = mm(lna, wqkv[...]) + bqkv[0:1, :]
    v_o[...] = qkv[:, 2 * w :].astype(BF16)
    for cols, wfc, bfc in ((slice(0, hh), wfc_a, bfc_a), (slice(hh, 2 * hh), wfc_b, bfc_b)):
        act, slope = gelu_pair(mm(lnm, wfc[...]) + bfc[...])
        act_o[:, cols] = act.astype(BF16)
        gp_o[:, cols] = slope.astype(BF16)

    head_of_lane, diag, causal = masks(w, hd)
    low_half = lax.broadcasted_iota(jnp.int32, (UNIT, w), 1) % hd < ROT // 2
    row_id = lax.broadcasted_iota(jnp.int32, (UNIT, 1), 0)
    ones_bd = jnp.where(diag, 1.0, 0.0).astype(BF16)
    head_ones = head_stack(jnp.ones((UNIT, w), BF16), head_of_lane, heads)
    cf_hi, cf_lo = cf[0], cf[1]
    for i in range(per):
        pos, real, _ = chunk_place(units, pads, step * per + i, nseq)
        at = pl.ds(pl.multiple_of(pos * UNIT, UNIT), UNIT)
        cosines = lanes(cos_t[at, :], w)
        sines = lanes(sin_t[at, :], w)
        rows = slice(i * UNIT, (i + 1) * UNIT)
        rq = turn(qkv[rows, 0:w], cosines, sines, low_half)
        rk = turn(qkv[rows, w : 2 * w], cosines, sines, low_half)
        qh, ql = split(rq)
        kh, kl = split(rk)
        rq_o[rows, :] = qh
        rk_o[rows, :] = kh
        fq = jnp.exp(mm(qh, cf_hi) + mm(ql, cf_hi) + mm(qh, cf_lo)).astype(BF16)
        ek = jnp.exp(mm(kh, cf_hi) + mm(kl, cf_hi) + mm(kh, cf_lo))
        fk = jnp.where(row_id < real, ek, 0.0).astype(BF16)
        fq_o[rows, :] = fq
        fk_o[rows, :] = fk
        v = v_o[rows, :]
        keep = jnp.where(pos == 0, 0.0, 1.0)
        s_old = state[...] * keep
        k_old = ksum[...] * keep
        s_hi, s_lo = split(s_old)
        s_o[i, 0] = s_hi
        s_o[i, 1] = s_lo
        ks_o[i] = k_old
        scores = jnp.where(causal, mm(head_stack(fq, head_of_lane, heads), fk, NT), 0.0).astype(BF16)
        wide = side_by_side(scores, heads)
        num = mm(wide, head_stack(v, head_of_lane, heads)) + mm(fq, s_hi) + mm(fq, s_lo)
        p_hi, p_lo = split(fq.astype(F32) * k_old)
        den = mm(wide, head_ones) + mm(p_hi, ones_bd) + mm(p_lo, ones_bd)
        rden = 1.0 / den
        o = num * rden
        o_o[rows, :] = o
        rd_o[rows, :] = rden
        ao_o[rows, :] = o.astype(BF16)
        state[...] = s_old + jnp.where(diag, mm(fk, v, TN), 0.0)
        ksum[...] = k_old + jnp.sum(fk.astype(F32), axis=0, keepdims=True)

    out = mm(ao_o[...], wd[...]) + mm(act_o[:, :hh], wp_a[...]) + mm(act_o[:, hh:], wp_b[...])
    put(outs, slot, out.astype(BF16))


def forward_call(meta, units, pads, xs, vec, wqkv, bqkv, wfc, bfc, cf, cos_t, sin_t, wd, wp, hd, parts, rows):
    width, cols = wqkv.shape
    w, hid = cols // 3, wfc.shape[1]
    hh = hid // 2
    rb = rows // parts
    per, n = rb // UNIT, rows // UNIT
    core = meta.shape[0] - 1
    smem = pl.BlockSpec(memory_space=pltpu.SMEM)
    sds = jax.ShapeDtypeStruct

    def at(i, m):
        return (m[i], 0)

    def half(shape, index):
        return pl.BlockSpec(shape, index, pipeline_mode=pl.Buffered(1))

    out_specs, out_shape = put_specs(len(xs) > 1, rb, width, rows, at)
    saved = [(width, BF16)] * 2 + [(hid, BF16)] * 2 + [(w, BF16)] * 6 + [(w, F32)] * 2
    return pl.pallas_call(
        partial(forward_kernel, hd, len(xs), units.shape[1]),
        grid_spec=pltpu.PrefetchScalarGridSpec(
            num_scalar_prefetch=1,
            grid=(parts,),
            in_specs=[smem, smem]
            + rows_specs(xs, rb, at)
            + [
                const(vec.shape),
                const(wqkv.shape),
                const(bqkv.shape),
                half((width, hh), lambda i, m: (0, m[core])),
                half((width, hh), lambda i, m: (0, 1 - m[core])),
                half((1, hh), lambda i, m: (0, m[core])),
                half((1, hh), lambda i, m: (0, 1 - m[core])),
                const(cf.shape),
                const(cos_t.shape),
                const(sin_t.shape),
                const(wd.shape),
                half((hh, width), lambda i, m: (m[core], 0)),
                half((hh, width), lambda i, m: (1 - m[core], 0)),
            ],
            out_specs=[pl.BlockSpec((rb, k), at) for k, _ in saved]
            + [
                pl.BlockSpec((per, 2, w, w), lambda i, m: (m[i], 0, 0, 0)),
                pl.BlockSpec((per, 1, w), lambda i, m: (m[i], 0, 0)),
            ]
            + out_specs,
            scratch_shapes=[pltpu.VMEM((rb, width), BF16), pltpu.VMEM((w, w), F32), pltpu.VMEM((1, w), F32)],
        ),
        out_shape=[sds((rows, k), t) for k, t in saved] + [sds((n, 2, w, w), BF16), sds((n, 1, w), F32)] + out_shape,
        compiler_params=params(),
        cost_estimate=SMALL_COST,
        name="forward",
    )(meta, units, pads, *xs, vec, wqkv, bqkv, wfc, wfc, bfc, bfc, cf, cos_t, sin_t, wd, wp, wp)


def grad_kernel(meta, g_ref, gp, wd, wp_a, wp_b, *refs):
    dao_o, dh_o, sum_o, g_sum_o = refs[-4:]

    @pl.when(pl.program_id(0) == 0)
    def _():
        sum_o[...] = jnp.zeros_like(sum_o)
        g_sum_o[...] = jnp.zeros_like(g_sum_o)

    hh = wp_a.shape[0]
    g = g_ref[...]
    g_sum_o[...] += jnp.sum(g.astype(F32), axis=0, keepdims=True)
    dao_o[...] = mm(g, wd[...], NT).astype(BF16)
    for cols, wp in ((slice(0, hh), wp_a), (slice(hh, 2 * hh), wp_b)):
        dh = (mm(g, wp[...], NT) * gp[:, cols].astype(F32)).astype(BF16)
        dh_o[:, cols] = dh
        sum_o[:, cols] += jnp.sum(dh.astype(F32), axis=0, keepdims=True)


def grad_call(meta, parts, g, gp, wd, wp, deps=()):
    rows, hid = gp.shape
    w, width = wd.shape
    rb = rows // parts
    core = meta.shape[0] - 1
    sds = jax.ShapeDtypeStruct

    def plain(n):
        return pl.BlockSpec((rb, n), lambda i, m: (i, 0))

    return pl.pallas_call(
        grad_kernel,
        grid_spec=pltpu.PrefetchScalarGridSpec(
            num_scalar_prefetch=1,
            grid=(parts,),
            in_specs=[
                plain(width),
                plain(hid),
                const(wd.shape),
                pl.BlockSpec((hid // 2, width), lambda i, m: (m[core], 0), pipeline_mode=pl.Buffered(1)),
                pl.BlockSpec((hid // 2, width), lambda i, m: (1 - m[core], 0), pipeline_mode=pl.Buffered(1)),
            ]
            + unread(deps),
            out_specs=[plain(w), plain(hid), whole((1, hid)), whole((1, width))],
        ),
        out_shape=[sds((rows, w), BF16), sds((rows, hid), BF16), sds((1, hid), F32), sds((1, width), F32)],
        compiler_params=params(),
        cost_estimate=SMALL_COST,
        name="branch_grads",
    )(meta, g, gp, wd, wp, wp, *deps)


def attn_bwd_kernel(
    hd, nseq, meta, units, pads, dao, v_ref, o_ref, rd_ref, fq_ref, fk_ref, rq_ref, rk_ref, s_ref, ks_ref,
    cf, cos_t, sin_t, dct_bd, *refs,
):
    dqkv_o, sum_o, feat_o, after, after_sum, feat = refs[-6:]
    w = v_ref.shape[1]
    heads = w // hd
    step = pl.program_id(0)
    block = pl.num_programs(0) - 1 - step
    per = dao.shape[0] // UNIT

    @pl.when(step == 0)
    def _():
        for ref in (after, after_sum, feat, sum_o):
            ref[...] = jnp.zeros_like(ref)

    head_of_lane, diag, causal = masks(w, hd)
    low_half = lax.broadcasted_iota(jnp.int32, (UNIT, w), 1) % hd < ROT // 2
    ones_bd = jnp.where(diag, 1.0, 0.0).astype(BF16)
    back_hi, back_lo = cf[2], cf[3]
    for i in reversed(range(per)):
        pos, _, last = chunk_place(units, pads, block * per + i, nseq)
        rows = slice(i * UNIT, (i + 1) * UNIT)
        at = pl.ds(pl.multiple_of(pos * UNIT, UNIT), UNIT)
        cosines = lanes(cos_t[at, :], w)
        sines = -lanes(sin_t[at, :], w)
        keep = jnp.where(last == 1, 0.0, 1.0)
        a_old = after[...] * keep
        as_old = after_sum[...] * keep
        fq, fk, v = fq_ref[rows, :], fk_ref[rows, :], v_ref[rows, :]
        fqf, fkf = fq.astype(F32), fk.astype(F32)
        dn = (dao[rows, :].astype(F32) * rd_ref[rows, :]).astype(BF16)
        p_hi, p_lo = split(dn.astype(F32) * o_ref[rows, :])
        dden = -(mm(p_hi, ones_bd) + mm(p_lo, ones_bd))
        dn_s = head_stack(dn, head_of_lane, heads)
        fq_s = head_stack(fq, head_of_lane, heads)
        dden_s = jnp.concatenate(
            [jnp.broadcast_to(dden[:, h * hd : h * hd + 1], (UNIT, UNIT)) for h in range(heads)], axis=0
        )
        da = jnp.where(causal, mm(dn_s, v, NT) + dden_s, 0.0).astype(BF16)
        a = jnp.where(causal, mm(fq_s, fk, NT), 0.0).astype(BF16)
        s_hi, s_lo = s_ref[i, 0], s_ref[i, 1]
        dfq = (
            mm(side_by_side(da, heads), head_stack(fk, head_of_lane, heads))
            + mm(dn, s_hi, NT)
            + mm(dn, s_lo, NT)
            + dden * ks_ref[i]
        )
        a_hi, a_lo = split(a_old)
        dfk = mm(da, fq_s, TN) + mm(v, a_hi, NT) + mm(v, a_lo, NT) + as_old
        dv = mm(a, dn_s, TN) + mm(fk, a_hi)
        after[...] = a_old + jnp.where(diag, mm(fq, dn, TN), 0.0)
        after_sum[...] = as_old + jnp.sum(fqf * dden, axis=0, keepdims=True)
        dsq = (dfq * fqf).astype(BF16)
        dsk = (dfk * fkf).astype(BF16)
        feat[...] += mm(rq_ref[rows, :], dsq, TN) + mm(rk_ref[rows, :], dsk, TN)
        dq = turn(mm(dsq, back_hi) + mm(dsq, back_lo), cosines, sines, low_half)
        dk = turn(mm(dsk, back_hi) + mm(dsk, back_lo), cosines, sines, low_half)
        for j, part in enumerate((dq, dk, dv)):
            part = part.astype(BF16)
            dqkv_o[rows, j * w : (j + 1) * w] = part
            sum_o[:, j * w : (j + 1) * w] += jnp.sum(part.astype(F32), axis=0, keepdims=True)

    @pl.when(block == 0)
    def _():
        turned = lax.dot_general(
            dct_bd[...],
            jnp.where(diag, feat[...], 0.0),
            TN,
            precision=lax.Precision.HIGHEST,
            preferred_element_type=F32,
        )
        total = turned[0:hd, :]
        for h in range(1, heads):
            total = total + turned[h * hd : (h + 1) * hd, :]
        feat_o[...] = total


def attn_bwd_call(meta, units, pads, dao, v, o, rd, fq, fk, rq, rk, s, ks, cf, cos_t, sin_t, dct_bd, hd, parts, deps=()):
    rows, w = v.shape
    rb = rows // parts
    per = rb // UNIT
    smem = pl.BlockSpec(memory_space=pltpu.SMEM)
    sds = jax.ShapeDtypeStruct

    def at(i, m):
        return (m[parts - 1 - i], 0)

    return pl.pallas_call(
        partial(attn_bwd_kernel, hd, units.shape[1]),
        grid_spec=pltpu.PrefetchScalarGridSpec(
            num_scalar_prefetch=1,
            grid=(parts,),
            in_specs=[smem, smem]
            + [pl.BlockSpec((rb, w), at)] * 8
            + [
                pl.BlockSpec((per, 2, w, w), lambda i, m: (m[parts - 1 - i], 0, 0, 0)),
                pl.BlockSpec((per, 1, w), lambda i, m: (m[parts - 1 - i], 0, 0)),
                const(cf.shape),
                const(cos_t.shape),
                const(sin_t.shape),
                const(dct_bd.shape),
            ]
            + unread(deps),
            out_specs=[pl.BlockSpec((rb, 3 * w), at), whole((1, 3 * w)), whole((hd, w))],
            scratch_shapes=[pltpu.VMEM((w, w), F32), pltpu.VMEM((1, w), F32), pltpu.VMEM((w, w), F32)],
        ),
        out_shape=[sds((rows, 3 * w), BF16), sds((1, 3 * w), F32), sds((hd, w), F32)],
        compiler_params=params(),
        cost_estimate=SMALL_COST,
        name="attn_bwd",
    )(meta, units, pads, dao, v, o, rd, fq, fk, rq, rk, s, ks, cf, cos_t, sin_t, dct_bd, *deps)


SMALL_ROWS = 32


def norms_kernel(shards, deps, meta, *refs):
    x_refs = refs[:shards]
    dqkv, dh, vec, wqkv, wfc_a, wfc_b, g_sum, hid_sum, qkv_sum, feat, *rest = refs[shards:]
    small_o, *outs, xbuf = rest[deps:]
    step = pl.program_id(0)
    hh = wfc_a.shape[1]
    slot = step

    @pl.when(step == 0)
    def _():
        small_o[...] = jnp.zeros_like(small_o)
        hid_row = hid_sum[...]
        swapped = jnp.concatenate([hid_row[:, hh:], hid_row[:, :hh]], axis=1)
        hid_row = jnp.where(meta[meta.shape[0] - 1] == 1, swapped, hid_row)
        for at, row in ((4, g_sum[...]), (5, hid_row), (6, qkv_sum[...])):
            small_o[at : at + 1, 0 : row.shape[1]] = row
        deep, w = feat.shape
        each = deep * w // small_o.shape[1]
        for j in range(deep // each):
            small_o[8 : 8 + each, j * w : (j + 1) * w] = feat[j * each : (j + 1) * each, :]

    xh, _ = norm_rows(pick_rows(x_refs, slot, xbuf).astype(F32))
    da = mm(dqkv[...], wqkv[...], NT)
    small_o[0:1, :] += jnp.sum(da * xh, axis=0, keepdims=True)
    small_o[1:2, :] += jnp.sum(da, axis=0, keepdims=True)
    dm = mm(dh[:, :hh], wfc_a[...], NT) + mm(dh[:, hh:], wfc_b[...], NT)
    small_o[2:3, :] += jnp.sum(dm * xh, axis=0, keepdims=True)
    small_o[3:4, :] += jnp.sum(dm, axis=0, keepdims=True)
    put(outs, slot, (da * vec[0:1, :] + dm * vec[2:3, :]).astype(BF16))


def norms_call(meta, parts, xs, dqkv, dh, vec, wqkv, wfc, g_sum, hid_sum, qkv_sum, feat, deps=()):
    rows, hid = dh.shape
    width, cols = wqkv.shape
    hh = hid // 2
    rb = rows // parts
    core = meta.shape[0] - 1

    def at(i, m):
        return (i, 0)

    def to(i, m):
        return (m[i], 0)

    def half(shape, index):
        return pl.BlockSpec(shape, index, pipeline_mode=pl.Buffered(1))

    out_specs, out_shape = put_specs(len(xs) > 1, rb, width, rows, at)
    small = (SMALL_ROWS, width)
    return pl.pallas_call(
        partial(norms_kernel, len(xs), len(deps)),
        grid_spec=pltpu.PrefetchScalarGridSpec(
            num_scalar_prefetch=1,
            grid=(parts,),
            in_specs=rows_specs(xs, rb, at)
            + [
                pl.BlockSpec((rb, cols), at),
                pl.BlockSpec((rb, hid), at),
                const(vec.shape),
                const(wqkv.shape),
                half((width, hh), lambda i, m: (0, m[core])),
                half((width, hh), lambda i, m: (0, 1 - m[core])),
                const(g_sum.shape),
                const(hid_sum.shape),
                const(qkv_sum.shape),
                const(feat.shape),
            ]
            + unread(deps),
            out_specs=[whole(small)] + out_specs,
            scratch_shapes=[pltpu.VMEM((rb, width), BF16)],
        ),
        out_shape=[jax.ShapeDtypeStruct(small, F32)] + out_shape,
        compiler_params=params(),
        cost_estimate=SMALL_COST,
        name="norm_grads",
    )(meta, *xs, dqkv, dh, vec, wqkv, wfc, wfc, g_sum, hid_sum, qkv_sum, feat, *deps)


class Order:
    def __init__(self):
        self.last = None

    def after(self, *arrays):
        if self.last is None:
            return arrays if len(arrays) > 1 else arrays[0]
        self.last, *arrays = lax.optimization_barrier((self.last, *arrays))
        return tuple(arrays) if len(arrays) > 1 else arrays[0]

    def did(self, array):
        self.last = array
        return array


def both(a, b):
    return (a.astype(F32) + b.astype(F32)).astype(a.dtype)


def totals_kernel(count, mid, *refs):
    total = refs[-1]
    rows = refs[0].shape[0]
    for k in range(count):
        own, sent = refs[2 * k], refs[2 * k + 1]

        @pl.when(mid[0] == 1)
        def _():
            total[k * rows : (k + 1) * rows, :] = own[...]

        @pl.when(mid[0] == 0)
        def _():
            total[k * rows : (k + 1) * rows, :] = sent[...]


def totals_call(mid, pairs, deps):
    rows, cols = pairs[0].shape
    count = len(pairs) // 2
    return pl.pallas_call(
        partial(totals_kernel, count),
        in_specs=[pl.BlockSpec(memory_space=pltpu.SMEM)] + [whole((rows, cols))] * len(pairs) + unread(deps),
        out_specs=whole((count * rows, cols)),
        out_shape=jax.ShapeDtypeStruct((count * rows, cols), BF16),
        compiler_params=pltpu.CompilerParams(vmem_limit_bytes=VMEM_BYTES),
        cost_estimate=SMALL_COST,
        name="totals",
    )(mid.astype(jnp.int32).reshape(1), *pairs, *deps)


class Line:
    swap = [(i, i ^ 1) for i in range(8)]
    inward = [(0, 2), (1, 3), (6, 4), (7, 5)]
    inner = [(2, 4), (4, 2), (3, 5), (5, 3)]
    outward = [(2, 0), (3, 1), (4, 6), (5, 7)]

    def __init__(self, order):
        index = lax.axis_index("batch")
        self.order = order
        self.core, z = index % 2, index // 2
        self.mid = (z == 1) | (z == 2)
        self.own, self.sent = {}, {}

    def start(self, k, own, other):
        self.own[k], self.sent[k] = own, lax.ppermute(other, "batch", self.swap)

    def add(self, k, to):
        own, sent = self.order.after(self.own[k], self.sent[k])
        self.own[k] = self.order.did(both(own, sent))
        self.sent[k] = lax.ppermute(self.own[k], "batch", to)

    def go_in(self, k):
        self.add(k, self.inward)

    def meet(self, k):
        self.add(k, self.inner)

    def go_out(self, k):
        self.add(k, self.outward)

    def held(self, *ks):
        return tuple(self.own[k] for k in ks)

    def arrived(self, *ks):
        return tuple(self.sent[k] for k in ks)

    def landed(self, *ks):
        for k in ks:
            self.own[k], self.sent[k] = self.order.after(self.own[k], self.sent[k])

    def end(self, *ks, deps=()):
        self.landed(*ks)
        if deps:
            total = totals_call(self.mid, [a for k in ks for a in (self.own[k], self.sent[k])], deps)
        else:
            total = jnp.concatenate([jnp.where(self.mid, self.own[k], self.sent[k]) for k in ks])
        total = self.order.did(total)
        return total, lax.ppermute(total, "batch", self.swap)

    def end_small(self, k):
        self.landed(k)
        return jnp.where(self.mid, self.own[k], self.sent[k])


def across(a, mask):
    return lax.ppermute(a, "tensor", [(i, i ^ mask) for i in range(4)])


def part_of_batch(a):
    return lax.psum_scatter(a, "batch", scatter_dimension=0, tiled=True)


class TwoStepSum:
    def __init__(self, order, blocks):
        self.order = order
        self.keep_a, send_a, self.keep_b, send_b = blocks
        self.got_a, self.got_b = across(send_a, 1), across(send_b, 2)

    def second(self):
        rb = self.keep_a.shape[0] // 2
        self.got_a, self.got_b = self.order.after(self.got_a, self.got_b)
        a = both(self.keep_a[rb:], self.got_a[rb:])
        b = both(self.keep_b[rb:], self.got_b[rb:])
        a, b = lax.optimization_barrier((a, b))
        self.order.did(b)
        self.last_a, self.last_b = across(a, 2), across(b, 1)

    def result(self):
        rb = self.keep_a.shape[0] // 2
        terms = ((self.keep_a, self.got_a, self.last_a), (self.keep_b, self.got_b, self.last_b))
        return jnp.concatenate([sum(t[:rb].astype(F32) for t in side) for side in terms], axis=1)


def cosine_blocks(hd, heads):
    spatial = np.arange(hd, dtype=np.float64)[:, None]
    frequency = np.arange(hd, dtype=np.float64)[None, :]
    table = np.cos(math.pi * (2.0 * spatial + 1.0) * frequency / (2.0 * hd)) * math.sqrt(2.0 / hd)
    table[:, 0] *= math.sqrt(0.5)
    return np.kron(np.eye(heads), table).astype(np.float32)


def turn_tables(rows, hd):
    half = ROT // 2
    inverse_freq = np.exp(-math.log(10000.0) * 2.0 * np.arange(half) / ROT)
    angles = np.arange(rows)[:, None] * inverse_freq[None, :]
    cosines, sines = np.cos(angles), np.sin(angles)
    rest = np.ones((rows, hd - ROT))
    reps = (1, 128 // hd)
    return (
        np.tile(np.concatenate([cosines, cosines, rest], axis=1), reps).astype(np.float32),
        np.tile(np.concatenate([-sines, sines, 0.0 * rest], axis=1), reps).astype(np.float32),
    )


def column_pick(heads, hd):
    n = 3 * heads * hd
    source = np.arange(n).reshape(heads, 3, hd).transpose(1, 0, 2).reshape(-1)
    pick = np.zeros((n, n), np.float32)
    pick[source, np.arange(n)] = 1.0
    return pick


def body(
    tokens,
    output_grad,
    attn_norm_gain,
    attn_norm_bias,
    mlp_norm_gain,
    mlp_norm_bias,
    qkv_weight,
    qkv_bias,
    dense_weight,
    dense_bias,
    fc_weight,
    fc_bias,
    proj_weight,
    feature_weight,
    seq_units,
    pad_tokens,
):
    rows_dev, width = tokens.shape
    parts = lax.axis_size("tensor")
    n_batch = lax.axis_size("batch")
    rows = rows_dev * parts
    heads, hd, _ = feature_weight.shape
    w = heads * hd
    hid = fc_weight.shape[1]

    square = parts == 4 and n_batch == 8 and hid == width and 4 * w == width
    position = lax.axis_index("tensor")
    order = Order()
    line = Line(order) if square else None
    slots = jnp.arange(parts, dtype=jnp.int32)
    core = jnp.int32(0)
    if square:
        slots = slots ^ position
        core = line.core
        mid = rows_dev // 2
        a1, a2 = across(tokens, 1), across(tokens, 2)
    tail = jnp.stack([jnp.int32(rows_dev // UNIT), core.astype(jnp.int32)])
    meta = jnp.concatenate([slots, tail])
    vec = jnp.stack([attn_norm_gain, attn_norm_bias, mlp_norm_gain, mlp_norm_bias]).astype(F32)
    dct_bd = jnp.asarray(cosine_blocks(hd, heads))
    cos_t, sin_t = (jnp.asarray(t) for t in turn_tables(rows, hd))
    pick = jnp.asarray(column_pick(heads, hd)).astype(BF16)
    bfc = fc_bias.astype(F32).reshape(1, hid)
    wqkv, bqkv, cf_pair = prep_call(
        qkv_weight, qkv_bias.reshape(1, 3 * w), feature_weight.reshape(w, hd), pick, dct_bd, hd, (meta, vec, bfc)
    )
    hh = hid // 2
    dm = width // 2
    g_float = output_grad.astype(F32)
    x_own = tokens.astype(F32)
    if square:
        order.did(wqkv)
        a1, a2 = order.after(a1, a2)
        b1, b2 = across(a1[:mid], 2), across(a2[mid:], 1)
        b1, b2 = order.after(b1, b2)
        g_own, b1, b2 = lax.optimization_barrier((output_grad, b1, b2))
        c1, c2, c3 = across(g_own, 1), across(g_own, 2), across(g_own, 3)
        xs = [tokens, a1, a2, b1, b2]
    else:
        xs = [lax.all_gather(tokens, "tensor", axis=0, tiled=True)]
        g_all = lax.all_gather(output_grad, "tensor", axis=0, tiled=True)
    lna, lnm, act, gp, fq, fk, rq, rk, v, ao, o, rd, s, ks, *outs = forward_call(
        meta, seq_units, pad_tokens, xs, vec, wqkv, bqkv, fc_weight, bfc, cf_pair, cos_t, sin_t,
        dense_weight, proj_weight, hd, parts, rows,
    )
    order.did(ao)
    def residual(total):
        return (x_own + total + dense_bias.astype(F32)).astype(BF16)

    def proj_piece(k, cols):
        g = order.after(g_all)[:, cols]
        line.start(k, mm(act[:, :hh], g, TN).astype(BF16), order.did(mm(act[:, hh:], g, TN).astype(BF16)))

    def fc_piece(k, cols):
        part = order.after(lnm)[:, cols]
        line.start(k, mm(part, dh[:, :hh], TN).astype(BF16), order.did(mm(part, dh[:, hh:], TN).astype(BF16)))

    def rest_piece(k, cols):
        part, cotangent = order.after(lna, dqkv)
        stack = jnp.concatenate([mm(ao, g_all[:, cols], TN), mm(cotangent, part[:, cols], TN)])
        stack = stack.astype(BF16).reshape(2, 2 * w, dm)
        own = lax.dynamic_index_in_dim(stack, line.core, 0, keepdims=False)
        other = lax.dynamic_index_in_dim(stack, 1 - line.core, 0, keepdims=False)
        order.did(other)
        line.start(k, own, other)

    left, right = slice(0, dm), slice(dm, width)
    if square:
        branch = TwoStepSum(order, outs)
        c1, c2, c3 = order.after(c1, c2, c3)
        g_all = order.did(jnp.concatenate([output_grad, c1, c2, c3]))
        proj_piece(0, left)
        proj_piece(1, right)
        line.go_in(0)
        line.go_in(1)
        g_all = order.after(g_all)
    dao, dh, hid_sum, g_sum = grad_call(meta, parts, g_all, gp, dense_weight, proj_weight, line.held(0, 1) if square else ())
    order.did(dao)
    if square:
        branch.second()
        line.meet(0)
        fc_piece(2, left)
        line.go_in(2)
        fc_piece(3, right)
        line.meet(1)
        branch.last_a, branch.last_b = order.after(branch.last_a, branch.last_b)
        output = order.did(residual(branch.result()))
        line.go_out(0)
        line.go_in(3)
    dao = order.after(dao)
    dqkv, qkv_sum, feat = attn_bwd_call(
        meta, seq_units, pad_tokens, dao, v, o, rd, fq, fk, rq, rk, s, ks, cf_pair, cos_t, sin_t, dct_bd, hd, parts,
        (*line.held(0, 1, 2, 3), output) if square else (),
    )
    order.did(dqkv)
    if square:
        line.meet(2)
        line.go_out(1)
        rest_piece(4, left)
        line.landed(0)
        line.meet(3)
        line.go_in(4)
        rest_piece(5, right)
        line.go_in(5)
        line.landed(1)
        line.go_out(2)
    dqkv = order.after(dqkv)
    small, *es = norms_call(meta, parts, xs, dqkv, dh, vec, wqkv, fc_weight, g_sum, hid_sum, qkv_sum, feat,
        (*line.held(2, 3, 4, 5), *line.arrived(0, 1)) if square else ())
    order.did(small)

    def rows_grad(e):
        x_hat, inv_std = norm_rows(x_own)
        mean = jnp.mean(e, axis=-1, keepdims=True)
        return (g_float + inv_std * (e - mean - x_hat * jnp.mean(e * x_hat, axis=-1, keepdims=True))).astype(BF16)

    if square:
        line.meet(4)
        line.go_out(3)
        line.landed(2)
        small = order.after(small)
        line.start(6, small, small)
        es[1], es[3] = order.after(es[1], es[3])
        e_sum = TwoStepSum(order, es)
        line.go_in(6)
        line.meet(5)
        line.landed(3)
        first = line.end(0, 1, 2, 3)
        line.meet(6)
        line.go_out(4)
        second = line.core == 1

        def pieces_of(pair, count):
            own, twin = order.after(*pair)
            low = jnp.where(second, twin, own).reshape(count, 2 * w, dm)
            high = jnp.where(second, own, twin).reshape(count, 2 * w, dm)
            return low, high

        low, high = pieces_of(first, 4)
        proj_grad = order.did(
            jnp.concatenate(
                [jnp.concatenate([low[k], high[k]], axis=0) for k in (0, 1)], axis=1
            ).astype(F32)
        )
        e_sum.second()
        line.go_out(6)
        fc_grad = order.did(
            jnp.concatenate([jnp.concatenate([low[k], high[k]], axis=1) for k in (2, 3)], axis=0).astype(F32)
        )
        line.go_out(5)
        small = order.did(line.end_small(6))
        norm_sums = small[:8]
        hop = across(norm_sums, 1)
        e_sum.last_a, e_sum.last_b = order.after(e_sum.last_a, e_sum.last_b)
        tokens_grad = order.did(rows_grad(e_sum.result()))
        norm_sums = order.did(norm_sums + order.after(hop))
        hop = across(norm_sums, 2)
        last = line.end(4, 5, deps=(proj_grad, fc_grad, tokens_grad, norm_sums))
        norm_sums = norm_sums + order.after(hop)
        low, high = pieces_of(last, 2)
        rest = jnp.concatenate([jnp.concatenate([low[k], high[k]], axis=0) for k in (0, 1)], axis=1)
        dense_grad, qkv_grad = rest[:w].astype(F32), rest[w:]
        hid_sum = small[5]
        pick = jnp.asarray(column_pick(heads, hd)).astype(BF16)
        qkv_grad = lax.dot_general(qkv_grad.astype(BF16), pick, (((0,), (1,)), ((), ())), preferred_element_type=F32)
    else:
        output = residual(lax.psum_scatter(outs[0], "tensor", scatter_dimension=0, tiled=True).astype(F32))
        tokens_grad = rows_grad(lax.psum_scatter(es[0], "tensor", scatter_dimension=0, tiled=True).astype(F32))
        sums = [mm(act, g_all, TN), mm(lnm, dh, TN), mm(ao, g_all, TN), mm(dqkv, lna, TN)]
        sums = lax.psum([a.astype(BF16) for a in sums], "batch")
        proj_grad, fc_grad, dense_grad, qkv_grad = (a.astype(F32) for a in sums)
        small = lax.psum(small, "batch")
        norm_sums = lax.psum(small[:4], "tensor")
        hid_sum = small[5, :hid]
        qkv_grad = qkv_grad.reshape(3, heads, hd, width).transpose(3, 1, 0, 2).reshape(width, 3 * w)
    each = hd * w // width
    feature_grad = small[8 : 8 + each].reshape(each, width // w, heads, hd).transpose(2, 1, 0, 3).reshape(heads, hd, hd)
    qkv_bias_grad = small[6, : 3 * w].reshape(3, heads, hd).transpose(1, 0, 2).reshape(3 * w)

    return (
        output,
        tokens_grad,
        norm_sums[0],
        norm_sums[1],
        norm_sums[2],
        norm_sums[3],
        qkv_grad,
        qkv_bias_grad,
        dense_grad,
        small[4],
        fc_grad,
        hid_sum,
        proj_grad,
        feature_grad,
    )


def solution(mesh):
    rows = P(("batch", "tensor"), None)
    placed = (
        rows,
        rows,
        P(),
        P(),
        P(),
        P(),
        P(None, "tensor"),
        P("tensor"),
        P("tensor", None),
        P(),
        P(None, "tensor"),
        P("tensor"),
        P("tensor", None),
        P("tensor", None, None),
        P("batch", None),
        P("batch", None),
    )
    return jax.shard_map(
        body,
        mesh=mesh,
        in_specs=placed,
        out_specs=(
            rows,
            rows,
            P(),
            P(),
            P(),
            P(),
            P(None, "tensor"),
            P("tensor"),
            P("tensor", None),
            P(),
            P(None, "tensor"),
            P("tensor"),
            P("tensor", None),
            P("tensor", None, None),
        ),
        check_vma=False,
    )
```

```python
from functools import partial
import math

import jax
import jax.numpy as jnp
import numpy as np
from jax import lax
from jax.experimental import pallas as pl
from jax.experimental.pallas import tpu as pltpu
from jax.sharding import PartitionSpec as P

ROT = 16
UNIT = 128
EPS = 1e-05
F32 = jnp.float32
BF16 = jnp.bfloat16
VMEM_BYTES = 54 * 1024 * 1024

NN = (((1,), (0,)), ((), ()))
NT = (((1,), (1,)), ((), ()))
TN = (((0,), (0,)), ((), ()))


def mm(a, b, dims=NN):
    return lax.dot_general(a, b, dims, preferred_element_type=F32)


def split(a):
    hi = a.astype(BF16)
    return hi, (a - hi.astype(F32)).astype(BF16)


HELD_SPACE = pl.ANY
SMALL_COST = pl.CostEstimate(flops=1000, bytes_accessed=1000, transcendentals=0)


def params(grid_rank=1):
    return pltpu.CompilerParams(
        dimension_semantics=("arbitrary",) * grid_rank, vmem_limit_bytes=VMEM_BYTES
    )


def whole(shape):
    return pl.BlockSpec(shape, lambda *_: (0,) * len(shape))


def rows_of(block, width):
    return pl.BlockSpec((block, width), lambda i: (i, 0))


def norm_rows(x):
    mean = jnp.mean(x, axis=-1, keepdims=True)
    cent = x - mean
    inv = lax.rsqrt(jnp.mean(cent * cent, axis=-1, keepdims=True) + EPS)
    return cent * inv, inv


def chunk_place(units, pads, chunk, nseq):
    start = jnp.int32(0)
    pos, real, last = jnp.int32(0), jnp.int32(0), jnp.int32(0)
    for n in range(nseq):
        u = units[0, n]
        inside = (chunk >= start) & (chunk < start + u)
        pos = jnp.where(inside, chunk - start, pos)
        real = jnp.where(inside, (start + u - chunk) * UNIT - pads[0, n], real)
        last = jnp.where(inside, (chunk == start + u - 1).astype(jnp.int32), last)
        start = start + u
    return pos, real, last


def lanes(table, w):
    return jnp.concatenate([table] * (w // table.shape[1]), axis=1) if w > table.shape[1] else table


def turn(a, cosines, sines, low_half):
    w = a.shape[1]
    other = jnp.where(low_half, pltpu.roll(a, w - ROT // 2, 1), pltpu.roll(a, ROT // 2, 1))
    return a * cosines + other * sines


def head_stack(a, head_of_lane, heads):
    zero = jnp.zeros_like(a)
    return jnp.concatenate([jnp.where(head_of_lane == h, a, zero) for h in range(heads)], axis=0)


def side_by_side(a, heads):
    return jnp.concatenate([a[h * UNIT : (h + 1) * UNIT, :] for h in range(heads)], axis=1)


def masks(w, hd):
    lane = lax.broadcasted_iota(jnp.int32, (UNIT, w), 1)
    head_of_lane = lane // hd
    bi = lax.broadcasted_iota(jnp.int32, (w, w), 0) // hd
    bj = lax.broadcasted_iota(jnp.int32, (w, w), 1) // hd
    heads = w // hd
    row = lax.broadcasted_iota(jnp.int32, (heads * UNIT, UNIT), 0) % UNIT
    col = lax.broadcasted_iota(jnp.int32, (heads * UNIT, UNIT), 1)
    return head_of_lane, bi == bj, row >= col


def prep_kernel(hd, wqkv, bqkv, feat, pick, dct_bd, *refs):
    wqkv_o, bqkv_o, cf_o = refs[-3:]
    w = dct_bd.shape[0]
    wqkv_o[...] = mm(wqkv[...], pick[...]).astype(BF16)
    bqkv_o[...] = mm(jnp.broadcast_to(bqkv[...], (8, 3 * w)), pick[...])
    diag = lax.broadcasted_iota(jnp.int32, (w, w), 0) // hd == lax.broadcasted_iota(jnp.int32, (w, w), 1) // hd
    spread = jnp.where(diag, jnp.concatenate([feat[...].astype(F32)] * (w // hd), axis=1), 0.0)
    cf_hi, cf_lo = split(
        lax.dot_general(dct_bd[...], spread, NN, precision=lax.Precision.HIGHEST, preferred_element_type=F32)
    )
    cf_o[0] = cf_hi
    cf_o[1] = cf_lo
    back_hi, back_lo = split(
        lax.dot_general(spread, dct_bd[...], (((0,), (1,)), ((), ())), precision=lax.Precision.HIGHEST, preferred_element_type=F32)
    )
    cf_o[2] = back_hi
    cf_o[3] = back_lo


def prep_call(wqkv, bqkv, feat, pick, dct_bd, hd, deps=()):
    width, cols = wqkv.shape
    w = cols // 3
    sds = jax.ShapeDtypeStruct
    return pl.pallas_call(
        partial(prep_kernel, hd),
        in_specs=[whole(a.shape) for a in (wqkv, bqkv, feat, pick, dct_bd)] + unread(deps),
        out_shape=[sds((width, cols), BF16), sds((8, cols), F32), sds((4, w, w), BF16)],
        compiler_params=pltpu.CompilerParams(vmem_limit_bytes=VMEM_BYTES),
        cost_estimate=SMALL_COST,
        name="prepare",
    )(wqkv, bqkv, feat, pick, dct_bd, *deps)


def gelu_pair(h):
    bell = jnp.exp(h * h * -0.5)
    cdf = 0.5 + 0.5 * lax.erf(h * math.sqrt(0.5))
    return h * cdf, cdf + (h * bell) * (1.0 / math.sqrt(2.0 * math.pi))


def pick_rows(refs, slot, into):
    if len(refs) == 1:
        return refs[0][...]
    rb = into.shape[0]
    for j, ref in enumerate(refs):
        at = slice(0, rb) if j < 3 else slice(0, rb // 2) if j == 3 else slice(rb // 2, rb)

        @pl.when(slot == min(j, 3))
        def _():
            into[at, :] = ref[...]

    return into[...]


def rows_specs(arrays, rb, at):
    if len(arrays) == 1:
        return [pl.BlockSpec((rb, arrays[0].shape[1]), at)]
    return [const(a.shape) for a in arrays]


def put(outs, slot, value):
    if len(outs) == 1:
        outs[0][...] = value
        return
    rb, half = value.shape[0], value.shape[1] // 2
    keep_a, send_a, keep_b, send_b = outs
    for j, (a, b) in enumerate(((keep_a, keep_b), (send_a, keep_b), (keep_a, send_b), (send_a, send_b))):

        @pl.when(slot == j)
        def _():
            a[(j // 2) * rb : (j // 2 + 1) * rb, :] = value[:, :half]
            b[(j % 2) * rb : (j % 2 + 1) * rb, :] = value[:, half:]


def put_specs(apart, rb, width, total, at):
    if apart:
        shape = (2 * rb, width // 2)
        return [whole(shape)] * 4, [jax.ShapeDtypeStruct(shape, BF16)] * 4
    return [pl.BlockSpec((rb, width), at)], [jax.ShapeDtypeStruct((total, width), BF16)]


def unread(arrays):
    return [pl.BlockSpec(memory_space=pl.ANY)] * len(arrays)


def const(shape):
    return pl.BlockSpec(shape, lambda *_: (0,) * len(shape), pipeline_mode=pl.Buffered(1))


def forward_kernel(hd, shards, nseq, meta, units, pads, *refs):
    x_refs = refs[:shards]
    vec, wqkv, bqkv, wfc_a, wfc_b, bfc_a, bfc_b, cf, cos_t, sin_t, wd, wp_a, wp_b = refs[shards : shards + 13]
    lna_o, lnm_o, act_o, gp_o, fq_o, fk_o, rq_o, rk_o, v_o, ao_o, o_o, rd_o, s_o, ks_o = refs[shards + 13 : shards + 27]
    *outs, xbuf, state, ksum = refs[shards + 27 :]
    step = pl.program_id(0)
    slot = meta[step]
    w, hh, per = v_o.shape[1], bfc_a.shape[1], xbuf.shape[0] // UNIT
    heads = w // hd

    @pl.when(step == 0)
    def _():
        state[...] = jnp.zeros_like(state)
        ksum[...] = jnp.zeros_like(ksum)

    xh, _ = norm_rows(pick_rows(x_refs, slot, xbuf).astype(F32))
    lna = (xh * vec[0:1, :] + vec[1:2, :]).astype(BF16)
    lnm = (xh * vec[2:3, :] + vec[3:4, :]).astype(BF16)
    lna_o[...] = lna
    lnm_o[...] = lnm
    qkv = mm(lna, wqkv[...]) + bqkv[0:1, :]
    v_o[...] = qkv[:, 2 * w :].astype(BF16)
    for cols, wfc, bfc in ((slice(0, hh), wfc_a, bfc_a), (slice(hh, 2 * hh), wfc_b, bfc_b)):
        act, slope = gelu_pair(mm(lnm, wfc[...]) + bfc[...])
        act_o[:, cols] = act.astype(BF16)
        gp_o[:, cols] = slope.astype(BF16)

    head_of_lane, diag, causal = masks(w, hd)
    low_half = lax.broadcasted_iota(jnp.int32, (UNIT, w), 1) % hd < ROT // 2
    row_id = lax.broadcasted_iota(jnp.int32, (UNIT, 1), 0)
    ones_bd = jnp.where(diag, 1.0, 0.0).astype(BF16)
    head_ones = head_stack(jnp.ones((UNIT, w), BF16), head_of_lane, heads)
    cf_hi, cf_lo = cf[0], cf[1]
    for i in range(per):
        pos, real, _ = chunk_place(units, pads, step * per + i, nseq)
        at = pl.ds(pl.multiple_of(pos * UNIT, UNIT), UNIT)
        cosines = lanes(cos_t[at, :], w)
        sines = lanes(sin_t[at, :], w)
        rows = slice(i * UNIT, (i + 1) * UNIT)
        rq = turn(qkv[rows, 0:w], cosines, sines, low_half)
        rk = turn(qkv[rows, w : 2 * w], cosines, sines, low_half)
        qh, ql = split(rq)
        kh, kl = split(rk)
        rq_o[rows, :] = qh
        rk_o[rows, :] = kh
        fq = jnp.exp(mm(qh, cf_hi) + mm(ql, cf_hi) + mm(qh, cf_lo)).astype(BF16)
        ek = jnp.exp(mm(kh, cf_hi) + mm(kl, cf_hi) + mm(kh, cf_lo))
        fk = jnp.where(row_id < real, ek, 0.0).astype(BF16)
        fq_o[rows, :] = fq
        fk_o[rows, :] = fk
        v = v_o[rows, :]
        keep = jnp.where(pos == 0, 0.0, 1.0)
        s_old = state[...] * keep
        k_old = ksum[...] * keep
        s_hi, s_lo = split(s_old)
        s_o[i, 0] = s_hi
        s_o[i, 1] = s_lo
        ks_o[i] = k_old
        scores = jnp.where(causal, mm(head_stack(fq, head_of_lane, heads), fk, NT), 0.0).astype(BF16)
        wide = side_by_side(scores, heads)
        num = mm(wide, head_stack(v, head_of_lane, heads)) + mm(fq, s_hi) + mm(fq, s_lo)
        p_hi, p_lo = split(fq.astype(F32) * k_old)
        den = mm(wide, head_ones) + mm(p_hi, ones_bd) + mm(p_lo, ones_bd)
        rden = 1.0 / den
        o = num * rden
        o_o[rows, :] = o
        rd_o[rows, :] = rden
        ao_o[rows, :] = o.astype(BF16)
        state[...] = s_old + jnp.where(diag, mm(fk, v, TN), 0.0)
        ksum[...] = k_old + jnp.sum(fk.astype(F32), axis=0, keepdims=True)

    out = mm(ao_o[...], wd[...]) + mm(act_o[:, :hh], wp_a[...]) + mm(act_o[:, hh:], wp_b[...])
    put(outs, slot, out.astype(BF16))


def forward_call(meta, units, pads, xs, vec, wqkv, bqkv, wfc, bfc, cf, cos_t, sin_t, wd, wp, hd, parts, rows):
    width, cols = wqkv.shape
    w, hid = cols // 3, wfc.shape[1]
    hh = hid // 2
    rb = rows // parts
    per, n = rb // UNIT, rows // UNIT
    core = meta.shape[0] - 1
    smem = pl.BlockSpec(memory_space=pltpu.SMEM)
    sds = jax.ShapeDtypeStruct

    def at(i, m):
        return (m[i], 0)

    def half(shape, index):
        return pl.BlockSpec(shape, index, pipeline_mode=pl.Buffered(1))

    out_specs, out_shape = put_specs(len(xs) > 1, rb, width, rows, at)
    saved = [(width, BF16)] * 2 + [(hid, BF16)] * 2 + [(w, BF16)] * 6 + [(w, F32)] * 2
    return pl.pallas_call(
        partial(forward_kernel, hd, len(xs), units.shape[1]),
        grid_spec=pltpu.PrefetchScalarGridSpec(
            num_scalar_prefetch=1,
            grid=(parts,),
            in_specs=[smem, smem]
            + rows_specs(xs, rb, at)
            + [
                const(vec.shape),
                const(wqkv.shape),
                const(bqkv.shape),
                half((width, hh), lambda i, m: (0, m[core])),
                half((width, hh), lambda i, m: (0, 1 - m[core])),
                half((1, hh), lambda i, m: (0, m[core])),
                half((1, hh), lambda i, m: (0, 1 - m[core])),
                const(cf.shape),
                const(cos_t.shape),
                const(sin_t.shape),
                const(wd.shape),
                half((hh, width), lambda i, m: (m[core], 0)),
                half((hh, width), lambda i, m: (1 - m[core], 0)),
            ],
            out_specs=[pl.BlockSpec((rb, k), at) for k, _ in saved]
            + [
                pl.BlockSpec((per, 2, w, w), lambda i, m: (m[i], 0, 0, 0)),
                pl.BlockSpec((per, 1, w), lambda i, m: (m[i], 0, 0)),
            ]
            + out_specs,
            scratch_shapes=[pltpu.VMEM((rb, width), BF16), pltpu.VMEM((w, w), F32), pltpu.VMEM((1, w), F32)],
        ),
        out_shape=[sds((rows, k), t) for k, t in saved] + [sds((n, 2, w, w), BF16), sds((n, 1, w), F32)] + out_shape,
        compiler_params=params(),
        cost_estimate=SMALL_COST,
        name="forward",
    )(meta, units, pads, *xs, vec, wqkv, bqkv, wfc, wfc, bfc, bfc, cf, cos_t, sin_t, wd, wp, wp)


def grad_kernel(meta, g_ref, gp, wd, wp_a, wp_b, *refs):
    dao_o, dh_o, sum_o, g_sum_o = refs[-4:]

    @pl.when(pl.program_id(0) == 0)
    def _():
        sum_o[...] = jnp.zeros_like(sum_o)
        g_sum_o[...] = jnp.zeros_like(g_sum_o)

    hh = wp_a.shape[0]
    g = g_ref[...]
    g_sum_o[...] += jnp.sum(g.astype(F32), axis=0, keepdims=True)
    dao_o[...] = mm(g, wd[...], NT).astype(BF16)
    for cols, wp in ((slice(0, hh), wp_a), (slice(hh, 2 * hh), wp_b)):
        dh = (mm(g, wp[...], NT) * gp[:, cols].astype(F32)).astype(BF16)
        dh_o[:, cols] = dh
        sum_o[:, cols] += jnp.sum(dh.astype(F32), axis=0, keepdims=True)


def grad_call(meta, parts, g, gp, wd, wp, deps=()):
    rows, hid = gp.shape
    w, width = wd.shape
    rb = rows // parts
    core = meta.shape[0] - 1
    sds = jax.ShapeDtypeStruct

    def plain(n):
        return pl.BlockSpec((rb, n), lambda i, m: (i, 0))

    return pl.pallas_call(
        grad_kernel,
        grid_spec=pltpu.PrefetchScalarGridSpec(
            num_scalar_prefetch=1,
            grid=(parts,),
            in_specs=[
                plain(width),
                plain(hid),
                const(wd.shape),
                pl.BlockSpec((hid // 2, width), lambda i, m: (m[core], 0), pipeline_mode=pl.Buffered(1)),
                pl.BlockSpec((hid // 2, width), lambda i, m: (1 - m[core], 0), pipeline_mode=pl.Buffered(1)),
            ]
            + unread(deps),
            out_specs=[plain(w), plain(hid), whole((1, hid)), whole((1, width))],
        ),
        out_shape=[sds((rows, w), BF16), sds((rows, hid), BF16), sds((1, hid), F32), sds((1, width), F32)],
        compiler_params=params(),
        cost_estimate=SMALL_COST,
        name="branch_grads",
    )(meta, g, gp, wd, wp, wp, *deps)


def attn_bwd_kernel(
    hd, nseq, meta, units, pads, dao, v_ref, o_ref, rd_ref, fq_ref, fk_ref, rq_ref, rk_ref, s_ref, ks_ref,
    cf, cos_t, sin_t, dct_bd, *refs,
):
    dqkv_o, sum_o, feat_o, after, after_sum, feat = refs[-6:]
    w = v_ref.shape[1]
    heads = w // hd
    step = pl.program_id(0)
    block = pl.num_programs(0) - 1 - step
    per = dao.shape[0] // UNIT

    @pl.when(step == 0)
    def _():
        for ref in (after, after_sum, feat, sum_o):
            ref[...] = jnp.zeros_like(ref)

    head_of_lane, diag, causal = masks(w, hd)
    low_half = lax.broadcasted_iota(jnp.int32, (UNIT, w), 1) % hd < ROT // 2
    ones_bd = jnp.where(diag, 1.0, 0.0).astype(BF16)
    back_hi, back_lo = cf[2], cf[3]
    for i in reversed(range(per)):
        pos, _, last = chunk_place(units, pads, block * per + i, nseq)
        rows = slice(i * UNIT, (i + 1) * UNIT)
        at = pl.ds(pl.multiple_of(pos * UNIT, UNIT), UNIT)
        cosines = lanes(cos_t[at, :], w)
        sines = -lanes(sin_t[at, :], w)
        keep = jnp.where(last == 1, 0.0, 1.0)
        a_old = after[...] * keep
        as_old = after_sum[...] * keep
        fq, fk, v = fq_ref[rows, :], fk_ref[rows, :], v_ref[rows, :]
        fqf, fkf = fq.astype(F32), fk.astype(F32)
        dn = (dao[rows, :].astype(F32) * rd_ref[rows, :]).astype(BF16)
        p_hi, p_lo = split(dn.astype(F32) * o_ref[rows, :])
        dden = -(mm(p_hi, ones_bd) + mm(p_lo, ones_bd))
        dn_s = head_stack(dn, head_of_lane, heads)
        fq_s = head_stack(fq, head_of_lane, heads)
        dden_s = jnp.concatenate(
            [jnp.broadcast_to(dden[:, h * hd : h * hd + 1], (UNIT, UNIT)) for h in range(heads)], axis=0
        )
        da = jnp.where(causal, mm(dn_s, v, NT) + dden_s, 0.0).astype(BF16)
        a = jnp.where(causal, mm(fq_s, fk, NT), 0.0).astype(BF16)
        s_hi, s_lo = s_ref[i, 0], s_ref[i, 1]
        dfq = (
            mm(side_by_side(da, heads), head_stack(fk, head_of_lane, heads))
            + mm(dn, s_hi, NT)
            + mm(dn, s_lo, NT)
            + dden * ks_ref[i]
        )
        a_hi, a_lo = split(a_old)
        dfk = mm(da, fq_s, TN) + mm(v, a_hi, NT) + mm(v, a_lo, NT) + as_old
        dv = mm(a, dn_s, TN) + mm(fk, a_hi)
        after[...] = a_old + jnp.where(diag, mm(fq, dn, TN), 0.0)
        after_sum[...] = as_old + jnp.sum(fqf * dden, axis=0, keepdims=True)
        dsq = (dfq * fqf).astype(BF16)
        dsk = (dfk * fkf).astype(BF16)
        feat[...] += mm(rq_ref[rows, :], dsq, TN) + mm(rk_ref[rows, :], dsk, TN)
        dq = turn(mm(dsq, back_hi) + mm(dsq, back_lo), cosines, sines, low_half)
        dk = turn(mm(dsk, back_hi) + mm(dsk, back_lo), cosines, sines, low_half)
        for j, part in enumerate((dq, dk, dv)):
            part = part.astype(BF16)
            dqkv_o[rows, j * w : (j + 1) * w] = part
            sum_o[:, j * w : (j + 1) * w] += jnp.sum(part.astype(F32), axis=0, keepdims=True)

    @pl.when(block == 0)
    def _():
        turned = lax.dot_general(
            dct_bd[...],
            jnp.where(diag, feat[...], 0.0),
            TN,
            precision=lax.Precision.HIGHEST,
            preferred_element_type=F32,
        )
        total = turned[0:hd, :]
        for h in range(1, heads):
            total = total + turned[h * hd : (h + 1) * hd, :]
        feat_o[...] = total


def attn_bwd_call(meta, units, pads, dao, v, o, rd, fq, fk, rq, rk, s, ks, cf, cos_t, sin_t, dct_bd, hd, parts, deps=()):
    rows, w = v.shape
    rb = rows // parts
    per = rb // UNIT
    smem = pl.BlockSpec(memory_space=pltpu.SMEM)
    sds = jax.ShapeDtypeStruct

    def at(i, m):
        return (m[parts - 1 - i], 0)

    return pl.pallas_call(
        partial(attn_bwd_kernel, hd, units.shape[1]),
        grid_spec=pltpu.PrefetchScalarGridSpec(
            num_scalar_prefetch=1,
            grid=(parts,),
            in_specs=[smem, smem]
            + [pl.BlockSpec((rb, w), at)] * 8
            + [
                pl.BlockSpec((per, 2, w, w), lambda i, m: (m[parts - 1 - i], 0, 0, 0)),
                pl.BlockSpec((per, 1, w), lambda i, m: (m[parts - 1 - i], 0, 0)),
                const(cf.shape),
                const(cos_t.shape),
                const(sin_t.shape),
                const(dct_bd.shape),
            ]
            + unread(deps),
            out_specs=[pl.BlockSpec((rb, 3 * w), at), whole((1, 3 * w)), whole((hd, w))],
            scratch_shapes=[pltpu.VMEM((w, w), F32), pltpu.VMEM((1, w), F32), pltpu.VMEM((w, w), F32)],
        ),
        out_shape=[sds((rows, 3 * w), BF16), sds((1, 3 * w), F32), sds((hd, w), F32)],
        compiler_params=params(),
        cost_estimate=SMALL_COST,
        name="attn_bwd",
    )(meta, units, pads, dao, v, o, rd, fq, fk, rq, rk, s, ks, cf, cos_t, sin_t, dct_bd, *deps)


SMALL_ROWS = 32


def norms_kernel(shards, deps, meta, *refs):
    x_refs = refs[:shards]
    dqkv, dh, vec, wqkv, wfc_a, wfc_b, g_sum, hid_sum, qkv_sum, feat, *rest = refs[shards:]
    small_o, *outs, xbuf = rest[deps:]
    step = pl.program_id(0)
    hh = wfc_a.shape[1]
    slot = step

    @pl.when(step == 0)
    def _():
        small_o[...] = jnp.zeros_like(small_o)
        hid_row = hid_sum[...]
        swapped = jnp.concatenate([hid_row[:, hh:], hid_row[:, :hh]], axis=1)
        hid_row = jnp.where(meta[meta.shape[0] - 1] == 1, swapped, hid_row)
        for at, row in ((4, g_sum[...]), (5, hid_row), (6, qkv_sum[...])):
            small_o[at : at + 1, 0 : row.shape[1]] = row
        deep, w = feat.shape
        each = deep * w // small_o.shape[1]
        for j in range(deep // each):
            small_o[8 : 8 + each, j * w : (j + 1) * w] = feat[j * each : (j + 1) * each, :]

    xh, _ = norm_rows(pick_rows(x_refs, slot, xbuf).astype(F32))
    da = mm(dqkv[...], wqkv[...], NT)
    small_o[0:1, :] += jnp.sum(da * xh, axis=0, keepdims=True)
    small_o[1:2, :] += jnp.sum(da, axis=0, keepdims=True)
    dm = mm(dh[:, :hh], wfc_a[...], NT) + mm(dh[:, hh:], wfc_b[...], NT)
    small_o[2:3, :] += jnp.sum(dm * xh, axis=0, keepdims=True)
    small_o[3:4, :] += jnp.sum(dm, axis=0, keepdims=True)
    put(outs, slot, (da * vec[0:1, :] + dm * vec[2:3, :]).astype(BF16))


def norms_call(meta, parts, xs, dqkv, dh, vec, wqkv, wfc, g_sum, hid_sum, qkv_sum, feat, deps=()):
    rows, hid = dh.shape
    width, cols = wqkv.shape
    hh = hid // 2
    rb = rows // parts
    core = meta.shape[0] - 1

    def at(i, m):
        return (i, 0)

    def to(i, m):
        return (m[i], 0)

    def half(shape, index):
        return pl.BlockSpec(shape, index, pipeline_mode=pl.Buffered(1))

    out_specs, out_shape = put_specs(len(xs) > 1, rb, width, rows, at)
    small = (SMALL_ROWS, width)
    return pl.pallas_call(
        partial(norms_kernel, len(xs), len(deps)),
        grid_spec=pltpu.PrefetchScalarGridSpec(
            num_scalar_prefetch=1,
            grid=(parts,),
            in_specs=rows_specs(xs, rb, at)
            + [
                pl.BlockSpec((rb, cols), at),
                pl.BlockSpec((rb, hid), at),
                const(vec.shape),
                const(wqkv.shape),
                half((width, hh), lambda i, m: (0, m[core])),
                half((width, hh), lambda i, m: (0, 1 - m[core])),
                const(g_sum.shape),
                const(hid_sum.shape),
                const(qkv_sum.shape),
                const(feat.shape),
            ]
            + unread(deps),
            out_specs=[whole(small)] + out_specs,
            scratch_shapes=[pltpu.VMEM((rb, width), BF16)],
        ),
        out_shape=[jax.ShapeDtypeStruct(small, F32)] + out_shape,
        compiler_params=params(),
        cost_estimate=SMALL_COST,
        name="norm_grads",
    )(meta, *xs, dqkv, dh, vec, wqkv, wfc, wfc, g_sum, hid_sum, qkv_sum, feat, *deps)


class Order:
    def __init__(self):
        self.last = None

    def after(self, *arrays):
        if self.last is None:
            return arrays if len(arrays) > 1 else arrays[0]
        self.last, *arrays = lax.optimization_barrier((self.last, *arrays))
        return tuple(arrays) if len(arrays) > 1 else arrays[0]

    def did(self, array):
        self.last = array
        return array


def both(a, b):
    return (a.astype(F32) + b.astype(F32)).astype(a.dtype)


def totals_kernel(count, mid, *refs):
    total = refs[-1]
    rows = refs[0].shape[0]
    for k in range(count):
        own, sent = refs[2 * k], refs[2 * k + 1]

        @pl.when(mid[0] == 1)
        def _():
            total[k * rows : (k + 1) * rows, :] = own[...]

        @pl.when(mid[0] == 0)
        def _():
            total[k * rows : (k + 1) * rows, :] = sent[...]


def totals_call(mid, pairs, deps):
    rows, cols = pairs[0].shape
    count = len(pairs) // 2
    return pl.pallas_call(
        partial(totals_kernel, count),
        in_specs=[pl.BlockSpec(memory_space=pltpu.SMEM)] + [whole((rows, cols))] * len(pairs) + unread(deps),
        out_specs=whole((count * rows, cols)),
        out_shape=jax.ShapeDtypeStruct((count * rows, cols), BF16),
        compiler_params=pltpu.CompilerParams(vmem_limit_bytes=VMEM_BYTES),
        cost_estimate=SMALL_COST,
        name="totals",
    )(mid.astype(jnp.int32).reshape(1), *pairs, *deps)


class Line:
    swap = [(i, i ^ 1) for i in range(8)]
    inward = [(0, 2), (1, 3), (6, 4), (7, 5)]
    inner = [(2, 4), (4, 2), (3, 5), (5, 3)]
    outward = [(2, 0), (3, 1), (4, 6), (5, 7)]

    def __init__(self, order):
        index = lax.axis_index("batch")
        self.order = order
        self.core, z = index % 2, index // 2
        self.mid = (z == 1) | (z == 2)
        self.own, self.sent = {}, {}

    def start(self, k, own, other):
        self.own[k], self.sent[k] = own, lax.ppermute(other, "batch", self.swap)

    def add(self, k, to):
        own, sent = self.order.after(self.own[k], self.sent[k])
        self.own[k] = self.order.did(both(own, sent))
        self.sent[k] = lax.ppermute(self.own[k], "batch", to)

    def go_in(self, k):
        self.add(k, self.inward)

    def meet(self, k):
        self.add(k, self.inner)

    def go_out(self, k):
        self.add(k, self.outward)

    def held(self, *ks):
        return tuple(self.own[k] for k in ks)

    def arrived(self, *ks):
        return tuple(self.sent[k] for k in ks)

    def landed(self, *ks):
        for k in ks:
            self.own[k], self.sent[k] = self.order.after(self.own[k], self.sent[k])

    def end(self, *ks, deps=()):
        self.landed(*ks)
        if deps:
            total = totals_call(self.mid, [a for k in ks for a in (self.own[k], self.sent[k])], deps)
        else:
            total = jnp.concatenate([jnp.where(self.mid, self.own[k], self.sent[k]) for k in ks])
        total = self.order.did(total)
        return total, lax.ppermute(total, "batch", self.swap)

    def end_small(self, k):
        self.landed(k)
        return jnp.where(self.mid, self.own[k], self.sent[k])


def across(a, mask):
    return lax.ppermute(a, "tensor", [(i, i ^ mask) for i in range(4)])


def part_of_batch(a):
    return lax.psum_scatter(a, "batch", scatter_dimension=0, tiled=True)


class TwoStepSum:
    def __init__(self, order, blocks):
        self.order = order
        self.keep_a, send_a, self.keep_b, send_b = blocks
        self.got_a, self.got_b = across(send_a, 1), across(send_b, 2)

    def second(self):
        rb = self.keep_a.shape[0] // 2
        self.got_a, self.got_b = self.order.after(self.got_a, self.got_b)
        a = both(self.keep_a[rb:], self.got_a[rb:])
        b = both(self.keep_b[rb:], self.got_b[rb:])
        a, b = lax.optimization_barrier((a, b))
        self.order.did(b)
        self.last_a, self.last_b = across(a, 2), across(b, 1)

    def result(self):
        rb = self.keep_a.shape[0] // 2
        terms = ((self.keep_a, self.got_a, self.last_a), (self.keep_b, self.got_b, self.last_b))
        return jnp.concatenate([sum(t[:rb].astype(F32) for t in side) for side in terms], axis=1)


def cosine_blocks(hd, heads):
    spatial = np.arange(hd, dtype=np.float64)[:, None]
    frequency = np.arange(hd, dtype=np.float64)[None, :]
    table = np.cos(math.pi * (2.0 * spatial + 1.0) * frequency / (2.0 * hd)) * math.sqrt(2.0 / hd)
    table[:, 0] *= math.sqrt(0.5)
    return np.kron(np.eye(heads), table).astype(np.float32)


def turn_tables(rows, hd):
    half = ROT // 2
    inverse_freq = np.exp(-math.log(10000.0) * 2.0 * np.arange(half) / ROT)
    angles = np.arange(rows)[:, None] * inverse_freq[None, :]
    cosines, sines = np.cos(angles), np.sin(angles)
    rest = np.ones((rows, hd - ROT))
    reps = (1, 128 // hd)
    return (
        np.tile(np.concatenate([cosines, cosines, rest], axis=1), reps).astype(np.float32),
        np.tile(np.concatenate([-sines, sines, 0.0 * rest], axis=1), reps).astype(np.float32),
    )


def column_pick(heads, hd):
    n = 3 * heads * hd
    source = np.arange(n).reshape(heads, 3, hd).transpose(1, 0, 2).reshape(-1)
    pick = np.zeros((n, n), np.float32)
    pick[source, np.arange(n)] = 1.0
    return pick


def body(
    tokens,
    output_grad,
    attn_norm_gain,
    attn_norm_bias,
    mlp_norm_gain,
    mlp_norm_bias,
    qkv_weight,
    qkv_bias,
    dense_weight,
    dense_bias,
    fc_weight,
    fc_bias,
    proj_weight,
    feature_weight,
    seq_units,
    pad_tokens,
):
    rows_dev, width = tokens.shape
    parts = lax.axis_size("tensor")
    n_batch = lax.axis_size("batch")
    rows = rows_dev * parts
    heads, hd, _ = feature_weight.shape
    w = heads * hd
    hid = fc_weight.shape[1]

    square = parts == 4 and n_batch == 8 and hid == width and 4 * w == width
    position = lax.axis_index("tensor")
    order = Order()
    line = Line(order) if square else None
    slots = jnp.arange(parts, dtype=jnp.int32)
    core = jnp.int32(0)
    if square:
        slots = slots ^ position
        core = line.core
        mid = rows_dev // 2
        a1, a2 = across(tokens, 1), across(tokens, 2)
    tail = jnp.stack([jnp.int32(rows_dev // UNIT), core.astype(jnp.int32)])
    meta = jnp.concatenate([slots, tail])
    vec = jnp.stack([attn_norm_gain, attn_norm_bias, mlp_norm_gain, mlp_norm_bias]).astype(F32)
    dct_bd = jnp.asarray(cosine_blocks(hd, heads))
    cos_t, sin_t = (jnp.asarray(t) for t in turn_tables(rows, hd))
    pick = jnp.asarray(column_pick(heads, hd)).astype(BF16)
    bfc = fc_bias.astype(F32).reshape(1, hid)
    wqkv, bqkv, cf_pair = prep_call(
        qkv_weight, qkv_bias.reshape(1, 3 * w), feature_weight.reshape(w, hd), pick, dct_bd, hd, (meta, vec, bfc)
    )
    hh = hid // 2
    dm = width // 2
    g_float = output_grad.astype(F32)
    x_own = tokens.astype(F32)
    if square:
        order.did(wqkv)
        a1, a2 = order.after(a1, a2)
        b1, b2 = across(a1[:mid], 2), across(a2[mid:], 1)
        b1, b2 = order.after(b1, b2)
        g_own, b1, b2 = lax.optimization_barrier((output_grad, b1, b2))
        c1, c2, c3 = across(g_own, 1), across(g_own, 2), across(g_own, 3)
        xs = [tokens, a1, a2, b1, b2]
    else:
        xs = [lax.all_gather(tokens, "tensor", axis=0, tiled=True)]
        g_all = lax.all_gather(output_grad, "tensor", axis=0, tiled=True)
    lna, lnm, act, gp, fq, fk, rq, rk, v, ao, o, rd, s, ks, *outs = forward_call(
        meta, seq_units, pad_tokens, xs, vec, wqkv, bqkv, fc_weight, bfc, cf_pair, cos_t, sin_t,
        dense_weight, proj_weight, hd, parts, rows,
    )
    order.did(ao)
    def residual(total):
        return (x_own + total + dense_bias.astype(F32)).astype(BF16)

    def proj_piece(k, cols):
        g = order.after(g_all)[:, cols]
        line.start(k, mm(act[:, :hh], g, TN).astype(BF16), order.did(mm(act[:, hh:], g, TN).astype(BF16)))

    def fc_piece(k, cols):
        part = order.after(lnm)[:, cols]
        line.start(k, mm(part, dh[:, :hh], TN).astype(BF16), order.did(mm(part, dh[:, hh:], TN).astype(BF16)))

    def rest_piece(k, cols):
        part, cotangent = order.after(lna, dqkv)
        stack = jnp.concatenate([mm(ao, g_all[:, cols], TN), mm(cotangent, part[:, cols], TN)])
        stack = stack.astype(BF16).reshape(2, 2 * w, dm)
        own = lax.dynamic_index_in_dim(stack, line.core, 0, keepdims=False)
        other = lax.dynamic_index_in_dim(stack, 1 - line.core, 0, keepdims=False)
        order.did(other)
        line.start(k, own, other)

    left, right = slice(0, dm), slice(dm, width)
    if square:
        branch = TwoStepSum(order, outs)
        c1, c2, c3 = order.after(c1, c2, c3)
        g_all = order.did(jnp.concatenate([output_grad, c1, c2, c3]))
        proj_piece(0, left)
        proj_piece(1, right)
        line.go_in(0)
        line.go_in(1)
        g_all = order.after(g_all)
    dao, dh, hid_sum, g_sum = grad_call(meta, parts, g_all, gp, dense_weight, proj_weight, line.held(0, 1) if square else ())
    order.did(dao)
    if square:
        branch.second()
        line.meet(0)
        fc_piece(2, left)
        line.go_in(2)
        fc_piece(3, right)
        line.meet(1)
        branch.last_a, branch.last_b = order.after(branch.last_a, branch.last_b)
        output = order.did(residual(branch.result()))
        line.go_out(0)
        line.go_in(3)
    dao = order.after(dao)
    dqkv, qkv_sum, feat = attn_bwd_call(
        meta, seq_units, pad_tokens, dao, v, o, rd, fq, fk, rq, rk, s, ks, cf_pair, cos_t, sin_t, dct_bd, hd, parts,
        (*line.held(0, 1, 2, 3), output) if square else (),
    )
    order.did(dqkv)
    if square:
        line.meet(2)
        line.go_out(1)
        rest_piece(4, left)
        line.landed(0)
        line.meet(3)
        line.go_in(4)
        rest_piece(5, right)
        line.go_in(5)
        line.landed(1)
        line.go_out(2)
    dqkv = order.after(dqkv)
    small, *es = norms_call(meta, parts, xs, dqkv, dh, vec, wqkv, fc_weight, g_sum, hid_sum, qkv_sum, feat,
        (*line.held(2, 3, 4, 5), *line.arrived(0, 1)) if square else ())
    order.did(small)

    def rows_grad(e):
        x_hat, inv_std = norm_rows(x_own)
        mean = jnp.mean(e, axis=-1, keepdims=True)
        return (g_float + inv_std * (e - mean - x_hat * jnp.mean(e * x_hat, axis=-1, keepdims=True))).astype(BF16)

    if square:
        line.meet(4)
        line.go_out(3)
        line.landed(2)
        small = order.after(small)
        line.start(6, small, small)
        es[1], es[3] = order.after(es[1], es[3])
        e_sum = TwoStepSum(order, es)
        line.go_in(6)
        line.meet(5)
        line.go_out(4)
        line.landed(3)
        first = line.end(0, 1, 2, 3)
        line.meet(6)
        second = line.core == 1

        def pieces_of(pair, count):
            own, twin = order.after(*pair)
            low = jnp.where(second, twin, own).reshape(count, 2 * w, dm)
            high = jnp.where(second, own, twin).reshape(count, 2 * w, dm)
            return low, high

        low, high = pieces_of(first, 4)
        proj_grad = order.did(
            jnp.concatenate(
                [jnp.concatenate([low[k], high[k]], axis=0) for k in (0, 1)], axis=1
            ).astype(F32)
        )
        e_sum.second()
        line.go_out(6)
        fc_grad = order.did(
            jnp.concatenate([jnp.concatenate([low[k], high[k]], axis=1) for k in (2, 3)], axis=0).astype(F32)
        )
        line.go_out(5)
        small = order.did(line.end_small(6))
        norm_sums = small[:8]
        hop = across(norm_sums, 1)
        e_sum.last_a, e_sum.last_b = order.after(e_sum.last_a, e_sum.last_b)
        tokens_grad = order.did(rows_grad(e_sum.result()))
        norm_sums = order.did(norm_sums + order.after(hop))
        hop = across(norm_sums, 2)
        last = line.end(4, 5, deps=(proj_grad, fc_grad, tokens_grad, norm_sums))
        norm_sums = norm_sums + order.after(hop)
        low, high = pieces_of(last, 2)
        rest = jnp.concatenate([jnp.concatenate([low[k], high[k]], axis=0) for k in (0, 1)], axis=1)
        dense_grad, qkv_grad = rest[:w].astype(F32), rest[w:]
        hid_sum = small[5]
        pick = jnp.asarray(column_pick(heads, hd)).astype(BF16)
        qkv_grad = lax.dot_general(qkv_grad.astype(BF16), pick, (((0,), (1,)), ((), ())), preferred_element_type=F32)
    else:
        output = residual(lax.psum_scatter(outs[0], "tensor", scatter_dimension=0, tiled=True).astype(F32))
        tokens_grad = rows_grad(lax.psum_scatter(es[0], "tensor", scatter_dimension=0, tiled=True).astype(F32))
        sums = [mm(act, g_all, TN), mm(lnm, dh, TN), mm(ao, g_all, TN), mm(dqkv, lna, TN)]
        sums = lax.psum([a.astype(BF16) for a in sums], "batch")
        proj_grad, fc_grad, dense_grad, qkv_grad = (a.astype(F32) for a in sums)
        small = lax.psum(small, "batch")
        norm_sums = lax.psum(small[:4], "tensor")
        hid_sum = small[5, :hid]
        qkv_grad = qkv_grad.reshape(3, heads, hd, width).transpose(3, 1, 0, 2).reshape(width, 3 * w)
    each = hd * w // width
    feature_grad = small[8 : 8 + each].reshape(each, width // w, heads, hd).transpose(2, 1, 0, 3).reshape(heads, hd, hd)
    qkv_bias_grad = small[6, : 3 * w].reshape(3, heads, hd).transpose(1, 0, 2).reshape(3 * w)

    return (
        output,
        tokens_grad,
        norm_sums[0],
        norm_sums[1],
        norm_sums[2],
        norm_sums[3],
        qkv_grad,
        qkv_bias_grad,
        dense_grad,
        small[4],
        fc_grad,
        hid_sum,
        proj_grad,
        feature_grad,
    )


def solution(mesh):
    rows = P(("batch", "tensor"), None)
    placed = (
        rows,
        rows,
        P(),
        P(),
        P(),
        P(),
        P(None, "tensor"),
        P("tensor"),
        P("tensor", None),
        P(),
        P(None, "tensor"),
        P("tensor"),
        P("tensor", None),
        P("tensor", None, None),
        P("batch", None),
        P("batch", None),
    )
    return jax.shard_map(
        body,
        mesh=mesh,
        in_specs=placed,
        out_specs=(
            rows,
            rows,
            P(),
            P(),
            P(),
            P(),
            P(None, "tensor"),
            P("tensor"),
            P("tensor", None),
            P(),
            P(None, "tensor"),
            P("tensor"),
            P("tensor", None),
            P("tensor", None, None),
        ),
        check_vma=False,
    )
```

```python
from functools import partial
import math

import jax
import jax.numpy as jnp
import numpy as np
from jax import lax
from jax.experimental import pallas as pl
from jax.experimental.pallas import tpu as pltpu
from jax.sharding import PartitionSpec as P

ROT = 16
UNIT = 128
EPS = 1e-05
F32 = jnp.float32
BF16 = jnp.bfloat16
VMEM_BYTES = 54 * 1024 * 1024

NN = (((1,), (0,)), ((), ()))
NT = (((1,), (1,)), ((), ()))
TN = (((0,), (0,)), ((), ()))


def mm(a, b, dims=NN):
    return lax.dot_general(a, b, dims, preferred_element_type=F32)


def split(a):
    hi = a.astype(BF16)
    return hi, (a - hi.astype(F32)).astype(BF16)


HELD_SPACE = pl.ANY
SMALL_COST = pl.CostEstimate(flops=1000, bytes_accessed=1000, transcendentals=0)


def params(grid_rank=1):
    return pltpu.CompilerParams(
        dimension_semantics=("arbitrary",) * grid_rank, vmem_limit_bytes=VMEM_BYTES
    )


def whole(shape):
    return pl.BlockSpec(shape, lambda *_: (0,) * len(shape))


def rows_of(block, width):
    return pl.BlockSpec((block, width), lambda i: (i, 0))


def norm_rows(x):
    mean = jnp.mean(x, axis=-1, keepdims=True)
    cent = x - mean
    inv = lax.rsqrt(jnp.mean(cent * cent, axis=-1, keepdims=True) + EPS)
    return cent * inv, inv


def chunk_place(units, pads, chunk, nseq):
    start = jnp.int32(0)
    pos, real, last = jnp.int32(0), jnp.int32(0), jnp.int32(0)
    for n in range(nseq):
        u = units[0, n]
        inside = (chunk >= start) & (chunk < start + u)
        pos = jnp.where(inside, chunk - start, pos)
        real = jnp.where(inside, (start + u - chunk) * UNIT - pads[0, n], real)
        last = jnp.where(inside, (chunk == start + u - 1).astype(jnp.int32), last)
        start = start + u
    return pos, real, last


def lanes(table, w):
    return jnp.concatenate([table] * (w // table.shape[1]), axis=1) if w > table.shape[1] else table


def turn(a, cosines, sines, low_half):
    w = a.shape[1]
    other = jnp.where(low_half, pltpu.roll(a, w - ROT // 2, 1), pltpu.roll(a, ROT // 2, 1))
    return a * cosines + other * sines


def head_stack(a, head_of_lane, heads):
    zero = jnp.zeros_like(a)
    return jnp.concatenate([jnp.where(head_of_lane == h, a, zero) for h in range(heads)], axis=0)


def side_by_side(a, heads):
    return jnp.concatenate([a[h * UNIT : (h + 1) * UNIT, :] for h in range(heads)], axis=1)


def masks(w, hd):
    lane = lax.broadcasted_iota(jnp.int32, (UNIT, w), 1)
    head_of_lane = lane // hd
    bi = lax.broadcasted_iota(jnp.int32, (w, w), 0) // hd
    bj = lax.broadcasted_iota(jnp.int32, (w, w), 1) // hd
    heads = w // hd
    row = lax.broadcasted_iota(jnp.int32, (heads * UNIT, UNIT), 0) % UNIT
    col = lax.broadcasted_iota(jnp.int32, (heads * UNIT, UNIT), 1)
    return head_of_lane, bi == bj, row >= col


def prep_kernel(hd, wqkv, bqkv, feat, pick, dct_bd, *refs):
    wqkv_o, bqkv_o, cf_o = refs[-3:]
    w = dct_bd.shape[0]
    wqkv_o[...] = mm(wqkv[...], pick[...]).astype(BF16)
    bqkv_o[...] = mm(jnp.broadcast_to(bqkv[...], (8, 3 * w)), pick[...])
    diag = lax.broadcasted_iota(jnp.int32, (w, w), 0) // hd == lax.broadcasted_iota(jnp.int32, (w, w), 1) // hd
    spread = jnp.where(diag, jnp.concatenate([feat[...].astype(F32)] * (w // hd), axis=1), 0.0)
    cf_hi, cf_lo = split(
        lax.dot_general(dct_bd[...], spread, NN, precision=lax.Precision.HIGHEST, preferred_element_type=F32)
    )
    cf_o[0] = cf_hi
    cf_o[1] = cf_lo
    back_hi, back_lo = split(
        lax.dot_general(spread, dct_bd[...], (((0,), (1,)), ((), ())), precision=lax.Precision.HIGHEST, preferred_element_type=F32)
    )
    cf_o[2] = back_hi
    cf_o[3] = back_lo


def prep_call(wqkv, bqkv, feat, pick, dct_bd, hd, deps=()):
    width, cols = wqkv.shape
    w = cols // 3
    sds = jax.ShapeDtypeStruct
    return pl.pallas_call(
        partial(prep_kernel, hd),
        in_specs=[whole(a.shape) for a in (wqkv, bqkv, feat, pick, dct_bd)] + unread(deps),
        out_shape=[sds((width, cols), BF16), sds((8, cols), F32), sds((4, w, w), BF16)],
        compiler_params=pltpu.CompilerParams(vmem_limit_bytes=VMEM_BYTES),
        cost_estimate=SMALL_COST,
        name="prepare",
    )(wqkv, bqkv, feat, pick, dct_bd, *deps)


def gelu_pair(h):
    bell = jnp.exp(h * h * -0.5)
    cdf = 0.5 + 0.5 * lax.erf(h * math.sqrt(0.5))
    return h * cdf, cdf + (h * bell) * (1.0 / math.sqrt(2.0 * math.pi))


def pick_rows(refs, slot, into):
    if len(refs) == 1:
        return refs[0][...]
    rb = into.shape[0]
    for j, ref in enumerate(refs):
        at = slice(0, rb) if j < 3 else slice(0, rb // 2) if j == 3 else slice(rb // 2, rb)

        @pl.when(slot == min(j, 3))
        def _():
            into[at, :] = ref[...]

    return into[...]


def rows_specs(arrays, rb, at):
    if len(arrays) == 1:
        return [pl.BlockSpec((rb, arrays[0].shape[1]), at)]
    return [const(a.shape) for a in arrays]


def put(outs, slot, value):
    if len(outs) == 1:
        outs[0][...] = value
        return
    rb, half = value.shape[0], value.shape[1] // 2
    keep_a, send_a, keep_b, send_b = outs
    for j, (a, b) in enumerate(((keep_a, keep_b), (send_a, keep_b), (keep_a, send_b), (send_a, send_b))):

        @pl.when(slot == j)
        def _():
            a[(j // 2) * rb : (j // 2 + 1) * rb, :] = value[:, :half]
            b[(j % 2) * rb : (j % 2 + 1) * rb, :] = value[:, half:]


def put_specs(apart, rb, width, total, at):
    if apart:
        shape = (2 * rb, width // 2)
        return [whole(shape)] * 4, [jax.ShapeDtypeStruct(shape, BF16)] * 4
    return [pl.BlockSpec((rb, width), at)], [jax.ShapeDtypeStruct((total, width), BF16)]


def unread(arrays):
    return [pl.BlockSpec(memory_space=pl.ANY)] * len(arrays)


def const(shape):
    return pl.BlockSpec(shape, lambda *_: (0,) * len(shape), pipeline_mode=pl.Buffered(1))


def forward_kernel(hd, shards, nseq, meta, units, pads, *refs):
    x_refs = refs[:shards]
    vec, wqkv, bqkv, wfc_a, wfc_b, bfc_a, bfc_b, cf, cos_t, sin_t, wd, wp_a, wp_b = refs[shards : shards + 13]
    lna_o, lnm_o, act_o, gp_o, fq_o, fk_o, rq_o, rk_o, v_o, ao_o, o_o, rd_o, s_o, ks_o = refs[shards + 13 : shards + 27]
    *outs, xbuf, state, ksum = refs[shards + 27 :]
    step = pl.program_id(0)
    slot = meta[step]
    w, hh, per = v_o.shape[1], bfc_a.shape[1], xbuf.shape[0] // UNIT
    heads = w // hd

    @pl.when(step == 0)
    def _():
        state[...] = jnp.zeros_like(state)
        ksum[...] = jnp.zeros_like(ksum)

    xh, _ = norm_rows(pick_rows(x_refs, slot, xbuf).astype(F32))
    lna = (xh * vec[0:1, :] + vec[1:2, :]).astype(BF16)
    lnm = (xh * vec[2:3, :] + vec[3:4, :]).astype(BF16)
    lna_o[...] = lna
    lnm_o[...] = lnm
    qkv = mm(lna, wqkv[...]) + bqkv[0:1, :]
    v_o[...] = qkv[:, 2 * w :].astype(BF16)
    for cols, wfc, bfc in ((slice(0, hh), wfc_a, bfc_a), (slice(hh, 2 * hh), wfc_b, bfc_b)):
        act, slope = gelu_pair(mm(lnm, wfc[...]) + bfc[...])
        act_o[:, cols] = act.astype(BF16)
        gp_o[:, cols] = slope.astype(BF16)

    head_of_lane, diag, causal = masks(w, hd)
    low_half = lax.broadcasted_iota(jnp.int32, (UNIT, w), 1) % hd < ROT // 2
    row_id = lax.broadcasted_iota(jnp.int32, (UNIT, 1), 0)
    ones_bd = jnp.where(diag, 1.0, 0.0).astype(BF16)
    head_ones = head_stack(jnp.ones((UNIT, w), BF16), head_of_lane, heads)
    cf_hi, cf_lo = cf[0], cf[1]
    for i in range(per):
        pos, real, _ = chunk_place(units, pads, step * per + i, nseq)
        at = pl.ds(pl.multiple_of(pos * UNIT, UNIT), UNIT)
        cosines = lanes(cos_t[at, :], w)
        sines = lanes(sin_t[at, :], w)
        rows = slice(i * UNIT, (i + 1) * UNIT)
        rq = turn(qkv[rows, 0:w], cosines, sines, low_half)
        rk = turn(qkv[rows, w : 2 * w], cosines, sines, low_half)
        qh, ql = split(rq)
        kh, kl = split(rk)
        rq_o[rows, :] = qh
        rk_o[rows, :] = kh
        fq = jnp.exp(mm(qh, cf_hi) + mm(ql, cf_hi) + mm(qh, cf_lo)).astype(BF16)
        ek = jnp.exp(mm(kh, cf_hi) + mm(kl, cf_hi) + mm(kh, cf_lo))
        fk = jnp.where(row_id < real, ek, 0.0).astype(BF16)
        fq_o[rows, :] = fq
        fk_o[rows, :] = fk
        v = v_o[rows, :]
        keep = jnp.where(pos == 0, 0.0, 1.0)
        s_old = state[...] * keep
        k_old = ksum[...] * keep
        s_hi, s_lo = split(s_old)
        s_o[i, 0] = s_hi
        s_o[i, 1] = s_lo
        ks_o[i] = k_old
        scores = jnp.where(causal, mm(head_stack(fq, head_of_lane, heads), fk, NT), 0.0).astype(BF16)
        wide = side_by_side(scores, heads)
        num = mm(wide, head_stack(v, head_of_lane, heads)) + mm(fq, s_hi) + mm(fq, s_lo)
        p_hi, p_lo = split(fq.astype(F32) * k_old)
        den = mm(wide, head_ones) + mm(p_hi, ones_bd) + mm(p_lo, ones_bd)
        rden = 1.0 / den
        o = num * rden
        o_o[rows, :] = o
        rd_o[rows, :] = rden
        ao_o[rows, :] = o.astype(BF16)
        state[...] = s_old + jnp.where(diag, mm(fk, v, TN), 0.0)
        ksum[...] = k_old + jnp.sum(fk.astype(F32), axis=0, keepdims=True)

    out = mm(ao_o[...], wd[...]) + mm(act_o[:, :hh], wp_a[...]) + mm(act_o[:, hh:], wp_b[...])
    put(outs, slot, out.astype(BF16))


def forward_call(meta, units, pads, xs, vec, wqkv, bqkv, wfc, bfc, cf, cos_t, sin_t, wd, wp, hd, parts, rows):
    width, cols = wqkv.shape
    w, hid = cols // 3, wfc.shape[1]
    hh = hid // 2
    rb = rows // parts
    per, n = rb // UNIT, rows // UNIT
    core = meta.shape[0] - 1
    smem = pl.BlockSpec(memory_space=pltpu.SMEM)
    sds = jax.ShapeDtypeStruct

    def at(i, m):
        return (m[i], 0)

    def half(shape, index):
        return pl.BlockSpec(shape, index, pipeline_mode=pl.Buffered(1))

    out_specs, out_shape = put_specs(len(xs) > 1, rb, width, rows, at)
    saved = [(width, BF16)] * 2 + [(hid, BF16)] * 2 + [(w, BF16)] * 6 + [(w, F32)] * 2
    return pl.pallas_call(
        partial(forward_kernel, hd, len(xs), units.shape[1]),
        grid_spec=pltpu.PrefetchScalarGridSpec(
            num_scalar_prefetch=1,
            grid=(parts,),
            in_specs=[smem, smem]
            + rows_specs(xs, rb, at)
            + [
                const(vec.shape),
                const(wqkv.shape),
                const(bqkv.shape),
                half((width, hh), lambda i, m: (0, m[core])),
                half((width, hh), lambda i, m: (0, 1 - m[core])),
                half((1, hh), lambda i, m: (0, m[core])),
                half((1, hh), lambda i, m: (0, 1 - m[core])),
                const(cf.shape),
                const(cos_t.shape),
                const(sin_t.shape),
                const(wd.shape),
                half((hh, width), lambda i, m: (m[core], 0)),
                half((hh, width), lambda i, m: (1 - m[core], 0)),
            ],
            out_specs=[pl.BlockSpec((rb, k), at) for k, _ in saved]
            + [
                pl.BlockSpec((per, 2, w, w), lambda i, m: (m[i], 0, 0, 0)),
                pl.BlockSpec((per, 1, w), lambda i, m: (m[i], 0, 0)),
            ]
            + out_specs,
            scratch_shapes=[pltpu.VMEM((rb, width), BF16), pltpu.VMEM((w, w), F32), pltpu.VMEM((1, w), F32)],
        ),
        out_shape=[sds((rows, k), t) for k, t in saved] + [sds((n, 2, w, w), BF16), sds((n, 1, w), F32)] + out_shape,
        compiler_params=params(),
        cost_estimate=SMALL_COST,
        name="forward",
    )(meta, units, pads, *xs, vec, wqkv, bqkv, wfc, wfc, bfc, bfc, cf, cos_t, sin_t, wd, wp, wp)


def grad_kernel(meta, g_ref, gp, wd, wp_a, wp_b, *refs):
    dao_o, dh_o, sum_o, g_sum_o = refs[-4:]

    @pl.when(pl.program_id(0) == 0)
    def _():
        sum_o[...] = jnp.zeros_like(sum_o)
        g_sum_o[...] = jnp.zeros_like(g_sum_o)

    hh = wp_a.shape[0]
    g = g_ref[...]
    g_sum_o[...] += jnp.sum(g.astype(F32), axis=0, keepdims=True)
    dao_o[...] = mm(g, wd[...], NT).astype(BF16)
    for cols, wp in ((slice(0, hh), wp_a), (slice(hh, 2 * hh), wp_b)):
        dh = (mm(g, wp[...], NT) * gp[:, cols].astype(F32)).astype(BF16)
        dh_o[:, cols] = dh
        sum_o[:, cols] += jnp.sum(dh.astype(F32), axis=0, keepdims=True)


def grad_call(meta, parts, g, gp, wd, wp, deps=()):
    rows, hid = gp.shape
    w, width = wd.shape
    rb = rows // parts
    core = meta.shape[0] - 1
    sds = jax.ShapeDtypeStruct

    def plain(n):
        return pl.BlockSpec((rb, n), lambda i, m: (i, 0))

    return pl.pallas_call(
        grad_kernel,
        grid_spec=pltpu.PrefetchScalarGridSpec(
            num_scalar_prefetch=1,
            grid=(parts,),
            in_specs=[
                plain(width),
                plain(hid),
                const(wd.shape),
                pl.BlockSpec((hid // 2, width), lambda i, m: (m[core], 0), pipeline_mode=pl.Buffered(1)),
                pl.BlockSpec((hid // 2, width), lambda i, m: (1 - m[core], 0), pipeline_mode=pl.Buffered(1)),
            ]
            + unread(deps),
            out_specs=[plain(w), plain(hid), whole((1, hid)), whole((1, width))],
        ),
        out_shape=[sds((rows, w), BF16), sds((rows, hid), BF16), sds((1, hid), F32), sds((1, width), F32)],
        compiler_params=params(),
        cost_estimate=SMALL_COST,
        name="branch_grads",
    )(meta, g, gp, wd, wp, wp, *deps)


def attn_bwd_kernel(
    hd, nseq, meta, units, pads, dao, v_ref, o_ref, rd_ref, fq_ref, fk_ref, rq_ref, rk_ref, s_ref, ks_ref,
    cf, cos_t, sin_t, dct_bd, *refs,
):
    dqkv_o, sum_o, feat_o, after, after_sum, feat = refs[-6:]
    w = v_ref.shape[1]
    heads = w // hd
    step = pl.program_id(0)
    block = pl.num_programs(0) - 1 - step
    per = dao.shape[0] // UNIT

    @pl.when(step == 0)
    def _():
        for ref in (after, after_sum, feat, sum_o):
            ref[...] = jnp.zeros_like(ref)

    head_of_lane, diag, causal = masks(w, hd)
    low_half = lax.broadcasted_iota(jnp.int32, (UNIT, w), 1) % hd < ROT // 2
    ones_bd = jnp.where(diag, 1.0, 0.0).astype(BF16)
    back_hi, back_lo = cf[2], cf[3]
    for i in reversed(range(per)):
        pos, _, last = chunk_place(units, pads, block * per + i, nseq)
        rows = slice(i * UNIT, (i + 1) * UNIT)
        at = pl.ds(pl.multiple_of(pos * UNIT, UNIT), UNIT)
        cosines = lanes(cos_t[at, :], w)
        sines = -lanes(sin_t[at, :], w)
        keep = jnp.where(last == 1, 0.0, 1.0)
        a_old = after[...] * keep
        as_old = after_sum[...] * keep
        fq, fk, v = fq_ref[rows, :], fk_ref[rows, :], v_ref[rows, :]
        fqf, fkf = fq.astype(F32), fk.astype(F32)
        dn = (dao[rows, :].astype(F32) * rd_ref[rows, :]).astype(BF16)
        p_hi, p_lo = split(dn.astype(F32) * o_ref[rows, :])
        dden = -(mm(p_hi, ones_bd) + mm(p_lo, ones_bd))
        dn_s = head_stack(dn, head_of_lane, heads)
        fq_s = head_stack(fq, head_of_lane, heads)
        dden_s = jnp.concatenate(
            [jnp.broadcast_to(dden[:, h * hd : h * hd + 1], (UNIT, UNIT)) for h in range(heads)], axis=0
        )
        da = jnp.where(causal, mm(dn_s, v, NT) + dden_s, 0.0).astype(BF16)
        a = jnp.where(causal, mm(fq_s, fk, NT), 0.0).astype(BF16)
        s_hi, s_lo = s_ref[i, 0], s_ref[i, 1]
        dfq = (
            mm(side_by_side(da, heads), head_stack(fk, head_of_lane, heads))
            + mm(dn, s_hi, NT)
            + mm(dn, s_lo, NT)
            + dden * ks_ref[i]
        )
        a_hi, a_lo = split(a_old)
        dfk = mm(da, fq_s, TN) + mm(v, a_hi, NT) + mm(v, a_lo, NT) + as_old
        dv = mm(a, dn_s, TN) + mm(fk, a_hi)
        after[...] = a_old + jnp.where(diag, mm(fq, dn, TN), 0.0)
        after_sum[...] = as_old + jnp.sum(fqf * dden, axis=0, keepdims=True)
        dsq = (dfq * fqf).astype(BF16)
        dsk = (dfk * fkf).astype(BF16)
        feat[...] += mm(rq_ref[rows, :], dsq, TN) + mm(rk_ref[rows, :], dsk, TN)
        dq = turn(mm(dsq, back_hi) + mm(dsq, back_lo), cosines, sines, low_half)
        dk = turn(mm(dsk, back_hi) + mm(dsk, back_lo), cosines, sines, low_half)
        for j, part in enumerate((dq, dk, dv)):
            part = part.astype(BF16)
            dqkv_o[rows, j * w : (j + 1) * w] = part
            sum_o[:, j * w : (j + 1) * w] += jnp.sum(part.astype(F32), axis=0, keepdims=True)

    @pl.when(block == 0)
    def _():
        turned = lax.dot_general(
            dct_bd[...],
            jnp.where(diag, feat[...], 0.0),
            TN,
            precision=lax.Precision.HIGHEST,
            preferred_element_type=F32,
        )
        total = turned[0:hd, :]
        for h in range(1, heads):
            total = total + turned[h * hd : (h + 1) * hd, :]
        feat_o[...] = total


def attn_bwd_call(meta, units, pads, dao, v, o, rd, fq, fk, rq, rk, s, ks, cf, cos_t, sin_t, dct_bd, hd, parts, deps=()):
    rows, w = v.shape
    rb = rows // parts
    per = rb // UNIT
    smem = pl.BlockSpec(memory_space=pltpu.SMEM)
    sds = jax.ShapeDtypeStruct

    def at(i, m):
        return (m[parts - 1 - i], 0)

    return pl.pallas_call(
        partial(attn_bwd_kernel, hd, units.shape[1]),
        grid_spec=pltpu.PrefetchScalarGridSpec(
            num_scalar_prefetch=1,
            grid=(parts,),
            in_specs=[smem, smem]
            + [pl.BlockSpec((rb, w), at)] * 8
            + [
                pl.BlockSpec((per, 2, w, w), lambda i, m: (m[parts - 1 - i], 0, 0, 0)),
                pl.BlockSpec((per, 1, w), lambda i, m: (m[parts - 1 - i], 0, 0)),
                const(cf.shape),
                const(cos_t.shape),
                const(sin_t.shape),
                const(dct_bd.shape),
            ]
            + unread(deps),
            out_specs=[pl.BlockSpec((rb, 3 * w), at), whole((1, 3 * w)), whole((hd, w))],
            scratch_shapes=[pltpu.VMEM((w, w), F32), pltpu.VMEM((1, w), F32), pltpu.VMEM((w, w), F32)],
        ),
        out_shape=[sds((rows, 3 * w), BF16), sds((1, 3 * w), F32), sds((hd, w), F32)],
        compiler_params=params(),
        cost_estimate=SMALL_COST,
        name="attn_bwd",
    )(meta, units, pads, dao, v, o, rd, fq, fk, rq, rk, s, ks, cf, cos_t, sin_t, dct_bd, *deps)


SMALL_ROWS = 32


def norms_kernel(shards, deps, meta, *refs):
    x_refs = refs[:shards]
    dqkv, dh, vec, wqkv, wfc_a, wfc_b, g_sum, hid_sum, qkv_sum, feat, *rest = refs[shards:]
    small_o, *outs, xbuf = rest[deps:]
    step = pl.program_id(0)
    hh = wfc_a.shape[1]
    slot = step

    @pl.when(step == 0)
    def _():
        small_o[...] = jnp.zeros_like(small_o)
        hid_row = hid_sum[...]
        swapped = jnp.concatenate([hid_row[:, hh:], hid_row[:, :hh]], axis=1)
        hid_row = jnp.where(meta[meta.shape[0] - 1] == 1, swapped, hid_row)
        for at, row in ((4, g_sum[...]), (5, hid_row), (6, qkv_sum[...])):
            small_o[at : at + 1, 0 : row.shape[1]] = row
        deep, w = feat.shape
        each = deep * w // small_o.shape[1]
        for j in range(deep // each):
            small_o[8 : 8 + each, j * w : (j + 1) * w] = feat[j * each : (j + 1) * each, :]

    xh, _ = norm_rows(pick_rows(x_refs, slot, xbuf).astype(F32))
    da = mm(dqkv[...], wqkv[...], NT)
    small_o[0:1, :] += jnp.sum(da * xh, axis=0, keepdims=True)
    small_o[1:2, :] += jnp.sum(da, axis=0, keepdims=True)
    dm = mm(dh[:, :hh], wfc_a[...], NT) + mm(dh[:, hh:], wfc_b[...], NT)
    small_o[2:3, :] += jnp.sum(dm * xh, axis=0, keepdims=True)
    small_o[3:4, :] += jnp.sum(dm, axis=0, keepdims=True)
    put(outs, slot, (da * vec[0:1, :] + dm * vec[2:3, :]).astype(BF16))


def norms_call(meta, parts, xs, dqkv, dh, vec, wqkv, wfc, g_sum, hid_sum, qkv_sum, feat, deps=()):
    rows, hid = dh.shape
    width, cols = wqkv.shape
    hh = hid // 2
    rb = rows // parts
    core = meta.shape[0] - 1

    def at(i, m):
        return (i, 0)

    def to(i, m):
        return (m[i], 0)

    def half(shape, index):
        return pl.BlockSpec(shape, index, pipeline_mode=pl.Buffered(1))

    out_specs, out_shape = put_specs(len(xs) > 1, rb, width, rows, at)
    small = (SMALL_ROWS, width)
    return pl.pallas_call(
        partial(norms_kernel, len(xs), len(deps)),
        grid_spec=pltpu.PrefetchScalarGridSpec(
            num_scalar_prefetch=1,
            grid=(parts,),
            in_specs=rows_specs(xs, rb, at)
            + [
                pl.BlockSpec((rb, cols), at),
                pl.BlockSpec((rb, hid), at),
                const(vec.shape),
                const(wqkv.shape),
                half((width, hh), lambda i, m: (0, m[core])),
                half((width, hh), lambda i, m: (0, 1 - m[core])),
                const(g_sum.shape),
                const(hid_sum.shape),
                const(qkv_sum.shape),
                const(feat.shape),
            ]
            + unread(deps),
            out_specs=[whole(small)] + out_specs,
            scratch_shapes=[pltpu.VMEM((rb, width), BF16)],
        ),
        out_shape=[jax.ShapeDtypeStruct(small, F32)] + out_shape,
        compiler_params=params(),
        cost_estimate=SMALL_COST,
        name="norm_grads",
    )(meta, *xs, dqkv, dh, vec, wqkv, wfc, wfc, g_sum, hid_sum, qkv_sum, feat, *deps)


class Order:
    def __init__(self):
        self.last = None

    def after(self, *arrays):
        if self.last is None:
            return arrays if len(arrays) > 1 else arrays[0]
        self.last, *arrays = lax.optimization_barrier((self.last, *arrays))
        return tuple(arrays) if len(arrays) > 1 else arrays[0]

    def did(self, array):
        self.last = array
        return array


def both(a, b):
    return (a.astype(F32) + b.astype(F32)).astype(a.dtype)


def totals_kernel(count, mid, *refs):
    total = refs[-1]
    rows = refs[0].shape[0]
    for k in range(count):
        own, sent = refs[2 * k], refs[2 * k + 1]

        @pl.when(mid[0] == 1)
        def _():
            total[k * rows : (k + 1) * rows, :] = own[...]

        @pl.when(mid[0] == 0)
        def _():
            total[k * rows : (k + 1) * rows, :] = sent[...]


def totals_call(mid, pairs, deps):
    rows, cols = pairs[0].shape
    count = len(pairs) // 2
    return pl.pallas_call(
        partial(totals_kernel, count),
        in_specs=[pl.BlockSpec(memory_space=pltpu.SMEM)] + [whole((rows, cols))] * len(pairs) + unread(deps),
        out_specs=whole((count * rows, cols)),
        out_shape=jax.ShapeDtypeStruct((count * rows, cols), BF16),
        compiler_params=pltpu.CompilerParams(vmem_limit_bytes=VMEM_BYTES),
        cost_estimate=SMALL_COST,
        name="totals",
    )(mid.astype(jnp.int32).reshape(1), *pairs, *deps)


class Line:
    swap = [(i, i ^ 1) for i in range(8)]
    inward = [(0, 2), (1, 3), (6, 4), (7, 5)]
    inner = [(2, 4), (4, 2), (3, 5), (5, 3)]
    outward = [(2, 0), (3, 1), (4, 6), (5, 7)]

    def __init__(self, order):
        index = lax.axis_index("batch")
        self.order = order
        self.core, z = index % 2, index // 2
        self.mid = (z == 1) | (z == 2)
        self.own, self.sent = {}, {}

    def start(self, k, own, other):
        self.own[k], self.sent[k] = own, lax.ppermute(other, "batch", self.swap)

    def add(self, k, to):
        own, sent = self.order.after(self.own[k], self.sent[k])
        self.own[k] = self.order.did(both(own, sent))
        self.sent[k] = lax.ppermute(self.own[k], "batch", to)

    def go_in(self, k):
        self.add(k, self.inward)

    def meet(self, k):
        self.add(k, self.inner)

    def go_out(self, k):
        self.add(k, self.outward)

    def held(self, *ks):
        return tuple(self.own[k] for k in ks)

    def arrived(self, *ks):
        return tuple(self.sent[k] for k in ks)

    def landed(self, *ks):
        for k in ks:
            self.own[k], self.sent[k] = self.order.after(self.own[k], self.sent[k])

    def end(self, *ks, deps=()):
        self.landed(*ks)
        if deps:
            total = totals_call(self.mid, [a for k in ks for a in (self.own[k], self.sent[k])], deps)
        else:
            total = jnp.concatenate([jnp.where(self.mid, self.own[k], self.sent[k]) for k in ks])
        total = self.order.did(total)
        return total, lax.ppermute(total, "batch", self.swap)

    def end_small(self, k):
        self.landed(k)
        return jnp.where(self.mid, self.own[k], self.sent[k])


def across(a, mask):
    return lax.ppermute(a, "tensor", [(i, i ^ mask) for i in range(4)])


def part_of_batch(a):
    return lax.psum_scatter(a, "batch", scatter_dimension=0, tiled=True)


class TwoStepSum:
    def __init__(self, order, blocks):
        self.order = order
        self.keep_a, send_a, self.keep_b, send_b = blocks
        self.got_a, self.got_b = across(send_a, 1), across(send_b, 2)

    def second(self):
        rb = self.keep_a.shape[0] // 2
        self.got_a, self.got_b = self.order.after(self.got_a, self.got_b)
        a = both(self.keep_a[rb:], self.got_a[rb:])
        b = both(self.keep_b[rb:], self.got_b[rb:])
        a, b = lax.optimization_barrier((a, b))
        self.order.did(b)
        self.last_a, self.last_b = across(a, 2), across(b, 1)

    def result(self):
        rb = self.keep_a.shape[0] // 2
        terms = ((self.keep_a, self.got_a, self.last_a), (self.keep_b, self.got_b, self.last_b))
        return jnp.concatenate([sum(t[:rb].astype(F32) for t in side) for side in terms], axis=1)


def cosine_blocks(hd, heads):
    spatial = np.arange(hd, dtype=np.float64)[:, None]
    frequency = np.arange(hd, dtype=np.float64)[None, :]
    table = np.cos(math.pi * (2.0 * spatial + 1.0) * frequency / (2.0 * hd)) * math.sqrt(2.0 / hd)
    table[:, 0] *= math.sqrt(0.5)
    return np.kron(np.eye(heads), table).astype(np.float32)


def turn_tables(rows, hd):
    half = ROT // 2
    inverse_freq = np.exp(-math.log(10000.0) * 2.0 * np.arange(half) / ROT)
    angles = np.arange(rows)[:, None] * inverse_freq[None, :]
    cosines, sines = np.cos(angles), np.sin(angles)
    rest = np.ones((rows, hd - ROT))
    reps = (1, 128 // hd)
    return (
        np.tile(np.concatenate([cosines, cosines, rest], axis=1), reps).astype(np.float32),
        np.tile(np.concatenate([-sines, sines, 0.0 * rest], axis=1), reps).astype(np.float32),
    )


def column_pick(heads, hd):
    n = 3 * heads * hd
    source = np.arange(n).reshape(heads, 3, hd).transpose(1, 0, 2).reshape(-1)
    pick = np.zeros((n, n), np.float32)
    pick[source, np.arange(n)] = 1.0
    return pick


def body(
    tokens,
    output_grad,
    attn_norm_gain,
    attn_norm_bias,
    mlp_norm_gain,
    mlp_norm_bias,
    qkv_weight,
    qkv_bias,
    dense_weight,
    dense_bias,
    fc_weight,
    fc_bias,
    proj_weight,
    feature_weight,
    seq_units,
    pad_tokens,
):
    rows_dev, width = tokens.shape
    parts = lax.axis_size("tensor")
    n_batch = lax.axis_size("batch")
    rows = rows_dev * parts
    heads, hd, _ = feature_weight.shape
    w = heads * hd
    hid = fc_weight.shape[1]

    square = parts == 4 and n_batch == 8 and hid == width and 4 * w == width
    position = lax.axis_index("tensor")
    order = Order()
    line = Line(order) if square else None
    slots = jnp.arange(parts, dtype=jnp.int32)
    core = jnp.int32(0)
    if square:
        slots = slots ^ position
        core = line.core
        mid = rows_dev // 2
        a1, a2 = across(tokens, 1), across(tokens, 2)
    tail = jnp.stack([jnp.int32(rows_dev // UNIT), core.astype(jnp.int32)])
    meta = jnp.concatenate([slots, tail])
    vec = jnp.stack([attn_norm_gain, attn_norm_bias, mlp_norm_gain, mlp_norm_bias]).astype(F32)
    dct_bd = jnp.asarray(cosine_blocks(hd, heads))
    cos_t, sin_t = (jnp.asarray(t) for t in turn_tables(rows, hd))
    pick = jnp.asarray(column_pick(heads, hd)).astype(BF16)
    bfc = fc_bias.astype(F32).reshape(1, hid)
    wqkv, bqkv, cf_pair = prep_call(
        qkv_weight, qkv_bias.reshape(1, 3 * w), feature_weight.reshape(w, hd), pick, dct_bd, hd, (meta, vec, bfc)
    )
    hh = hid // 2
    dm = width // 2
    g_float = output_grad.astype(F32)
    x_own = tokens.astype(F32)
    if square:
        order.did(wqkv)
        a1, a2 = order.after(a1, a2)
        b1, b2 = across(a1[:mid], 2), across(a2[mid:], 1)
        b1, b2 = order.after(b1, b2)
        g_own, b1, b2 = lax.optimization_barrier((output_grad, b1, b2))
        c1, c2, c3 = across(g_own, 1), across(g_own, 2), across(g_own, 3)
        xs = [tokens, a1, a2, b1, b2]
    else:
        xs = [lax.all_gather(tokens, "tensor", axis=0, tiled=True)]
        g_all = lax.all_gather(output_grad, "tensor", axis=0, tiled=True)
    lna, lnm, act, gp, fq, fk, rq, rk, v, ao, o, rd, s, ks, *outs = forward_call(
        meta, seq_units, pad_tokens, xs, vec, wqkv, bqkv, fc_weight, bfc, cf_pair, cos_t, sin_t,
        dense_weight, proj_weight, hd, parts, rows,
    )
    order.did(ao)
    def residual(total):
        return (x_own + total + dense_bias.astype(F32)).astype(BF16)

    def proj_piece(k, cols):
        g = order.after(g_all)[:, cols]
        line.start(k, mm(act[:, :hh], g, TN).astype(BF16), order.did(mm(act[:, hh:], g, TN).astype(BF16)))

    def fc_piece(k, cols):
        part = order.after(lnm)[:, cols]
        line.start(k, mm(part, dh[:, :hh], TN).astype(BF16), order.did(mm(part, dh[:, hh:], TN).astype(BF16)))

    def rest_piece(k, cols):
        part, cotangent = order.after(lna, dqkv)
        stack = jnp.concatenate([mm(ao, g_all[:, cols], TN), mm(cotangent, part[:, cols], TN)])
        stack = stack.astype(BF16).reshape(2, 2 * w, dm)
        own = lax.dynamic_index_in_dim(stack, line.core, 0, keepdims=False)
        other = lax.dynamic_index_in_dim(stack, 1 - line.core, 0, keepdims=False)
        order.did(other)
        line.start(k, own, other)

    left, right = slice(0, dm), slice(dm, width)
    if square:
        branch = TwoStepSum(order, outs)
        c1, c2, c3 = order.after(c1, c2, c3)
        g_all = order.did(jnp.concatenate([output_grad, c1, c2, c3]))
        proj_piece(0, left)
        proj_piece(1, right)
        line.go_in(0)
        line.go_in(1)
        g_all = order.after(g_all)
    dao, dh, hid_sum, g_sum = grad_call(meta, parts, g_all, gp, dense_weight, proj_weight, line.held(0, 1) if square else ())
    order.did(dao)
    if square:
        branch.second()
        line.meet(0)
        fc_piece(2, left)
        line.go_in(2)
        fc_piece(3, right)
        line.meet(1)
        branch.last_a, branch.last_b = order.after(branch.last_a, branch.last_b)
        output = order.did(residual(branch.result()))
        line.go_out(0)
        line.go_in(3)
    dao = order.after(dao)
    dqkv, qkv_sum, feat = attn_bwd_call(
        meta, seq_units, pad_tokens, dao, v, o, rd, fq, fk, rq, rk, s, ks, cf_pair, cos_t, sin_t, dct_bd, hd, parts,
        (*line.held(0, 1, 2, 3), output) if square else (),
    )
    order.did(dqkv)
    if square:
        line.meet(2)
        line.go_out(1)
        rest_piece(4, left)
        line.landed(0)
        line.meet(3)
        line.go_in(4)
        rest_piece(5, right)
        line.go_in(5)
        line.landed(1)
        line.go_out(2)
    dqkv = order.after(dqkv)
    small, *es = norms_call(meta, parts, xs, dqkv, dh, vec, wqkv, fc_weight, g_sum, hid_sum, qkv_sum, feat,
        (*line.held(2, 3, 4, 5), *line.arrived(0, 1)) if square else ())
    order.did(small)

    def rows_grad(e):
        x_hat, inv_std = norm_rows(x_own)
        mean = jnp.mean(e, axis=-1, keepdims=True)
        return (g_float + inv_std * (e - mean - x_hat * jnp.mean(e * x_hat, axis=-1, keepdims=True))).astype(BF16)

    if square:
        line.meet(4)
        line.go_out(3)
        line.landed(2)
        small = order.after(small)
        line.start(6, small, small)
        es[1], es[3] = order.after(es[1], es[3])
        e_sum = TwoStepSum(order, es)
        line.go_in(6)
        line.meet(5)
        line.go_out(4)
        line.meet(6)
        line.landed(3)
        first = line.end(0, 1, 2, 3)
        second = line.core == 1

        def pieces_of(pair, count):
            own, twin = order.after(*pair)
            low = jnp.where(second, twin, own).reshape(count, 2 * w, dm)
            high = jnp.where(second, own, twin).reshape(count, 2 * w, dm)
            return low, high

        low, high = pieces_of(first, 4)
        proj_grad = order.did(
            jnp.concatenate(
                [jnp.concatenate([low[k], high[k]], axis=0) for k in (0, 1)], axis=1
            ).astype(F32)
        )
        e_sum.second()
        line.go_out(6)
        fc_grad = order.did(
            jnp.concatenate([jnp.concatenate([low[k], high[k]], axis=1) for k in (2, 3)], axis=0).astype(F32)
        )
        line.go_out(5)
        small = order.did(line.end_small(6))
        norm_sums = small[:8]
        hop = across(norm_sums, 1)
        e_sum.last_a, e_sum.last_b = order.after(e_sum.last_a, e_sum.last_b)
        tokens_grad = order.did(rows_grad(e_sum.result()))
        norm_sums = order.did(norm_sums + order.after(hop))
        hop = across(norm_sums, 2)
        last = line.end(4, 5, deps=(proj_grad, fc_grad, tokens_grad, norm_sums))
        norm_sums = norm_sums + order.after(hop)
        low, high = pieces_of(last, 2)
        rest = jnp.concatenate([jnp.concatenate([low[k], high[k]], axis=0) for k in (0, 1)], axis=1)
        dense_grad, qkv_grad = rest[:w].astype(F32), rest[w:]
        hid_sum = small[5]
        pick = jnp.asarray(column_pick(heads, hd)).astype(BF16)
        qkv_grad = lax.dot_general(qkv_grad.astype(BF16), pick, (((0,), (1,)), ((), ())), preferred_element_type=F32)
    else:
        output = residual(lax.psum_scatter(outs[0], "tensor", scatter_dimension=0, tiled=True).astype(F32))
        tokens_grad = rows_grad(lax.psum_scatter(es[0], "tensor", scatter_dimension=0, tiled=True).astype(F32))
        sums = [mm(act, g_all, TN), mm(lnm, dh, TN), mm(ao, g_all, TN), mm(dqkv, lna, TN)]
        sums = lax.psum([a.astype(BF16) for a in sums], "batch")
        proj_grad, fc_grad, dense_grad, qkv_grad = (a.astype(F32) for a in sums)
        small = lax.psum(small, "batch")
        norm_sums = lax.psum(small[:4], "tensor")
        hid_sum = small[5, :hid]
        qkv_grad = qkv_grad.reshape(3, heads, hd, width).transpose(3, 1, 0, 2).reshape(width, 3 * w)
    each = hd * w // width
    feature_grad = small[8 : 8 + each].reshape(each, width // w, heads, hd).transpose(2, 1, 0, 3).reshape(heads, hd, hd)
    qkv_bias_grad = small[6, : 3 * w].reshape(3, heads, hd).transpose(1, 0, 2).reshape(3 * w)

    return (
        output,
        tokens_grad,
        norm_sums[0],
        norm_sums[1],
        norm_sums[2],
        norm_sums[3],
        qkv_grad,
        qkv_bias_grad,
        dense_grad,
        small[4],
        fc_grad,
        hid_sum,
        proj_grad,
        feature_grad,
    )


def solution(mesh):
    rows = P(("batch", "tensor"), None)
    placed = (
        rows,
        rows,
        P(),
        P(),
        P(),
        P(),
        P(None, "tensor"),
        P("tensor"),
        P("tensor", None),
        P(),
        P(None, "tensor"),
        P("tensor"),
        P("tensor", None),
        P("tensor", None, None),
        P("batch", None),
        P("batch", None),
    )
    return jax.shard_map(
        body,
        mesh=mesh,
        in_specs=placed,
        out_specs=(
            rows,
            rows,
            P(),
            P(),
            P(),
            P(),
            P(None, "tensor"),
            P("tensor"),
            P("tensor", None),
            P(),
            P(None, "tensor"),
            P("tensor"),
            P("tensor", None),
            P("tensor", None, None),
        ),
        check_vma=False,
    )
```

```python
from functools import partial
import math

import jax
import jax.numpy as jnp
import numpy as np
from jax import lax
from jax.experimental import pallas as pl
from jax.experimental.pallas import tpu as pltpu
from jax.sharding import PartitionSpec as P

ROT = 16
UNIT = 128
EPS = 1e-05
F32 = jnp.float32
BF16 = jnp.bfloat16
VMEM_BYTES = 54 * 1024 * 1024

NN = (((1,), (0,)), ((), ()))
NT = (((1,), (1,)), ((), ()))
TN = (((0,), (0,)), ((), ()))


def mm(a, b, dims=NN):
    return lax.dot_general(a, b, dims, preferred_element_type=F32)


def split(a):
    hi = a.astype(BF16)
    return hi, (a - hi.astype(F32)).astype(BF16)


HELD_SPACE = pl.ANY
SMALL_COST = pl.CostEstimate(flops=1000, bytes_accessed=1000, transcendentals=0)


def params(grid_rank=1):
    return pltpu.CompilerParams(
        dimension_semantics=("arbitrary",) * grid_rank, vmem_limit_bytes=VMEM_BYTES
    )


def whole(shape):
    return pl.BlockSpec(shape, lambda *_: (0,) * len(shape))


def rows_of(block, width):
    return pl.BlockSpec((block, width), lambda i: (i, 0))


def norm_rows(x):
    mean = jnp.mean(x, axis=-1, keepdims=True)
    cent = x - mean
    inv = lax.rsqrt(jnp.mean(cent * cent, axis=-1, keepdims=True) + EPS)
    return cent * inv, inv


def chunk_place(units, pads, chunk, nseq):
    start = jnp.int32(0)
    pos, real, last = jnp.int32(0), jnp.int32(0), jnp.int32(0)
    for n in range(nseq):
        u = units[0, n]
        inside = (chunk >= start) & (chunk < start + u)
        pos = jnp.where(inside, chunk - start, pos)
        real = jnp.where(inside, (start + u - chunk) * UNIT - pads[0, n], real)
        last = jnp.where(inside, (chunk == start + u - 1).astype(jnp.int32), last)
        start = start + u
    return pos, real, last


def lanes(table, w):
    return jnp.concatenate([table] * (w // table.shape[1]), axis=1) if w > table.shape[1] else table


def turn(a, cosines, sines, low_half):
    w = a.shape[1]
    other = jnp.where(low_half, pltpu.roll(a, w - ROT // 2, 1), pltpu.roll(a, ROT // 2, 1))
    return a * cosines + other * sines


def head_stack(a, head_of_lane, heads):
    zero = jnp.zeros_like(a)
    return jnp.concatenate([jnp.where(head_of_lane == h, a, zero) for h in range(heads)], axis=0)


def side_by_side(a, heads):
    return jnp.concatenate([a[h * UNIT : (h + 1) * UNIT, :] for h in range(heads)], axis=1)


def masks(w, hd):
    lane = lax.broadcasted_iota(jnp.int32, (UNIT, w), 1)
    head_of_lane = lane // hd
    bi = lax.broadcasted_iota(jnp.int32, (w, w), 0) // hd
    bj = lax.broadcasted_iota(jnp.int32, (w, w), 1) // hd
    heads = w // hd
    row = lax.broadcasted_iota(jnp.int32, (heads * UNIT, UNIT), 0) % UNIT
    col = lax.broadcasted_iota(jnp.int32, (heads * UNIT, UNIT), 1)
    return head_of_lane, bi == bj, row >= col


def prep_kernel(hd, wqkv, bqkv, feat, pick, dct_bd, *refs):
    wqkv_o, bqkv_o, cf_o = refs[-3:]
    w = dct_bd.shape[0]
    wqkv_o[...] = mm(wqkv[...], pick[...]).astype(BF16)
    bqkv_o[...] = mm(jnp.broadcast_to(bqkv[...], (8, 3 * w)), pick[...])
    diag = lax.broadcasted_iota(jnp.int32, (w, w), 0) // hd == lax.broadcasted_iota(jnp.int32, (w, w), 1) // hd
    spread = jnp.where(diag, jnp.concatenate([feat[...].astype(F32)] * (w // hd), axis=1), 0.0)
    cf_hi, cf_lo = split(
        lax.dot_general(dct_bd[...], spread, NN, precision=lax.Precision.HIGHEST, preferred_element_type=F32)
    )
    cf_o[0] = cf_hi
    cf_o[1] = cf_lo
    back_hi, back_lo = split(
        lax.dot_general(spread, dct_bd[...], (((0,), (1,)), ((), ())), precision=lax.Precision.HIGHEST, preferred_element_type=F32)
    )
    cf_o[2] = back_hi
    cf_o[3] = back_lo


def prep_call(wqkv, bqkv, feat, pick, dct_bd, hd, deps=()):
    width, cols = wqkv.shape
    w = cols // 3
    sds = jax.ShapeDtypeStruct
    return pl.pallas_call(
        partial(prep_kernel, hd),
        in_specs=[whole(a.shape) for a in (wqkv, bqkv, feat, pick, dct_bd)] + unread(deps),
        out_shape=[sds((width, cols), BF16), sds((8, cols), F32), sds((4, w, w), BF16)],
        compiler_params=pltpu.CompilerParams(vmem_limit_bytes=VMEM_BYTES),
        cost_estimate=SMALL_COST,
        name="prepare",
    )(wqkv, bqkv, feat, pick, dct_bd, *deps)


def gelu_pair(h):
    bell = jnp.exp(h * h * -0.5)
    cdf = 0.5 + 0.5 * lax.erf(h * math.sqrt(0.5))
    return h * cdf, cdf + (h * bell) * (1.0 / math.sqrt(2.0 * math.pi))


def pick_rows(refs, slot, into):
    if len(refs) == 1:
        return refs[0][...]
    rb = into.shape[0]
    for j, ref in enumerate(refs):
        at = slice(0, rb) if j < 3 else slice(0, rb // 2) if j == 3 else slice(rb // 2, rb)

        @pl.when(slot == min(j, 3))
        def _():
            into[at, :] = ref[...]

    return into[...]


def rows_specs(arrays, rb, at):
    if len(arrays) == 1:
        return [pl.BlockSpec((rb, arrays[0].shape[1]), at)]
    return [const(a.shape) for a in arrays]


def put(outs, slot, value):
    if len(outs) == 1:
        outs[0][...] = value
        return
    rb, half = value.shape[0], value.shape[1] // 2
    keep_a, send_a, keep_b, send_b = outs
    for j, (a, b) in enumerate(((keep_a, keep_b), (send_a, keep_b), (keep_a, send_b), (send_a, send_b))):

        @pl.when(slot == j)
        def _():
            a[(j // 2) * rb : (j // 2 + 1) * rb, :] = value[:, :half]
            b[(j % 2) * rb : (j % 2 + 1) * rb, :] = value[:, half:]


def put_specs(apart, rb, width, total, at):
    if apart:
        shape = (2 * rb, width // 2)
        return [whole(shape)] * 4, [jax.ShapeDtypeStruct(shape, BF16)] * 4
    return [pl.BlockSpec((rb, width), at)], [jax.ShapeDtypeStruct((total, width), BF16)]


def unread(arrays):
    return [pl.BlockSpec(memory_space=pl.ANY)] * len(arrays)


def const(shape):
    return pl.BlockSpec(shape, lambda *_: (0,) * len(shape), pipeline_mode=pl.Buffered(1))


def forward_kernel(hd, shards, nseq, meta, units, pads, *refs):
    x_refs = refs[:shards]
    vec, wqkv, bqkv, wfc_a, wfc_b, bfc_a, bfc_b, cf, cos_t, sin_t, wd, wp_a, wp_b = refs[shards : shards + 13]
    lna_o, lnm_o, act_o, gp_o, fq_o, fk_o, rq_o, rk_o, v_o, ao_o, o_o, rd_o, s_o, ks_o = refs[shards + 13 : shards + 27]
    *outs, xbuf, state, ksum = refs[shards + 27 :]
    step = pl.program_id(0)
    slot = meta[step]
    w, hh, per = v_o.shape[1], bfc_a.shape[1], xbuf.shape[0] // UNIT
    heads = w // hd

    @pl.when(step == 0)
    def _():
        state[...] = jnp.zeros_like(state)
        ksum[...] = jnp.zeros_like(ksum)

    xh, _ = norm_rows(pick_rows(x_refs, slot, xbuf).astype(F32))
    lna = (xh * vec[0:1, :] + vec[1:2, :]).astype(BF16)
    lnm = (xh * vec[2:3, :] + vec[3:4, :]).astype(BF16)
    lna_o[...] = lna
    lnm_o[...] = lnm
    qkv = mm(lna, wqkv[...]) + bqkv[0:1, :]
    v_o[...] = qkv[:, 2 * w :].astype(BF16)
    for cols, wfc, bfc in ((slice(0, hh), wfc_a, bfc_a), (slice(hh, 2 * hh), wfc_b, bfc_b)):
        act, slope = gelu_pair(mm(lnm, wfc[...]) + bfc[...])
        act_o[:, cols] = act.astype(BF16)
        gp_o[:, cols] = slope.astype(BF16)

    head_of_lane, diag, causal = masks(w, hd)
    low_half = lax.broadcasted_iota(jnp.int32, (UNIT, w), 1) % hd < ROT // 2
    row_id = lax.broadcasted_iota(jnp.int32, (UNIT, 1), 0)
    ones_bd = jnp.where(diag, 1.0, 0.0).astype(BF16)
    head_ones = head_stack(jnp.ones((UNIT, w), BF16), head_of_lane, heads)
    cf_hi, cf_lo = cf[0], cf[1]
    for i in range(per):
        pos, real, _ = chunk_place(units, pads, step * per + i, nseq)
        at = pl.ds(pl.multiple_of(pos * UNIT, UNIT), UNIT)
        cosines = lanes(cos_t[at, :], w)
        sines = lanes(sin_t[at, :], w)
        rows = slice(i * UNIT, (i + 1) * UNIT)
        rq = turn(qkv[rows, 0:w], cosines, sines, low_half)
        rk = turn(qkv[rows, w : 2 * w], cosines, sines, low_half)
        qh, ql = split(rq)
        kh, kl = split(rk)
        rq_o[rows, :] = qh
        rk_o[rows, :] = kh
        high, low = jnp.concatenate([qh, kh]), jnp.concatenate([ql, kl])
        grown = jnp.exp(mm(high, cf_hi) + mm(low, cf_hi) + mm(high, cf_lo))
        fq, ek = grown[:UNIT].astype(BF16), grown[UNIT:]
        fk = jnp.where(row_id < real, ek, 0.0).astype(BF16)
        fq_o[rows, :] = fq
        fk_o[rows, :] = fk
        v = v_o[rows, :]
        keep = jnp.where(pos == 0, 0.0, 1.0)
        s_old = state[...] * keep
        k_old = ksum[...] * keep
        s_hi, s_lo = split(s_old)
        s_o[i, 0] = s_hi
        s_o[i, 1] = s_lo
        ks_o[i] = k_old
        scores = jnp.where(causal, mm(head_stack(fq, head_of_lane, heads), fk, NT), 0.0).astype(BF16)
        wide = side_by_side(scores, heads)
        num = mm(wide, head_stack(v, head_of_lane, heads)) + mm(fq, s_hi) + mm(fq, s_lo)
        p_hi, p_lo = split(fq.astype(F32) * k_old)
        den = mm(wide, head_ones) + mm(p_hi, ones_bd) + mm(p_lo, ones_bd)
        rden = 1.0 / den
        o = num * rden
        o_o[rows, :] = o
        rd_o[rows, :] = rden
        ao_o[rows, :] = o.astype(BF16)
        state[...] = s_old + jnp.where(diag, mm(fk, v, TN), 0.0)
        ksum[...] = k_old + jnp.sum(fk.astype(F32), axis=0, keepdims=True)

    out = mm(ao_o[...], wd[...]) + mm(act_o[:, :hh], wp_a[...]) + mm(act_o[:, hh:], wp_b[...])
    put(outs, slot, out.astype(BF16))


def forward_call(meta, units, pads, xs, vec, wqkv, bqkv, wfc, bfc, cf, cos_t, sin_t, wd, wp, hd, parts, rows):
    width, cols = wqkv.shape
    w, hid = cols // 3, wfc.shape[1]
    hh = hid // 2
    rb = rows // parts
    per, n = rb // UNIT, rows // UNIT
    core = meta.shape[0] - 1
    smem = pl.BlockSpec(memory_space=pltpu.SMEM)
    sds = jax.ShapeDtypeStruct

    def at(i, m):
        return (m[i], 0)

    def half(shape, index):
        return pl.BlockSpec(shape, index, pipeline_mode=pl.Buffered(1))

    out_specs, out_shape = put_specs(len(xs) > 1, rb, width, rows, at)
    saved = [(width, BF16)] * 2 + [(hid, BF16)] * 2 + [(w, BF16)] * 6 + [(w, F32)] * 2
    return pl.pallas_call(
        partial(forward_kernel, hd, len(xs), units.shape[1]),
        grid_spec=pltpu.PrefetchScalarGridSpec(
            num_scalar_prefetch=1,
            grid=(parts,),
            in_specs=[smem, smem]
            + rows_specs(xs, rb, at)
            + [
                const(vec.shape),
                const(wqkv.shape),
                const(bqkv.shape),
                half((width, hh), lambda i, m: (0, m[core])),
                half((width, hh), lambda i, m: (0, 1 - m[core])),
                half((1, hh), lambda i, m: (0, m[core])),
                half((1, hh), lambda i, m: (0, 1 - m[core])),
                const(cf.shape),
                const(cos_t.shape),
                const(sin_t.shape),
                const(wd.shape),
                half((hh, width), lambda i, m: (m[core], 0)),
                half((hh, width), lambda i, m: (1 - m[core], 0)),
            ],
            out_specs=[pl.BlockSpec((rb, k), at) for k, _ in saved]
            + [
                pl.BlockSpec((per, 2, w, w), lambda i, m: (m[i], 0, 0, 0)),
                pl.BlockSpec((per, 1, w), lambda i, m: (m[i], 0, 0)),
            ]
            + out_specs,
            scratch_shapes=[pltpu.VMEM((rb, width), BF16), pltpu.VMEM((w, w), F32), pltpu.VMEM((1, w), F32)],
        ),
        out_shape=[sds((rows, k), t) for k, t in saved] + [sds((n, 2, w, w), BF16), sds((n, 1, w), F32)] + out_shape,
        compiler_params=params(),
        cost_estimate=SMALL_COST,
        name="forward",
    )(meta, units, pads, *xs, vec, wqkv, bqkv, wfc, wfc, bfc, bfc, cf, cos_t, sin_t, wd, wp, wp)


def grad_kernel(meta, g_ref, gp, wd, wp_a, wp_b, *refs):
    dao_o, dh_o, sum_o, g_sum_o = refs[-4:]

    @pl.when(pl.program_id(0) == 0)
    def _():
        sum_o[...] = jnp.zeros_like(sum_o)
        g_sum_o[...] = jnp.zeros_like(g_sum_o)

    hh = wp_a.shape[0]
    g = g_ref[...]
    g_sum_o[...] += jnp.sum(g.astype(F32), axis=0, keepdims=True)
    dao_o[...] = mm(g, wd[...], NT).astype(BF16)
    for cols, wp in ((slice(0, hh), wp_a), (slice(hh, 2 * hh), wp_b)):
        dh = (mm(g, wp[...], NT) * gp[:, cols].astype(F32)).astype(BF16)
        dh_o[:, cols] = dh
        sum_o[:, cols] += jnp.sum(dh.astype(F32), axis=0, keepdims=True)


def grad_call(meta, parts, g, gp, wd, wp, deps=()):
    rows, hid = gp.shape
    w, width = wd.shape
    rb = rows // parts
    core = meta.shape[0] - 1
    sds = jax.ShapeDtypeStruct

    def plain(n):
        return pl.BlockSpec((rb, n), lambda i, m: (i, 0))

    return pl.pallas_call(
        grad_kernel,
        grid_spec=pltpu.PrefetchScalarGridSpec(
            num_scalar_prefetch=1,
            grid=(parts,),
            in_specs=[
                plain(width),
                plain(hid),
                const(wd.shape),
                pl.BlockSpec((hid // 2, width), lambda i, m: (m[core], 0), pipeline_mode=pl.Buffered(1)),
                pl.BlockSpec((hid // 2, width), lambda i, m: (1 - m[core], 0), pipeline_mode=pl.Buffered(1)),
            ]
            + unread(deps),
            out_specs=[plain(w), plain(hid), whole((1, hid)), whole((1, width))],
        ),
        out_shape=[sds((rows, w), BF16), sds((rows, hid), BF16), sds((1, hid), F32), sds((1, width), F32)],
        compiler_params=params(),
        cost_estimate=SMALL_COST,
        name="branch_grads",
    )(meta, g, gp, wd, wp, wp, *deps)


def attn_bwd_kernel(
    hd, nseq, meta, units, pads, dao, v_ref, o_ref, rd_ref, fq_ref, fk_ref, rq_ref, rk_ref, s_ref, ks_ref,
    cf, cos_t, sin_t, dct_bd, *refs,
):
    dqkv_o, sum_o, feat_o, after, after_sum, feat = refs[-6:]
    w = v_ref.shape[1]
    heads = w // hd
    step = pl.program_id(0)
    block = pl.num_programs(0) - 1 - step
    per = dao.shape[0] // UNIT

    @pl.when(step == 0)
    def _():
        for ref in (after, after_sum, feat, sum_o):
            ref[...] = jnp.zeros_like(ref)

    head_of_lane, diag, causal = masks(w, hd)
    low_half = lax.broadcasted_iota(jnp.int32, (UNIT, w), 1) % hd < ROT // 2
    ones_bd = jnp.where(diag, 1.0, 0.0).astype(BF16)
    back_hi, back_lo = cf[2], cf[3]
    for i in reversed(range(per)):
        pos, _, last = chunk_place(units, pads, block * per + i, nseq)
        rows = slice(i * UNIT, (i + 1) * UNIT)
        at = pl.ds(pl.multiple_of(pos * UNIT, UNIT), UNIT)
        cosines = lanes(cos_t[at, :], w)
        sines = -lanes(sin_t[at, :], w)
        keep = jnp.where(last == 1, 0.0, 1.0)
        a_old = after[...] * keep
        as_old = after_sum[...] * keep
        fq, fk, v = fq_ref[rows, :], fk_ref[rows, :], v_ref[rows, :]
        fqf, fkf = fq.astype(F32), fk.astype(F32)
        dn = (dao[rows, :].astype(F32) * rd_ref[rows, :]).astype(BF16)
        p_hi, p_lo = split(dn.astype(F32) * o_ref[rows, :])
        dden = -(mm(p_hi, ones_bd) + mm(p_lo, ones_bd))
        dn_s = head_stack(dn, head_of_lane, heads)
        fq_s = head_stack(fq, head_of_lane, heads)
        dden_s = jnp.concatenate(
            [jnp.broadcast_to(dden[:, h * hd : h * hd + 1], (UNIT, UNIT)) for h in range(heads)], axis=0
        )
        da = jnp.where(causal, mm(dn_s, v, NT) + dden_s, 0.0).astype(BF16)
        a = jnp.where(causal, mm(fq_s, fk, NT), 0.0).astype(BF16)
        s_hi, s_lo = s_ref[i, 0], s_ref[i, 1]
        dfq = (
            mm(side_by_side(da, heads), head_stack(fk, head_of_lane, heads))
            + mm(dn, s_hi, NT)
            + mm(dn, s_lo, NT)
            + dden * ks_ref[i]
        )
        a_hi, a_lo = split(a_old)
        dfk = mm(da, fq_s, TN) + mm(v, a_hi, NT) + mm(v, a_lo, NT) + as_old
        dv = mm(a, dn_s, TN) + mm(fk, a_hi)
        after[...] = a_old + jnp.where(diag, mm(fq, dn, TN), 0.0)
        after_sum[...] = as_old + jnp.sum(fqf * dden, axis=0, keepdims=True)
        dsq = (dfq * fqf).astype(BF16)
        dsk = (dfk * fkf).astype(BF16)
        feat[...] += mm(rq_ref[rows, :], dsq, TN) + mm(rk_ref[rows, :], dsk, TN)
        pair = jnp.concatenate([dsq, dsk])
        turned = mm(pair, back_hi) + mm(pair, back_lo)
        dq = turn(turned[:UNIT], cosines, sines, low_half)
        dk = turn(turned[UNIT:], cosines, sines, low_half)
        for j, part in enumerate((dq, dk, dv)):
            part = part.astype(BF16)
            dqkv_o[rows, j * w : (j + 1) * w] = part
            sum_o[:, j * w : (j + 1) * w] += jnp.sum(part.astype(F32), axis=0, keepdims=True)

    @pl.when(block == 0)
    def _():
        turned = lax.dot_general(
            dct_bd[...],
            jnp.where(diag, feat[...], 0.0),
            TN,
            precision=lax.Precision.HIGHEST,
            preferred_element_type=F32,
        )
        total = turned[0:hd, :]
        for h in range(1, heads):
            total = total + turned[h * hd : (h + 1) * hd, :]
        feat_o[...] = total


def attn_bwd_call(meta, units, pads, dao, v, o, rd, fq, fk, rq, rk, s, ks, cf, cos_t, sin_t, dct_bd, hd, parts, deps=()):
    rows, w = v.shape
    rb = rows // parts
    per = rb // UNIT
    smem = pl.BlockSpec(memory_space=pltpu.SMEM)
    sds = jax.ShapeDtypeStruct

    def at(i, m):
        return (m[parts - 1 - i], 0)

    return pl.pallas_call(
        partial(attn_bwd_kernel, hd, units.shape[1]),
        grid_spec=pltpu.PrefetchScalarGridSpec(
            num_scalar_prefetch=1,
            grid=(parts,),
            in_specs=[smem, smem]
            + [pl.BlockSpec((rb, w), at)] * 8
            + [
                pl.BlockSpec((per, 2, w, w), lambda i, m: (m[parts - 1 - i], 0, 0, 0)),
                pl.BlockSpec((per, 1, w), lambda i, m: (m[parts - 1 - i], 0, 0)),
                const(cf.shape),
                const(cos_t.shape),
                const(sin_t.shape),
                const(dct_bd.shape),
            ]
            + unread(deps),
            out_specs=[pl.BlockSpec((rb, 3 * w), at), whole((1, 3 * w)), whole((hd, w))],
            scratch_shapes=[pltpu.VMEM((w, w), F32), pltpu.VMEM((1, w), F32), pltpu.VMEM((w, w), F32)],
        ),
        out_shape=[sds((rows, 3 * w), BF16), sds((1, 3 * w), F32), sds((hd, w), F32)],
        compiler_params=params(),
        cost_estimate=SMALL_COST,
        name="attn_bwd",
    )(meta, units, pads, dao, v, o, rd, fq, fk, rq, rk, s, ks, cf, cos_t, sin_t, dct_bd, *deps)


SMALL_ROWS = 32


def norms_kernel(shards, deps, meta, *refs):
    x_refs = refs[:shards]
    dqkv, dh, vec, wqkv, wfc_a, wfc_b, g_sum, hid_sum, qkv_sum, feat, *rest = refs[shards:]
    small_o, *outs, xbuf = rest[deps:]
    step = pl.program_id(0)
    hh = wfc_a.shape[1]
    slot = step

    @pl.when(step == 0)
    def _():
        small_o[...] = jnp.zeros_like(small_o)
        hid_row = hid_sum[...]
        swapped = jnp.concatenate([hid_row[:, hh:], hid_row[:, :hh]], axis=1)
        hid_row = jnp.where(meta[meta.shape[0] - 1] == 1, swapped, hid_row)
        for at, row in ((4, g_sum[...]), (5, hid_row), (6, qkv_sum[...])):
            small_o[at : at + 1, 0 : row.shape[1]] = row
        deep, w = feat.shape
        each = deep * w // small_o.shape[1]
        for j in range(deep // each):
            small_o[8 : 8 + each, j * w : (j + 1) * w] = feat[j * each : (j + 1) * each, :]

    xh, _ = norm_rows(pick_rows(x_refs, slot, xbuf).astype(F32))
    da = mm(dqkv[...], wqkv[...], NT)
    small_o[0:1, :] += jnp.sum(da * xh, axis=0, keepdims=True)
    small_o[1:2, :] += jnp.sum(da, axis=0, keepdims=True)
    dm = mm(dh[:, :hh], wfc_a[...], NT) + mm(dh[:, hh:], wfc_b[...], NT)
    small_o[2:3, :] += jnp.sum(dm * xh, axis=0, keepdims=True)
    small_o[3:4, :] += jnp.sum(dm, axis=0, keepdims=True)
    put(outs, slot, (da * vec[0:1, :] + dm * vec[2:3, :]).astype(BF16))


def norms_call(meta, parts, xs, dqkv, dh, vec, wqkv, wfc, g_sum, hid_sum, qkv_sum, feat, deps=()):
    rows, hid = dh.shape
    width, cols = wqkv.shape
    hh = hid // 2
    rb = rows // parts
    core = meta.shape[0] - 1

    def at(i, m):
        return (i, 0)

    def to(i, m):
        return (m[i], 0)

    def half(shape, index):
        return pl.BlockSpec(shape, index, pipeline_mode=pl.Buffered(1))

    out_specs, out_shape = put_specs(len(xs) > 1, rb, width, rows, at)
    small = (SMALL_ROWS, width)
    return pl.pallas_call(
        partial(norms_kernel, len(xs), len(deps)),
        grid_spec=pltpu.PrefetchScalarGridSpec(
            num_scalar_prefetch=1,
            grid=(parts,),
            in_specs=rows_specs(xs, rb, at)
            + [
                pl.BlockSpec((rb, cols), at),
                pl.BlockSpec((rb, hid), at),
                const(vec.shape),
                const(wqkv.shape),
                half((width, hh), lambda i, m: (0, m[core])),
                half((width, hh), lambda i, m: (0, 1 - m[core])),
                const(g_sum.shape),
                const(hid_sum.shape),
                const(qkv_sum.shape),
                const(feat.shape),
            ]
            + unread(deps),
            out_specs=[whole(small)] + out_specs,
            scratch_shapes=[pltpu.VMEM((rb, width), BF16)],
        ),
        out_shape=[jax.ShapeDtypeStruct(small, F32)] + out_shape,
        compiler_params=params(),
        cost_estimate=SMALL_COST,
        name="norm_grads",
    )(meta, *xs, dqkv, dh, vec, wqkv, wfc, wfc, g_sum, hid_sum, qkv_sum, feat, *deps)


class Order:
    def __init__(self):
        self.last = None

    def after(self, *arrays):
        if self.last is None:
            return arrays if len(arrays) > 1 else arrays[0]
        self.last, *arrays = lax.optimization_barrier((self.last, *arrays))
        return tuple(arrays) if len(arrays) > 1 else arrays[0]

    def did(self, array):
        self.last = array
        return array


def both(a, b):
    return (a.astype(F32) + b.astype(F32)).astype(a.dtype)


def totals_kernel(count, mid, *refs):
    total = refs[-1]
    rows = refs[0].shape[0]
    for k in range(count):
        own, sent = refs[2 * k], refs[2 * k + 1]

        @pl.when(mid[0] == 1)
        def _():
            total[k * rows : (k + 1) * rows, :] = own[...]

        @pl.when(mid[0] == 0)
        def _():
            total[k * rows : (k + 1) * rows, :] = sent[...]


def totals_call(mid, pairs, deps):
    rows, cols = pairs[0].shape
    count = len(pairs) // 2
    return pl.pallas_call(
        partial(totals_kernel, count),
        in_specs=[pl.BlockSpec(memory_space=pltpu.SMEM)] + [whole((rows, cols))] * len(pairs) + unread(deps),
        out_specs=whole((count * rows, cols)),
        out_shape=jax.ShapeDtypeStruct((count * rows, cols), BF16),
        compiler_params=pltpu.CompilerParams(vmem_limit_bytes=VMEM_BYTES),
        cost_estimate=SMALL_COST,
        name="totals",
    )(mid.astype(jnp.int32).reshape(1), *pairs, *deps)


class Line:
    swap = [(i, i ^ 1) for i in range(8)]
    inward = [(0, 2), (1, 3), (6, 4), (7, 5)]
    inner = [(2, 4), (4, 2), (3, 5), (5, 3)]
    outward = [(2, 0), (3, 1), (4, 6), (5, 7)]

    def __init__(self, order):
        index = lax.axis_index("batch")
        self.order = order
        self.core, z = index % 2, index // 2
        self.mid = (z == 1) | (z == 2)
        self.own, self.sent = {}, {}

    def start(self, k, own, other):
        self.own[k], self.sent[k] = own, lax.ppermute(other, "batch", self.swap)

    def add(self, k, to):
        own, sent = self.order.after(self.own[k], self.sent[k])
        self.own[k] = self.order.did(both(own, sent))
        self.sent[k] = lax.ppermute(self.own[k], "batch", to)

    def go_in(self, k):
        self.add(k, self.inward)

    def meet(self, k):
        self.add(k, self.inner)

    def go_out(self, k):
        self.add(k, self.outward)

    def held(self, *ks):
        return tuple(self.own[k] for k in ks)

    def arrived(self, *ks):
        return tuple(self.sent[k] for k in ks)

    def landed(self, *ks):
        for k in ks:
            self.own[k], self.sent[k] = self.order.after(self.own[k], self.sent[k])

    def end(self, *ks, deps=()):
        self.landed(*ks)
        if deps:
            total = totals_call(self.mid, [a for k in ks for a in (self.own[k], self.sent[k])], deps)
        else:
            total = jnp.concatenate([jnp.where(self.mid, self.own[k], self.sent[k]) for k in ks])
        total = self.order.did(total)
        return total, lax.ppermute(total, "batch", self.swap)

    def end_small(self, k):
        self.landed(k)
        return jnp.where(self.mid, self.own[k], self.sent[k])


def across(a, mask):
    return lax.ppermute(a, "tensor", [(i, i ^ mask) for i in range(4)])


def part_of_batch(a):
    return lax.psum_scatter(a, "batch", scatter_dimension=0, tiled=True)


class TwoStepSum:
    def __init__(self, order, blocks):
        self.order = order
        self.keep_a, send_a, self.keep_b, send_b = blocks
        self.got_a, self.got_b = across(send_a, 1), across(send_b, 2)

    def second(self):
        rb = self.keep_a.shape[0] // 2
        self.got_a, self.got_b = self.order.after(self.got_a, self.got_b)
        a = both(self.keep_a[rb:], self.got_a[rb:])
        b = both(self.keep_b[rb:], self.got_b[rb:])
        a, b = lax.optimization_barrier((a, b))
        self.order.did(b)
        self.last_a, self.last_b = across(a, 2), across(b, 1)

    def result(self):
        rb = self.keep_a.shape[0] // 2
        terms = ((self.keep_a, self.got_a, self.last_a), (self.keep_b, self.got_b, self.last_b))
        return jnp.concatenate([sum(t[:rb].astype(F32) for t in side) for side in terms], axis=1)


def cosine_blocks(hd, heads):
    spatial = np.arange(hd, dtype=np.float64)[:, None]
    frequency = np.arange(hd, dtype=np.float64)[None, :]
    table = np.cos(math.pi * (2.0 * spatial + 1.0) * frequency / (2.0 * hd)) * math.sqrt(2.0 / hd)
    table[:, 0] *= math.sqrt(0.5)
    return np.kron(np.eye(heads), table).astype(np.float32)


def turn_tables(rows, hd):
    half = ROT // 2
    inverse_freq = np.exp(-math.log(10000.0) * 2.0 * np.arange(half) / ROT)
    angles = np.arange(rows)[:, None] * inverse_freq[None, :]
    cosines, sines = np.cos(angles), np.sin(angles)
    rest = np.ones((rows, hd - ROT))
    reps = (1, 128 // hd)
    return (
        np.tile(np.concatenate([cosines, cosines, rest], axis=1), reps).astype(np.float32),
        np.tile(np.concatenate([-sines, sines, 0.0 * rest], axis=1), reps).astype(np.float32),
    )


def column_pick(heads, hd):
    n = 3 * heads * hd
    source = np.arange(n).reshape(heads, 3, hd).transpose(1, 0, 2).reshape(-1)
    pick = np.zeros((n, n), np.float32)
    pick[source, np.arange(n)] = 1.0
    return pick


def body(
    tokens,
    output_grad,
    attn_norm_gain,
    attn_norm_bias,
    mlp_norm_gain,
    mlp_norm_bias,
    qkv_weight,
    qkv_bias,
    dense_weight,
    dense_bias,
    fc_weight,
    fc_bias,
    proj_weight,
    feature_weight,
    seq_units,
    pad_tokens,
):
    rows_dev, width = tokens.shape
    parts = lax.axis_size("tensor")
    n_batch = lax.axis_size("batch")
    rows = rows_dev * parts
    heads, hd, _ = feature_weight.shape
    w = heads * hd
    hid = fc_weight.shape[1]

    square = parts == 4 and n_batch == 8 and hid == width and 4 * w == width
    position = lax.axis_index("tensor")
    order = Order()
    line = Line(order) if square else None
    slots = jnp.arange(parts, dtype=jnp.int32)
    core = jnp.int32(0)
    if square:
        slots = slots ^ position
        core = line.core
        mid = rows_dev // 2
        a1, a2 = across(tokens, 1), across(tokens, 2)
    tail = jnp.stack([jnp.int32(rows_dev // UNIT), core.astype(jnp.int32)])
    meta = jnp.concatenate([slots, tail])
    vec = jnp.stack([attn_norm_gain, attn_norm_bias, mlp_norm_gain, mlp_norm_bias]).astype(F32)
    dct_bd = jnp.asarray(cosine_blocks(hd, heads))
    cos_t, sin_t = (jnp.asarray(t) for t in turn_tables(rows, hd))
    pick = jnp.asarray(column_pick(heads, hd)).astype(BF16)
    bfc = fc_bias.astype(F32).reshape(1, hid)
    wqkv, bqkv, cf_pair = prep_call(
        qkv_weight, qkv_bias.reshape(1, 3 * w), feature_weight.reshape(w, hd), pick, dct_bd, hd, (meta, vec, bfc)
    )
    hh = hid // 2
    dm = width // 2
    g_float = output_grad.astype(F32)
    x_own = tokens.astype(F32)
    if square:
        order.did(wqkv)
        a1, a2 = order.after(a1, a2)
        b1, b2 = across(a1[:mid], 2), across(a2[mid:], 1)
        b1, b2 = order.after(b1, b2)
        g_own, b1, b2 = lax.optimization_barrier((output_grad, b1, b2))
        c1, c2, c3 = across(g_own, 1), across(g_own, 2), across(g_own, 3)
        xs = [tokens, a1, a2, b1, b2]
    else:
        xs = [lax.all_gather(tokens, "tensor", axis=0, tiled=True)]
        g_all = lax.all_gather(output_grad, "tensor", axis=0, tiled=True)
    lna, lnm, act, gp, fq, fk, rq, rk, v, ao, o, rd, s, ks, *outs = forward_call(
        meta, seq_units, pad_tokens, xs, vec, wqkv, bqkv, fc_weight, bfc, cf_pair, cos_t, sin_t,
        dense_weight, proj_weight, hd, parts, rows,
    )
    order.did(ao)
    def residual(total):
        return (x_own + total + dense_bias.astype(F32)).astype(BF16)

    def proj_piece(k, cols):
        g = order.after(g_all)[:, cols]
        line.start(k, mm(act[:, :hh], g, TN).astype(BF16), order.did(mm(act[:, hh:], g, TN).astype(BF16)))

    def fc_piece(k, cols):
        part = order.after(lnm)[:, cols]
        line.start(k, mm(part, dh[:, :hh], TN).astype(BF16), order.did(mm(part, dh[:, hh:], TN).astype(BF16)))

    def rest_piece(k, cols):
        part, cotangent = order.after(lna, dqkv)
        stack = jnp.concatenate([mm(ao, g_all[:, cols], TN), mm(cotangent, part[:, cols], TN)])
        stack = stack.astype(BF16).reshape(2, 2 * w, dm)
        own = lax.dynamic_index_in_dim(stack, line.core, 0, keepdims=False)
        other = lax.dynamic_index_in_dim(stack, 1 - line.core, 0, keepdims=False)
        order.did(other)
        line.start(k, own, other)

    left, right = slice(0, dm), slice(dm, width)
    if square:
        branch = TwoStepSum(order, outs)
        c1, c2, c3 = order.after(c1, c2, c3)
        g_all = order.did(jnp.concatenate([output_grad, c1, c2, c3]))
        proj_piece(0, left)
        proj_piece(1, right)
        line.go_in(0)
        line.go_in(1)
        g_all = order.after(g_all)
    dao, dh, hid_sum, g_sum = grad_call(meta, parts, g_all, gp, dense_weight, proj_weight, line.held(0, 1) if square else ())
    order.did(dao)
    if square:
        branch.second()
        line.meet(0)
        fc_piece(2, left)
        line.go_in(2)
        fc_piece(3, right)
        line.meet(1)
        branch.last_a, branch.last_b = order.after(branch.last_a, branch.last_b)
        output = order.did(residual(branch.result()))
        line.go_out(0)
        line.go_in(3)
    dao = order.after(dao)
    dqkv, qkv_sum, feat = attn_bwd_call(
        meta, seq_units, pad_tokens, dao, v, o, rd, fq, fk, rq, rk, s, ks, cf_pair, cos_t, sin_t, dct_bd, hd, parts,
        (*line.held(0, 1, 2, 3), output) if square else (),
    )
    order.did(dqkv)
    if square:
        line.meet(2)
        line.go_out(1)
        rest_piece(4, left)
        line.landed(0)
        line.meet(3)
        line.go_in(4)
        rest_piece(5, right)
        line.go_in(5)
        line.landed(1)
        line.go_out(2)
    dqkv = order.after(dqkv)
    small, *es = norms_call(meta, parts, xs, dqkv, dh, vec, wqkv, fc_weight, g_sum, hid_sum, qkv_sum, feat,
        (*line.held(2, 3, 4, 5), *line.arrived(0, 1)) if square else ())
    order.did(small)

    def rows_grad(e):
        x_hat, inv_std = norm_rows(x_own)
        mean = jnp.mean(e, axis=-1, keepdims=True)
        return (g_float + inv_std * (e - mean - x_hat * jnp.mean(e * x_hat, axis=-1, keepdims=True))).astype(BF16)

    if square:
        line.meet(4)
        line.go_out(3)
        line.landed(2)
        small = order.after(small)
        line.start(6, small, small)
        es[1], es[3] = order.after(es[1], es[3])
        e_sum = TwoStepSum(order, es)
        line.go_in(6)
        line.meet(5)
        line.go_out(4)
        line.meet(6)
        line.landed(3)
        first = line.end(0, 1, 2, 3)
        second = line.core == 1

        def pieces_of(pair, count):
            own, twin = order.after(*pair)
            low = jnp.where(second, twin, own).reshape(count, 2 * w, dm)
            high = jnp.where(second, own, twin).reshape(count, 2 * w, dm)
            return low, high

        low, high = pieces_of(first, 4)
        proj_grad = order.did(
            jnp.concatenate(
                [jnp.concatenate([low[k], high[k]], axis=0) for k in (0, 1)], axis=1
            ).astype(F32)
        )
        e_sum.second()
        line.go_out(6)
        fc_grad = order.did(
            jnp.concatenate([jnp.concatenate([low[k], high[k]], axis=1) for k in (2, 3)], axis=0).astype(F32)
        )
        line.go_out(5)
        small = order.did(line.end_small(6))
        norm_sums = small[:8]
        hop = across(norm_sums, 1)
        e_sum.last_a, e_sum.last_b = order.after(e_sum.last_a, e_sum.last_b)
        tokens_grad = order.did(rows_grad(e_sum.result()))
        norm_sums = order.did(norm_sums + order.after(hop))
        hop = across(norm_sums, 2)
        last = line.end(4, 5, deps=(proj_grad, fc_grad, tokens_grad, norm_sums))
        norm_sums = norm_sums + order.after(hop)
        low, high = pieces_of(last, 2)
        rest = jnp.concatenate([jnp.concatenate([low[k], high[k]], axis=0) for k in (0, 1)], axis=1)
        dense_grad, qkv_grad = rest[:w].astype(F32), rest[w:]
        hid_sum = small[5]
        pick = jnp.asarray(column_pick(heads, hd)).astype(BF16)
        qkv_grad = lax.dot_general(qkv_grad.astype(BF16), pick, (((0,), (1,)), ((), ())), preferred_element_type=F32)
    else:
        output = residual(lax.psum_scatter(outs[0], "tensor", scatter_dimension=0, tiled=True).astype(F32))
        tokens_grad = rows_grad(lax.psum_scatter(es[0], "tensor", scatter_dimension=0, tiled=True).astype(F32))
        sums = [mm(act, g_all, TN), mm(lnm, dh, TN), mm(ao, g_all, TN), mm(dqkv, lna, TN)]
        sums = lax.psum([a.astype(BF16) for a in sums], "batch")
        proj_grad, fc_grad, dense_grad, qkv_grad = (a.astype(F32) for a in sums)
        small = lax.psum(small, "batch")
        norm_sums = lax.psum(small[:4], "tensor")
        hid_sum = small[5, :hid]
        qkv_grad = qkv_grad.reshape(3, heads, hd, width).transpose(3, 1, 0, 2).reshape(width, 3 * w)
    each = hd * w // width
    feature_grad = small[8 : 8 + each].reshape(each, width // w, heads, hd).transpose(2, 1, 0, 3).reshape(heads, hd, hd)
    qkv_bias_grad = small[6, : 3 * w].reshape(3, heads, hd).transpose(1, 0, 2).reshape(3 * w)

    return (
        output,
        tokens_grad,
        norm_sums[0],
        norm_sums[1],
        norm_sums[2],
        norm_sums[3],
        qkv_grad,
        qkv_bias_grad,
        dense_grad,
        small[4],
        fc_grad,
        hid_sum,
        proj_grad,
        feature_grad,
    )


def solution(mesh):
    rows = P(("batch", "tensor"), None)
    placed = (
        rows,
        rows,
        P(),
        P(),
        P(),
        P(),
        P(None, "tensor"),
        P("tensor"),
        P("tensor", None),
        P(),
        P(None, "tensor"),
        P("tensor"),
        P("tensor", None),
        P("tensor", None, None),
        P("batch", None),
        P("batch", None),
    )
    return jax.shard_map(
        body,
        mesh=mesh,
        in_specs=placed,
        out_specs=(
            rows,
            rows,
            P(),
            P(),
            P(),
            P(),
            P(None, "tensor"),
            P("tensor"),
            P("tensor", None),
            P(),
            P(None, "tensor"),
            P("tensor"),
            P("tensor", None),
            P("tensor", None, None),
        ),
        check_vma=False,
    )
```
